32 devices in a mesh: dp: 8 (over y, x, core), mp: 4 (over z).
Axes of the slice: x: 2, y: 2, z: 4, core: 2. Of those that a mesh axis runs over, the one named last changes fastest.
Arguments:
- tokens: bfloat16 [8192, 2048], P(('dp', 'mp')), may hold values from -6 to 6
- ln_gain: bfloat16 [2048], P('dp'), may hold values from 0.5 to 1.5
- ln_bias: bfloat16 [2048], P('dp'), may hold values from -1.75 to 1.75
- w_qkv: bfloat16 [2048, 3, 2048], P('dp', None, 'mp'), may hold values from -0.125 to 0.125
- b_qkv: bfloat16 [3, 32, 64], P(None, 'mp', 'dp'), may hold values from -3 to 3
- w_out: bfloat16 [2048, 2048], P('mp', 'dp'), may hold values from -0.5 to 0.5
- b_out: bfloat16 [2048], P('dp'), may hold values from -1.75 to 1.75
- w_up: bfloat16 [2048, 8192], P('dp', 'mp'), may hold values from -0.125 to 0.125
- b_up: bfloat16 [128, 64], P('mp', 'dp'), may hold values from -3 to 3
- w_down: bfloat16 [8192, 2048], P('mp', 'dp'), may hold values from -0.09375 to 0.09375
- b_down: bfloat16 [2048], P('dp'), may hold values from -1.75 to 1.75
- cotangent: bfloat16 [8192, 2048], P(('dp', 'mp')), may hold values from -6 to 6
Outputs:
- layer_out: bfloat16 [8192, 2048], P(('dp', 'mp'))
- grad_tokens: float32 [8192, 2048], P(('dp', 'mp'))
- grad_ln_gain: float32 [2048], P('dp')
- grad_ln_bias: float32 [2048], P('dp')
- grad_w_qkv: float32 [2048, 3, 2048], P('dp', None, 'mp')
- grad_b_qkv: float32 [3, 32, 64], P(None, 'mp', 'dp')
- grad_w_out: float32 [2048, 2048], P('mp', 'dp')
- grad_b_out: float32 [2048], P('dp')
- grad_w_up: float32 [2048, 8192], P('dp', 'mp')
- grad_b_up: float32 [128, 64], P('mp', 'dp')
- grad_w_down: float32 [8192, 2048], P('mp', 'dp')
- grad_b_down: float32 [2048], P('dp')
The draws below stay inside these ranges and needn't reach their ends.
All inputs are finite; a program needn't handle non-finite values.
Results may differ from the reference program's by a relative error of at most 0.015.
Values may be sent and summed in bfloat16 or wider, within the bound.
A program may use at most 192 MiB of HBM per device.

```python
import jax
import jax.numpy as jnp
from jax import lax

D = 2048
H = 32
HD = 64
ROT = 32
FF = 8192
SEQ = 1024
TOKENS = 8192
N_DP = 8


def block_levels(rng, extent, cuts, low, largest):
    level, own = 1.0, jax.random.fold_in(rng, 6)
    for dim, blocks in cuts:
        heights = jnp.exp(jax.random.uniform(jax.random.fold_in(own, dim), (blocks,), jnp.float32, low / len(cuts), largest / len(cuts)))
        level = level * jnp.repeat(heights, extent[dim] // blocks).reshape([-1 if axis == dim else 1 for axis in range(len(extent))])
    return level


def bell_draw(own_key, extent, width, reach, split=(), kind=jnp.bfloat16):
    loudness = block_levels(own_key, extent, split, -0.22, 0.18) if split else 1.0
    entries = jax.random.normal(own_key, extent, jnp.float32) * width * loudness
    return jnp.minimum(jnp.maximum(entries, -reach), reach).astype(kind)


def setup_inputs(seed: int = 0) -> dict:
    seeds = jax.random.split(jax.random.key(seed), 13)
    return {
        "tokens": bell_draw(seeds[0], (TOKENS, D), 1.0, 6.0, ((0, 32),)),
        "ln_gain": jnp.clip(1.0 + 0.1 * jax.random.normal(seeds[1], (D,), jnp.float32), 0.5, 1.5).astype(jnp.bfloat16),
        "ln_bias": bell_draw(seeds[2], (D,), 0.3, 1.75, ((0, 8),)),
        "w_qkv": bell_draw(seeds[3], (D, 3, D), D ** -0.5, 0.125, ((0, 8), (2, 4))),
        "b_qkv": bell_draw(seeds[4], (3, H, HD), 0.5, 3.0, ((1, 4), (2, 8))),
        "w_out": bell_draw(seeds[5], (D, D), (D // 16) ** -0.5, 0.5, ((0, 4), (1, 8))),
        "b_out": bell_draw(seeds[6], (D,), 0.3, 1.75, ((0, 8),)),
        "w_up": bell_draw(seeds[7], (D, FF), D ** -0.5, 0.125, ((0, 8), (1, 4))),
        "b_up": bell_draw(seeds[8], (FF // HD, HD), 0.5, 3.0, ((0, 4), (1, 8))),
        "w_down": bell_draw(seeds[9], (FF, D), (FF // 2) ** -0.5, 0.09375, ((0, 4), (1, 8))),
        "b_down": bell_draw(seeds[10], (D,), 0.3, 1.75, ((0, 8),)),
        "cotangent": bell_draw(seeds[11], (TOKENS, D), 1.0, 6.0, ((0, 32),)),
    }


@jax.custom_vjp
def low(v):
    return lax.optimization_barrier(v.astype(jnp.bfloat16)).astype(jnp.float32)

@jax.custom_vjp
def low_back(v):
    return v

def low_keep(v):
    return (low(v), None)

def low_pass(kept, grad):
    return (grad,)

def back_keep(v):
    return (v, None)

def back_low(kept, grad):
    return (low(grad),)
low.defvjp(low_keep, low_pass)
low_back.defvjp(back_keep, back_low)
epsilon = 1e-05
highest = lax.Precision.HIGHEST

def product(left, right):
    return jnp.dot(left, right, precision=highest, preferred_element_type=jnp.float32)

def norm_rows(values, gain, shift):
    centre = lax.optimization_barrier(jnp.mean(values, -1, keepdims=True))
    offset = values - centre
    spread = lax.optimization_barrier(jnp.mean(offset * offset, -1, keepdims=True))
    return offset * lax.rsqrt(spread + epsilon) * gain + shift

def rope_tables(length):
    places = jnp.arange(length, dtype=jnp.float32)
    inverse = 10000.0 ** (-jnp.arange(0, ROT, 2, dtype=jnp.float32) / ROT)
    angles = places[:, None] * inverse[None, :]
    angles = jnp.concatenate([angles, angles], -1)
    return (jnp.cos(angles), jnp.sin(angles))

def rotate(stacked, cosine_table, sine_table):
    halfway = ROT // 2
    turned_part = stacked[..., :ROT]
    swapped = jnp.concatenate([-turned_part[..., halfway:], turned_part[..., :halfway]], -1)
    return jnp.concatenate([turned_part * cosine_table + swapped * sine_table, stacked[..., ROT:]], -1)

def gelu_tanh(values):
    return jax.nn.gelu(values, approximate=True)

def layer_forward(sequence, ln_gain, ln_bias, w_qkv, b_qkv, w_out, b_out, w_up, b_up, w_down, b_down):
    normed = low(norm_rows(sequence, ln_gain, ln_bias))
    mixed = low_back(product(normed, w_qkv.reshape(D, 3 * D)) + b_qkv.reshape(3 * D))
    mixed = mixed.reshape(SEQ, 3, H, HD).transpose(1, 2, 0, 3)
    cosine_table, sine_table = rope_tables(SEQ)
    queries = low(rotate(mixed[0], cosine_table, sine_table))
    keys_all = low(rotate(mixed[1], cosine_table, sine_table))
    values_all = low(mixed[2])
    block_rows = min(512, SEQ)
    score_scale = HD ** (-0.5)

    def one_block(number):
        first_row = number * block_rows
        query_rows = lax.dynamic_slice_in_dim(queries, first_row, block_rows, 1)
        scores = low_back(jnp.einsum('hqd,hkd->hqk', query_rows, keys_all, precision=highest) * score_scale)
        row_place = first_row + jnp.arange(block_rows, dtype=jnp.int32)
        column_place = jnp.arange(SEQ, dtype=jnp.int32)
        scores = jnp.where(row_place[:, None] >= column_place[None, :], scores, -1e+30)
        weights = low(jax.nn.softmax(scores, -1))
        return jnp.einsum('hqk,hkd->hqd', weights, values_all, precision=highest)
    blocks = lax.map(jax.checkpoint(one_block), jnp.arange(SEQ // block_rows, dtype=jnp.int32))
    attended = low(low_back(blocks.transpose(0, 2, 1, 3).reshape(SEQ, D)))
    hidden = low_back(product(normed, w_up) + b_up.reshape(FF))
    activated = low(gelu_tanh(hidden))
    return sequence + product(attended, w_out) + b_out + product(activated, w_down) + b_down

def reference(tokens, ln_gain, ln_bias, w_qkv, b_qkv, w_out, b_out, w_up, b_up, w_down, b_down, cotangent):
    params = tuple((member.astype(jnp.float32) for member in (ln_gain, ln_bias, w_qkv, b_qkv, w_out, b_out, w_up, b_up, w_down, b_down)))
    inputs = tokens.astype(jnp.float32).reshape(N_DP, SEQ, D)
    pulled = cotangent.astype(jnp.float32).reshape(N_DP, SEQ, D)

    def one_sequence(running, couple):
        sequence, incoming = couple
        result, puller = jax.vjp(layer_forward, sequence, *params)
        gradients = puller(incoming)
        running = tuple((summed + gradient for summed, gradient in zip(running, gradients[1:])))
        return (running, (result.astype(jnp.bfloat16), gradients[0]))
    starting = tuple((jnp.zeros_like(member) for member in params))
    running, (results, input_grads) = lax.scan(one_sequence, starting, (inputs, pulled))
    grad_gain, grad_shift, grad_qkv, grad_qkv_bias, grad_outw, grad_outb, grad_upw, grad_upb, grad_downw, grad_downb = running
    return (results.reshape(TOKENS, D), input_grads.reshape(TOKENS, D), grad_gain, grad_shift, grad_qkv, grad_qkv_bias, grad_outw, grad_outb, grad_upw, grad_upb, grad_downw, grad_downb)
```

```python
import types

import jax
import jax.numpy as jnp
from jax import lax
from jax.experimental import pallas as pl
from jax.experimental.pallas import tpu as pltpu
from jax.sharding import PartitionSpec as P

D = 2048
HD = 64
ROT = 32
EPS = 1e-05
BQ = 256
MESH = pl.DeviceIdType.MESH
NN = (((1,), (0,)), ((), ()))
NT = (((1,), (1,)), ((), ()))
TN = (((0,), (0,)), ((), ()))
bf16 = jnp.bfloat16
f32 = jnp.float32


def mm(left, right, dims):
    return lax.dot_general(left, right, dims, preferred_element_type=f32)


def flip(index, mask):
    bit = 1
    while bit <= mask:
        if mask & bit:
            index = index + bit * (1 - 2 * lax.rem(lax.div(index, bit), 2))
        bit *= 2
    return index


def span(bits):
    found = [0]
    for bit in bits:
        found = found + [m + bit for m in found]
    return found


def maybe(pred, act):
    if pred is None:
        act()
    else:
        pl.when(pred)(act)


class Sent:
    def __init__(self, out, into, pred_out, pred_into):
        self.out, self.into, self.pred_out, self.pred_into = out, into, pred_out, pred_into
        self.left = False

    def start(self):
        maybe(self.pred_out, self.out.start)

    def arrive(self):
        maybe(self.pred_into, self.into.wait_recv)

    def finish(self):
        if not self.left:
            self.left = True
            maybe(self.pred_out, self.out.wait_send)


class Wire:
    def __init__(self, sems, count):
        self.sems, self.count, self.used, self.open = sems, count, 0, []

    def sem(self):
        assert self.used < self.count
        self.used += 1
        return self.sems.at[self.used - 1]

    def sems_of(self, n):
        assert self.used + n <= self.count
        self.used += n
        base = self.used - n
        return lambda j: self.sems.at[base + j]

    def send(self, src, dst, got, dev, pred_out=None, pred_into=None):
        s, r = self.sem(), self.sem()
        out = pltpu.make_async_remote_copy(src, dst, s, r, dev, MESH)
        into = pltpu.make_async_remote_copy(got, got, s, r, dev, MESH)
        one = Sent(out, into, pred_out, pred_into)
        one.start()
        self.open.append(one)
        return one

    def local(self, src, dst):
        copy = pltpu.make_async_copy(src, dst, self.sem())
        copy.start()
        return copy

    def finish(self):
        for one in self.open:
            one.finish()


def make_kernel(n_dp, n_mp, R, F, L, names, n_sems):
    S = R * n_mp
    CD = D // n_dp
    NC = n_dp // 2
    T = min(512, F)
    bits = [b for b in (2, 4, 8, 16, 32) if b < n_dp]
    orders = [bits, bits[1:] + bits[:1]]
    masks = sorted(span(bits), key=lambda m: -bin(m).count("1"))
    RB = min(BQ, S)

    def kernel(*refs):
        ref = types.SimpleNamespace(**dict(zip(names, refs)))
        me = lax.axis_index("dp")
        z = lax.axis_index("mp")
        wire = Wire(ref.sems, n_sems)
        slot_sems = ref.slot_sems
        mate = (flip(me, 1), z)

        barrier = pltpu.get_barrier_semaphore()
        for m in range(1, n_dp):
            pl.semaphore_signal(barrier, inc=1, device_id=(flip(me, m), z), device_id_type=MESH)
        for k in range(1, n_mp):
            pl.semaphore_signal(barrier, inc=1, device_id=(me, lax.rem(z + k, n_mp)), device_id_type=MESH)
        pl.semaphore_wait(barrier, n_dp - 1 + n_mp - 1)

        def ds(k, size):
            return pl.ds(pl.multiple_of(k * size, size), size)

        def row_pieces(own, full, rows):
            half = rows // 2

            def piece(k, h):
                if h is None:
                    return full.at[ds(k, rows), :]
                return full.at[pl.ds(pl.multiple_of(k * rows + h * half, half), half), :]

            return own, piece, lambda h: own.at[pl.ds(h * half, half), :]

        def cube_pieces(own, full, rows):
            half = rows // 2

            def piece(k, h):
                if h is None:
                    return full.at[:, ds(k, rows), :]
                return full.at[:, pl.ds(pl.multiple_of(k * rows + h * half, half), half), :]

            return own, piece, lambda h: own.at[:, pl.ds(h * half, half), :]

        def column_pieces(own, full, rows):
            half = rows // 2

            def piece(k, h):
                if h is None:
                    return full.at[:, ds(k, CD)]
                return full.at[pl.ds(h * half, half), ds(k, CD)]

            return own, piece, lambda h: own.at[pl.ds(h * half, half), :]

        weights = {
            "up": row_pieces(ref.w_up, ref.full_up, CD),
            "qkv": cube_pieces(ref.w_qkv, ref.full_qkv, CD),
            "down": column_pieces(ref.w_down, ref.full_down, F),
            "out": column_pieces(ref.w_out, ref.full_out, L),
        }
        order = ["up", "qkv", "down", "out"]
        arrivals = {w: [[] for _ in bits] for w in order}
        own_copies = {}

        def gather_step(w, j):
            own, piece, own_half = weights[w]
            if j > 0:
                for one in arrivals[w][j - 1]:
                    one.arrive()
            for h in range(2):
                way = orders[h]
                for sub in span(way[:j]):
                    k = flip(me, sub)
                    src = own_half(h) if sub == 0 else piece(k, h)
                    got = piece(flip(k, way[j]), h)
                    arrivals[w][j].append(wire.send(src, piece(k, h), got, (flip(me, way[j]), z)))

        def gather_mate(w):
            own, piece, _ = weights[w]
            for one in arrivals[w][-1]:
                one.arrive()
            sent = []
            for m in span(bits):
                k = flip(me, m)
                src = own if m == 0 else piece(k, None)
                sent.append(wire.send(src, piece(k, None), piece(flip(k, 1), None), mate))
            arrivals[w].append(sent)

        def gathered(w):
            for one in arrivals[w][-1]:
                one.arrive()
            own_copies[w].wait()

        hr = R // 2

        def line_step(own, full, s, hh, log):
            rows = pl.ds(hh * hr, hr)
            if s > 1:
                for one in log[(s - 1, hh)]:
                    one.arrive()
            up, down = z - (s - 1), z + (s - 1)
            first = own.at[rows, :] if s == 1 else None
            one = wire.send(
                first if s == 1 else full.at[jnp.maximum(up, 0), rows, :],
                full.at[jnp.maximum(up, 0), rows, :],
                full.at[jnp.maximum(z - s, 0), rows, :],
                (me, jnp.minimum(z + 1, n_mp - 1)),
                jnp.logical_and(z + 1 < n_mp, up >= 0),
                z - s >= 0,
            )
            two = wire.send(
                first if s == 1 else full.at[jnp.minimum(down, n_mp - 1), rows, :],
                full.at[jnp.minimum(down, n_mp - 1), rows, :],
                full.at[jnp.minimum(z + s, n_mp - 1), rows, :],
                (me, jnp.maximum(z - 1, 0)),
                jnp.logical_and(z >= 1, down < n_mp),
                z + s < n_mp,
            )
            log[(s, hh)] = [one, two]

        def line_done(log):
            for hh in range(2):
                for one in log[(n_mp - 1, hh)]:
                    one.arrive()


        def add_rows(out, terms, count, block, wide):
            @pl.loop(0, count // block)
            def _(i):
                rows = pl.ds(pl.multiple_of(i * block, block), block)
                total = terms[0][rows, 0:wide].astype(f32)
                for term in terms[1:]:
                    total = total + term[rows, 0:wide].astype(f32)
                out[rows, 0:wide] = total.astype(out.dtype)

        class LineSum:
            def __init__(self, part, from_below, from_above):
                self.part, self.below, self.above = part, from_below, from_above
                self.us, self.ur = wire.sems_of(n_mp), wire.sems_of(n_mp)
                self.ds, self.dr = wire.sems_of(n_mp), wire.sems_of(n_mp)

            def up(self, j):
                return pltpu.make_async_remote_copy(
                    self.part.at[j], self.below.at[j], self.us(j), self.ur(j),
                    (me, jnp.minimum(z + 1, n_mp - 1)), MESH,
                )

            def down(self, j):
                return pltpu.make_async_remote_copy(
                    self.part.at[j], self.above.at[j], self.ds(j), self.dr(j),
                    (me, jnp.maximum(z - 1, 0)), MESH,
                )

            def begin(self):
                @pl.when(z == 0)
                def _():
                    for j in range(n_mp - 1, 0, -1):
                        self.up(j).start()

                @pl.when(z == n_mp - 1)
                def _():
                    for j in range(n_mp - 1):
                        self.down(j).start()

            def merge(self, j, got):
                a, b = ref.zs.at[0], ref.zs.at[1]
                one = pltpu.make_async_copy(self.part.at[j], a, slot_sems.at[4])
                two = pltpu.make_async_copy(got.at[j], b, slot_sems.at[5])
                one.start()
                two.start()
                one.wait()
                two.wait()
                add_rows(a, [a, b], R, 32, D)
                back = pltpu.make_async_copy(a, self.part.at[j], slot_sems.at[4])
                back.start()
                back.wait()

            def step(self, tau):
                j = n_mp - 1 - tau + z

                @pl.when(jnp.logical_and(z > 0, jnp.logical_and(j < n_mp, tau >= z)))
                def _():
                    self.up(j).wait_recv()
                    self.merge(j, self.below)
                    self.up(j).start()

                i = tau - (n_mp - 1 - z)

                @pl.when(jnp.logical_and(z < n_mp - 1, i >= 0))
                def _():
                    self.down(i).wait_recv()
                    self.merge(i, self.above)
                    self.down(i).start()

            def arrive(self):
                @pl.when(z > 0)
                def _():
                    self.up(z).wait_recv()

                @pl.when(z < n_mp - 1)
                def _():
                    self.down(z).wait_recv()

            def load(self, out):
                copies = [pltpu.make_async_copy(self.part.at[z], out.at[0], slot_sems.at[4])]
                copies[0].start()

                @pl.when(z > 0)
                def _():
                    one = pltpu.make_async_copy(self.below.at[z], out.at[1], slot_sems.at[5])
                    one.start()
                    one.wait()

                @pl.when(z == 0)
                def _():
                    out[1] = jnp.zeros((R, D), bf16)

                @pl.when(z < n_mp - 1)
                def _():
                    one = pltpu.make_async_copy(self.above.at[z], out.at[2], slot_sems.at[6])
                    one.start()
                    one.wait()

                @pl.when(z == n_mp - 1)
                def _():
                    out[2] = jnp.zeros((R, D), bf16)

                copies[0].wait()

            def finish(self):
                for j in range(n_mp):
                    @pl.when(j > z)
                    def _():
                        self.up(j).wait_send()

                    @pl.when(j < z)
                    def _():
                        self.down(j).wait_send()

        def stream(count, copies, work):
            def each(i, slot, act):
                for n, (src, dst) in enumerate(copies(i, slot)):
                    act(pltpu.make_async_copy(src, dst, slot_sems.at[2 * n + slot]))

            each(0, 0, lambda c: c.start())

            @pl.loop(0, count)
            def _(i):
                slot = lax.rem(i, 2)

                @pl.when(i + 1 < count)
                def _():
                    each(i + 1, 1 - slot, lambda c: c.start())

                each(i, slot, lambda c: c.wait())
                work(i, slot)

        normed, pulled = ref.full_normed, ref.full_pulled
        pulled_log, normed_log = {}, {}
        vec_all = ref.vec_all
        vec_sent = []
        for m in range(1, n_dp):
            vec_sent.append(
                wire.send(ref.vec, vec_all.at[me], vec_all.at[flip(me, m)], (flip(me, m), z))
            )
        vec_own = wire.local(ref.vec, vec_all.at[me])
        tok_copy = wire.local(ref.tokens, ref.tok)
        for hh in range(2):
            line_step(ref.cotangent, pulled, 1, hh, pulled_log)
        for w in order:
            gather_step(w, 0)
        pulled_own = wire.local(ref.cotangent, pulled.at[z])
        for w in order:
            own, piece, _ = weights[w]
            own_copies[w] = wire.local(own, piece(me, None))

        for one in vec_sent:
            one.arrive()
        vec_own.wait()
        vrow = ref.vrow
        total = vec_all[0]
        for k in range(1, n_dp):
            total = total + vec_all[k]
        vrow[...] = total
        tok_copy.wait()
        tok, own_normed = ref.tok, ref.own_normed
        LB = 32

        def stats(rows):
            x = tok[rows, :].astype(f32)
            centre = jnp.mean(x, -1, keepdims=True)
            offset = x - centre
            spread = jnp.mean(offset * offset, -1, keepdims=True)
            scale = lax.rsqrt(spread + EPS)
            return x, offset * scale, scale

        @pl.loop(0, R // LB)
        def _(i):
            rows = ds(i, LB)
            x, xhat, _ = stats(rows)
            own_normed[rows, :] = (xhat * vrow[0:1, :] + vrow[1:2, :]).astype(bf16)

        for hh in range(2):
            line_step(own_normed, normed, 1, hh, normed_log)
        normed_own = wire.local(own_normed, normed.at[z])

        for w in order:
            for j in range(1, len(bits)):
                gather_step(w, j)
        for s in range(2, n_mp):
            for hh in range(2):
                line_step(own_normed, normed, s, hh, normed_log)
        for s in range(2, n_mp):
            for hh in range(2):
                if s == 2:
                    line_step(ref.cotangent, pulled, s, hh, pulled_log)
        gather_mate("up")
        line_done(normed_log)
        normed_own.wait()
        pulled_own.wait()
        Nv, Gv, Av, Hv = ref.Nv, ref.Gv, ref.Av, ref.Hv
        nv_copies = [wire.local(normed.at[j], Nv.at[pl.ds(j * R, R), :]) for j in range(n_mp)]
        normed_mate = wire.send(normed, ref.mate_normed, ref.mate_normed, mate)
        gathered("up")
        gather_mate("qkv")
        for one in nv_copies:
            one.wait()

        wa, wb = ref.wa, ref.wb
        per = D // S if D >= S else 1
        per_f = F // S if F >= S else 1
        half_rows = [pl.ds(i * (S // 2), S // 2) for i in range(2)]
        C0, C1 = 0.7978845608028654, 0.044715

        def wa_slot(slot, n):
            return wa.at[pl.ds(slot * per, n)]

        def tall(full, rows, i, slot, width):
            return [
                (
                    full.at[pl.ds(p * S, S), ds(i, width)],
                    wa.at[slot * per + p, :, pl.ds(0, width)],
                )
                for p in range(rows // S)
            ]

        def tall_value(slot, rows, width):
            return jnp.concatenate(
                [wa[slot * per + p, :, 0:width] for p in range(rows // S)], 0
            )

        def up_tile(i, slot):
            cols = ds(i, T)
            w = tall_value(slot, D, T)
            for rows in half_rows:
                v = mm(Nv[rows, :], w, NN) + vrow[4:5, cols]
                v2 = v * v
                t = jnp.tanh(C0 * v * (1.0 + C1 * v2))
                Av[rows, cols] = (0.5 * v * (1.0 + t)).astype(bf16)
                slope = 0.5 * (1.0 + t) + (0.5 * C0) * v * (1.0 - t * t) * (1.0 + 3.0 * C1 * v2)
                Hv[rows, cols] = slope.astype(bf16)

        stream(F // T, lambda i, s: tall(ref.full_up, D, i, s, T), up_tile)
        act_mate = wire.send(Av, ref.mate_act, ref.mate_act, mate)

        gathered("qkv")
        for s in range(3, n_mp):
            for hh in range(2):
                line_step(ref.cotangent, pulled, s, hh, pulled_log)
        gather_mate("down")
        gather_mate("out")
        QKV, ATv, LSE = ref.QKV, ref.ATv, ref.LSE
        tc, ts1, ts2 = ref.rope_c, ref.rope_l, ref.rope_r

        def turn(u, rows, sign):
            left = pltpu.roll(u, 128 - ROT // 2, 1)
            right = pltpu.roll(u, ROT // 2, 1)
            return u * tc[rows, :] + sign * (left * ts1[rows, :] + right * ts2[rows, :])

        def qkv_tile(i, slot):
            w = tall_value(slot, D, L)
            for rows in half_rows:
                v = mm(Nv[rows, :], w, NN)
                for c in range(L // 128):
                    lanes = pl.ds(c * 128, 128)
                    b = vrow[3:4, pl.ds(pl.multiple_of(i * L + c * 128, 128), 128)]
                    u = v[:, c * 128 : (c + 1) * 128] + b

                    @pl.when(i == 0)
                    def _():
                        QKV[0, rows, lanes] = turn(u, rows, 1.0).astype(bf16) * bf16(HD**-0.5)

                    @pl.when(i == 1)
                    def _():
                        QKV[1, rows, lanes] = turn(u, rows, 1.0).astype(bf16)

                    @pl.when(i == 2)
                    def _():
                        QKV[2, rows, lanes] = u.astype(bf16)

        def qkv_copies(i, slot):
            return [
                (ref.full_qkv.at[i, pl.ds(p * S, S), :], wa.at[slot * per + p, :, pl.ds(0, L)])
                for p in range(D // S)
            ]

        stream(3, qkv_copies, qkv_tile)

        lane = lax.broadcasted_iota(jnp.int32, (1, 128), 1)
        low_half = lane < HD
        pair_masks = [low_half, jnp.logical_not(low_half)]
        corner = lax.broadcasted_iota(jnp.int32, (RB, RB), 0) >= lax.broadcasted_iota(
            jnp.int32, (RB, RB), 1
        )

        def only(values, mask):
            return jnp.where(mask, values, jnp.zeros_like(values))

        @pl.loop(0, L // 128)
        def _(hp):
            lanes = ds(hp, 128)
            for i in range(S // RB):
                rows = pl.ds(i * RB, RB)
                q = QKV[0, rows, lanes]
                total = jnp.zeros((RB, 128), f32)
                logs = []
                for mask in pair_masks:
                    own_k = only(QKV[1, rows, lanes], mask)
                    own_v = only(QKV[2, rows, lanes], mask)
                    s_own = jnp.where(corner, mm(q, own_k, NT), -1e30)
                    top = jnp.max(s_own, -1, keepdims=True)
                    if i > 0:
                        past = pl.ds(0, i * RB)
                        s_past = mm(q, only(QKV[1, past, lanes], mask), NT)
                        top = jnp.maximum(top, jnp.max(s_past, -1, keepdims=True))
                    p_own = jnp.exp(s_own - top)
                    mass = jnp.sum(p_own, -1, keepdims=True)
                    if i > 0:
                        p_past = jnp.exp(s_past - top)
                        mass = mass + jnp.sum(p_past, -1, keepdims=True)
                    inverse = 1.0 / mass
                    total = total + mm((p_own * inverse).astype(bf16), own_v, NN)
                    if i > 0:
                        total = total + mm(
                            (p_past * inverse).astype(bf16), only(QKV[2, past, lanes], mask), NN
                        )
                    logs.append(top + jnp.log(mass))
                ATv[rows, lanes] = total.astype(bf16)
                LSE[rows, lanes] = jnp.where(low_half, logs[0], logs[1])

        att_mate = wire.send(ATv, ref.mate_att, ref.mate_att, mate)
        gathered("down")
        gathered("out")

        ob = ref.ob
        TD = min(512, D)

        def wo_slot(slot):
            return wb.at[slot, pl.ds(0, L), pl.ds(0, TD)]

        out_sems = ref.out_sems

        def put(dst_of, i, slot, count):
            return [
                pltpu.make_async_copy(
                    ob.at[slot, pl.ds(j * R, R), :], dst_of.at[j, :, ds(i, TD)], out_sems.at[slot, j]
                )
                for j in range(n_mp)
            ]

        def flush(dst_of, count):
            for i in range(max(0, count - 2), count):
                for c in put(dst_of, i, i % 2, count):
                    c.wait()

        def out_copies(i, slot):
            return tall(ref.full_down, F, i, slot, TD) + [
                (ref.full_out.at[:, ds(i, TD)], wo_slot(slot))
            ]

        def out_tile(i, slot):
            @pl.when(i >= 2)
            def _():
                for c in put(ref.part1, i - 2, slot, 0):
                    c.wait()

            w = tall_value(slot, F, TD)
            for rows in half_rows:
                v = mm(Av[rows, :], w, NN) + mm(ATv[rows, :], wb[slot, 0:L, 0:TD], NN)
                ob[slot, rows, :] = v.astype(bf16)
            for c in put(ref.part1, i, slot, 0):
                c.start()

        stream(D // TD, out_copies, out_tile)
        flush(ref.part1, D // TD)
        sum1 = LineSum(ref.part1, ref.below1, ref.above1)
        sum1.begin()

        line_done(pulled_log)
        gv_copies = [wire.local(pulled.at[j], Gv.at[pl.ds(j * R, R), :]) for j in range(n_mp)]
        pulled_mate = wire.send(pulled, ref.mate_pulled, ref.mate_pulled, mate)
        for one in gv_copies:
            one.wait()
        small = ref.small
        small[...] = jnp.zeros_like(small)

        def down_tile(i, slot):
            cols = ds(i, T)
            total = jnp.zeros((1, T), f32)
            for rows in half_rows:
                d = (mm(Gv[rows, :], wb[slot], NT) * Hv[rows, cols].astype(f32)).astype(bf16)
                Hv[rows, cols] = d
                total = total + jnp.sum(d.astype(f32), 0, keepdims=True)
            small[4:5, cols] = total

        stream(
            F // T, lambda i, s: [(ref.full_down.at[ds(i, T), :], wb.at[s])], down_tile
        )
        hid_mate = wire.send(Hv, ref.mate_hid, ref.mate_hid, mate)

        YP = ref.YP
        grad_info = {
            "down": (ref.gw_down, ref.rb_down, ref.st_down, ref.ta_down, F // 2, 128),
            "out": (ref.gw_out, ref.rb_out, ref.st_out, ref.ta_out, L // 2, 128),
            "up": (ref.gw_up, ref.rb_up, ref.st_up, ref.ta_up, CD // 2, 16),
            "qkv": (ref.gw_qkv, ref.rb_qkv, ref.st_up, ref.ta_up, CD // 2, 16),
        }
        place = {m: n for n, m in enumerate(masks)}
        offset, position = 0, []
        for i in range(len(bits)):
            position.append(offset)
            offset += 2 ** (len(bits) - 1 - i)

        def half_of(w, chunk, h):
            n = grad_info[w][4]
            if w == "qkv":
                return chunk.at[:, pl.ds(h * n, n), :]
            return chunk.at[pl.ds(h * n, n), :]

        came = {}

        def scatter_send(w, h, i, m):
            gw, rb = grad_info[w][:2]
            rest = span(orders[h][i + 1 :])
            keep = m - orders[h][i]
            pos = position[i] + rest.index(keep)
            one = wire.send(
                half_of(w, gw.at[place[m]], h), rb.at[h, pos], rb.at[h, pos],
                (flip(me, orders[h][i]), z),
            )
            came[(w, h, i, keep)] = one

        def scatter_first(w, m):
            for h in range(2):
                if m & orders[h][0]:
                    scatter_send(w, h, 0, m)

        def moves(w, far, near, base, out, sems=None):
            pairs = [(far, near)]
            if w == "qkv":
                pairs = [(far.at[j], near.at[:, pl.ds(j * L, L)]) for j in range(3)]
            return [
                pltpu.make_async_copy(*(p[::-1] if out else p), slot_sems.at[base + n])
                for n, p in enumerate(pairs)
            ]

        def run(copies):
            for c in copies:
                c.start()
            for c in copies:
                c.wait()

        def scatter_step(w, i):
            gw, rb, _, ta, n, block = grad_info[w]
            for h in range(2):
                way = orders[h]
                for m in [way[i] + sub for sub in span(way[i + 1 :])]:
                    terms = []
                    for e in range(i):
                        came[(w, h, e, m)].arrive()
                        rest = span(way[e + 1 :])
                        terms.append(rb.at[h, position[e] + rest.index(m)])
                    home = half_of(w, gw.at[place[m]], h)
                    run(moves(w, home, ta.at[0], 6, False))
                    for term in terms:
                        run(moves(w, term, ta.at[1], 9, False))
                        wide = 3 * L if w == "qkv" else ta.shape[-1]
                        add_rows(ta.at[0], [ta.at[0], ta.at[1]], n, block, wide)
                    run(moves(w, home, ta.at[0], 6, True))
                    scatter_send(w, h, i, m)

        def scatter_done(w):
            for h in range(2):
                for i in range(len(bits)):
                    came[(w, h, i, 0)].arrive()

        def grad_chunks(w, work):
            gw, _, st = grad_info[w][:3]
            pending = None

            def settle():
                for c in pending[0]:
                    c.wait()
                scatter_first(w, pending[1])

            for n, m in enumerate(masks):
                slot = n % 2
                work(m, flip(me, m), st.at[slot])
                copies = moves(w, gw.at[place[m]], st.at[slot], 12 + 3 * slot, True)
                for c in copies:
                    c.start()
                if pending is not None:
                    settle()
                pending = (copies, m)
            settle()

        def load_mate_columns(source):
            copies = []
            for n, m in enumerate(masks):
                k = flip(me, m)
                for j in range(n_mp):
                    copies.append(
                        wire.local(source.at[j, :, ds(k, CD)], YP.at[n, pl.ds(j * R, R), :])
                    )
            return copies

        def load_mate_tiles(source, count, width):
            return [
                wire.local(source.at[:, pl.ds(i * width, width)], wa.at[i, :, pl.ds(0, width)])
                for i in range(count)
            ]

        act_mate.arrive()
        loads = load_mate_tiles(ref.mate_act, F // T, T)
        pulled_mate.arrive()
        loads = loads + load_mate_columns(ref.mate_pulled)
        small[2:3, :] = sum_rows_of(Gv, S)
        for one in loads:
            one.wait()

        def grad_down(m, k, st):
            @pl.loop(0, F // T)
            def _(i):
                v = mm(Av[:, ds(i, T)], Gv[:, ds(k, CD)], TN)
                v = v + mm(wa[i], YP[place[m]], TN)
                st[ds(i, T), :] = v.astype(bf16)

        grad_chunks("down", grad_down)
        att_mate.arrive()
        loads = load_mate_tiles(ref.mate_att, 1, L)
        for one in loads:
            one.wait()

        def grad_out(m, k, st):
            v = mm(ATv[...], Gv[:, ds(k, CD)], TN)
            v = v + mm(wa[0, :, 0:L], YP[place[m]], TN)
            st[...] = v.astype(bf16)

        grad_chunks("out", grad_out)
        for tau in range(1, n_mp - 1):
            sum1.step(tau)

        DAv, DMv = ref.DAv, ref.DMv
        out_copy = wire.local(ref.full_out, wb.at[0, pl.ds(0, L), :])
        out_copy.wait()
        for rows in half_rows:
            DAv[rows, :] = mm(Gv[rows, :], wb[0, 0:L, :], NT).astype(bf16)

        dk, dv = ref.dk, ref.dv

        @pl.loop(0, L // 128)
        def _(hp):
            lanes = ds(hp, 128)
            dk[...] = jnp.zeros_like(dk)
            dv[...] = jnp.zeros_like(dv)
            for i in range(S // RB):
                rows = pl.ds(i * RB, RB)
                q = QKV[0, rows, lanes]
                do = DAv[rows, lanes]
                dq = jnp.zeros((RB, 128), f32)
                for e, mask in enumerate(pair_masks):
                    log_mass = LSE[rows, lanes][:, e * HD : e * HD + 1]
                    q_one, do_one = only(q, mask), only(do, mask)

                    def weights_of(where, diagonal):
                        k_one = only(QKV[1, where, lanes], mask)
                        v_one = only(QKV[2, where, lanes], mask)
                        p = jnp.exp(mm(q, k_one, NT) - log_mass)
                        if diagonal:
                            p = jnp.where(corner, p, 0.0)
                        return k_one, p, mm(do, v_one, NT)

                    k_own, p_own, dp_own = weights_of(rows, True)
                    delta = jnp.sum(p_own * dp_own, -1, keepdims=True)
                    if i > 0:
                        past = pl.ds(0, i * RB)
                        k_past, p_past, dp_past = weights_of(past, False)
                        delta = delta + jnp.sum(p_past * dp_past, -1, keepdims=True)
                        s_past = (p_past * (dp_past - delta)).astype(bf16)
                        dq = dq + mm(s_past, k_past, NN)
                        dk[past, :] += mm(s_past, q_one, TN)
                        dv[past, :] += mm(p_past.astype(bf16), do_one, TN)
                    s_own = (p_own * (dp_own - delta)).astype(bf16)
                    dq = dq + mm(s_own, k_own, NN)
                    dk[rows, :] += mm(s_own, q_one, TN)
                    dv[rows, :] += mm(p_own.astype(bf16), do_one, TN)
                DMv[0, rows, lanes] = turn(dq * HD**-0.5, rows, -1.0).astype(bf16)
            everything = pl.ds(0, S)
            DMv[1, :, lanes] = turn(dk[...], everything, -1.0).astype(bf16)
            DMv[2, :, lanes] = dv[...].astype(bf16)

        mix_mate = wire.send(DMv, ref.mate_mix, ref.mate_mix, mate)
        scatter_all = ["down", "out"]
        for w in scatter_all:
            for i in range(1, len(bits)):
                scatter_step(w, i)

        fold = S // TD

        def back_copies(i, slot):
            rows = ds(i, TD)
            return [(ref.full_up.at[rows, :], wb.at[slot, :, pl.ds(0, F)])] + [
                (
                    ref.full_qkv.at[j, rows, :],
                    wa.at[slot * per + j // fold, pl.ds(j % fold * TD, TD), pl.ds(0, L)],
                )
                for j in range(3)
            ]

        def back_tile(i, slot):
            @pl.when(i >= 2)
            def _():
                for c in put(ref.part2, i - 2, slot, 0):
                    c.wait()

            for rows in half_rows:
                v = mm(Hv[rows, :], wb[slot, :, 0:F], NT)
                for j in range(3):
                    w = wa[slot * per + j // fold, j % fold * TD : j % fold * TD + TD, 0:L]
                    v = v + mm(DMv[j, rows, :], w, NT)
                ob[slot, rows, :] = v.astype(bf16)
            for c in put(ref.part2, i, slot, 0):
                c.start()

        stream(D // TD, back_copies, back_tile)
        flush(ref.part2, D // TD)
        sum2 = LineSum(ref.part2, ref.below2, ref.above2)
        sum2.begin()

        hid_mate.arrive()
        loads = load_mate_tiles(ref.mate_hid, F // T, T)
        normed_mate.arrive()
        loads = loads + load_mate_columns(ref.mate_normed)
        for j in range(3):
            small[3:4, pl.ds(j * L, L)] = sum_rows_of(DMv.at[j], S)
        for one in loads:
            one.wait()

        def grad_up(m, k, st):
            @pl.loop(0, F // T)
            def _(i):
                v = mm(Nv[:, ds(k, CD)], Hv[:, ds(i, T)], TN)
                v = v + mm(YP[place[m]], wa[i], TN)
                st[:, ds(i, T)] = v.astype(bf16)

        grad_chunks("up", grad_up)
        mix_mate.arrive()
        loads = [
            wire.local(ref.mate_mix.at[j], wa.at[j, :, pl.ds(0, L)]) for j in range(3)
        ]
        for one in loads:
            one.wait()

        def grad_qkv(m, k, st):
            @pl.loop(0, 3)
            def _(j):
                v = mm(Nv[:, ds(k, CD)], DMv[j], TN)
                v = v + mm(YP[place[m]], wa[j, :, 0:L], TN)
                st[:, ds(j, L)] = v.astype(bf16)

        grad_chunks("qkv", grad_qkv)

        zs = ref.zs
        for hh in range(2):
            for one in normed_log[(1, hh)]:
                one.finish()
        sum1.arrive()
        sum1.load(zs)

        @pl.loop(0, R // LB)
        def _(i):
            rows = ds(i, LB)
            v = tok[rows, :].astype(f32) + vrow[2:3, :]
            v = v + zs[0, rows, :].astype(f32)
            v = v + zs[1, rows, :].astype(f32) + zs[2, rows, :].astype(f32)
            own_normed[rows, :] = v.astype(bf16)

        out1 = pltpu.make_async_copy(own_normed, ref.layer_out, slot_sems.at[0])

        for tau in range(1, n_mp - 1):
            sum2.step(tau)
        for i in range(1, len(bits)):
            scatter_step("up", i)
            scatter_step("qkv", i)
        out1.start()
        out1.wait()

        sum2.arrive()
        sum2.load(zs)
        cot = own_normed
        cot_copy = wire.local(ref.cotangent, cot)
        cot_copy.wait()
        stacks = D // L

        @pl.loop(0, R // LB)
        def _(i):
            rows = ds(i, LB)
            x, xhat, scale = stats(rows)
            d = zs[0, rows, :].astype(f32) + zs[1, rows, :].astype(f32)
            d = d + zs[2, rows, :].astype(f32)
            small[0:1, :] += jnp.sum(d * xhat, 0, keepdims=True)
            small[1:2, :] += jnp.sum(d, 0, keepdims=True)
            e = d * vrow[0:1, :]
            centre = jnp.mean(e, -1, keepdims=True)
            along = jnp.mean(e * xhat, -1, keepdims=True)
            result = cot[rows, :].astype(f32) + scale * (e - centre - xhat * along)
            for c in range(stacks):
                LSE[pl.ds(pl.multiple_of(c * R + i * LB, LB), LB), :] = result[:, c * L : (c + 1) * L]

        outs = [
            wire.local(LSE.at[pl.ds(c * R, R), :], ref.grad_tokens.at[:, pl.ds(c * L, L)])
            for c in range(stacks)
        ]

        mp_all, dp_all = ref.small_mp, ref.small_dp
        across = []
        for k in range(1, n_mp):
            to, fro = lax.rem(z + k, n_mp), lax.rem(z + n_mp - k, n_mp)
            across.append(wire.send(small, mp_all.at[k], mp_all.at[k], (me, to)))
        for one in across:
            one.arrive()
        first_two = lax.broadcasted_iota(jnp.int32, (8, 1), 0) < 2
        others = mp_all[1]
        for k in range(2, n_mp):
            others = others + mp_all[k]
        small2 = ref.small2
        small2[...] = small[...] + jnp.where(first_two, others, 0.0)
        across = []
        for m in range(1, n_dp):
            k = flip(me, m)
            across.append(wire.send(small2, dp_all.at[me], dp_all.at[k], (k, z)))
        own_small = wire.local(small2, dp_all.at[me])
        for one in across:
            one.arrive()
        own_small.wait()
        for w in order:
            scatter_done(w)
        for one in outs:
            one.wait()
        sum1.finish()
        sum2.finish()
        wire.finish()

    return kernel


def sum_rows_of(array, rows):
    total = None
    for i in range(rows // 128):
        part = jnp.sum(array[pl.ds(i * 128, 128), :].astype(f32), 0, keepdims=True)
        total = part if total is None else total + part
    return total


def rope_tables(length):
    places = jnp.arange(length, dtype=f32)
    inverse = 10000.0 ** (-jnp.arange(0, ROT, 2, dtype=f32) / ROT)
    angles = places[:, None] * inverse[None, :]
    cosine, sine = jnp.cos(angles), jnp.sin(angles)
    n = ROT // 2
    zero = jnp.zeros((length, HD - ROT), f32)
    c = jnp.concatenate([cosine, cosine, zero + 1.0], -1)
    left = jnp.concatenate([-sine, jnp.zeros((length, n), f32), zero], -1)
    right = jnp.concatenate([jnp.zeros((length, n), f32), sine, zero], -1)
    return [jnp.concatenate([t, t], -1) for t in (c, left, right)]


def make_body(n_dp, n_mp):
    def body(
        tokens, ln_gain, ln_bias, w_qkv, b_qkv, w_out, b_out, w_up, b_up, w_down, b_down, cotangent
    ):
        me = lax.axis_index("dp")
        R = tokens.shape[0]
        S = R * n_mp
        CD = D // n_dp
        NC = n_dp // 2
        F = w_up.shape[1]
        L = w_qkv.shape[2]
        heads = b_qkv.shape[1]
        share = HD // n_dp
        T = min(512, F)
        TD = 512

        def spread(shape, own, axis, size):
            return lax.dynamic_update_slice_in_dim(
                jnp.zeros(shape, f32), own.astype(f32), me * size, axis
            )

        def row(values):
            values = values.reshape(1, -1)
            return jnp.pad(values, ((0, 0), (0, D - values.shape[1])))

        vec = jnp.concatenate(
            [
                row(spread((D,), ln_gain, 0, CD)),
                row(spread((D,), ln_bias, 0, CD)),
                row(spread((D,), b_out.astype(f32) + b_down.astype(f32), 0, CD)),
                row(spread((3, heads, HD), b_qkv, 2, share)),
                row(spread((F // HD, HD), b_up, 1, share)),
                jnp.zeros((3, D), f32),
            ],
            0,
        )
        ins = dict(
            tokens=tokens,
            cotangent=cotangent,
            vec=vec,
            w_up=w_up,
            w_qkv=w_qkv.transpose(1, 0, 2),
            w_down=w_down,
            w_out=w_out,
        )
        rope_c, rope_l, rope_r = rope_tables(S)
        tables = dict(rope_c=rope_c, rope_l=rope_l, rope_r=rope_r)
        outs = dict(
            layer_out=((R, D), bf16),
            grad_tokens=((R, D), f32),
            small_dp=((n_dp, 8, D), f32),
            gw_up=((NC, CD, F), bf16),
            gw_qkv=((NC, 3, CD, L), bf16),
            gw_down=((NC, F, CD), bf16),
            gw_out=((NC, L, CD), bf16),
            rb_up=((2, NC - 1, CD // 2, F), bf16),
            rb_qkv=((2, NC - 1, 3, CD // 2, L), bf16),
            rb_down=((2, NC - 1, F // 2, CD), bf16),
            rb_out=((2, NC - 1, L // 2, CD), bf16),
            full_up=((D, F), bf16),
            full_qkv=((3, D, L), bf16),
            full_down=((F, D), bf16),
            full_out=((L, D), bf16),
            full_normed=((n_mp, R, D), bf16),
            full_pulled=((n_mp, R, D), bf16),
            mate_normed=((n_mp, R, D), bf16),
            mate_pulled=((n_mp, R, D), bf16),
            mate_act=((S, F), bf16),
            mate_hid=((S, F), bf16),
            mate_att=((S, L), bf16),
            mate_mix=((3, S, L), bf16),
            part1=((n_mp, R, D), bf16),
            below1=((n_mp, R, D), bf16),
            above1=((n_mp, R, D), bf16),
            part2=((n_mp, R, D), bf16),
            below2=((n_mp, R, D), bf16),
            above2=((n_mp, R, D), bf16),
        )
        n_sems = 40 * (n_dp + n_mp)
        scratch = dict(
            vec_all=pltpu.VMEM((n_dp, 8, D), f32),
            vrow=pltpu.VMEM((8, D), f32),
            small=pltpu.VMEM((8, D), f32),
            small2=pltpu.VMEM((8, D), f32),
            small_mp=pltpu.VMEM((n_mp, 8, D), f32),
            tok=pltpu.VMEM((R, D), bf16),
            own_normed=pltpu.VMEM((R, D), bf16),
            Nv=pltpu.VMEM((S, D), bf16),
            Gv=pltpu.VMEM((S, D), bf16),
            Av=pltpu.VMEM((S, F), bf16),
            Hv=pltpu.VMEM((S, F), bf16),
            QKV=pltpu.VMEM((3, S, L), bf16),
            ATv=pltpu.VMEM((S, L), bf16),
            DAv=pltpu.VMEM((S, L), bf16),
            DMv=pltpu.VMEM((3, S, L), bf16),
            LSE=pltpu.VMEM((S, L), f32),
            dk=pltpu.VMEM((S, 128), f32),
            dv=pltpu.VMEM((S, 128), f32),
            wa=pltpu.VMEM((2 * (D // S), S, T), bf16),
            wb=pltpu.VMEM((2, T, D), bf16),
            ob=pltpu.VMEM((2, S, TD), bf16),
            YP=pltpu.VMEM((NC, S, CD), bf16),
            zs=pltpu.VMEM((3, R, D), bf16),
            st_up=pltpu.VMEM((2, CD, F), bf16),
            st_down=pltpu.VMEM((2, F, CD), bf16),
            st_out=pltpu.VMEM((2, L, CD), bf16),
            ta_up=pltpu.VMEM((2, CD // 2, F), bf16),
            ta_down=pltpu.VMEM((2, F // 2, CD), bf16),
            ta_out=pltpu.VMEM((2, L // 2, CD), bf16),
            sems=pltpu.SemaphoreType.DMA((n_sems,)),
            slot_sems=pltpu.SemaphoreType.DMA((18,)),
            out_sems=pltpu.SemaphoreType.DMA((2, n_mp)),
        )
        names = list(ins) + list(tables) + list(outs) + list(scratch)
        any_spec = pl.BlockSpec(memory_space=pl.ANY)
        got = pl.pallas_call(
            make_kernel(n_dp, n_mp, R, F, L, names, n_sems),
            out_shape=[jax.ShapeDtypeStruct(s, t) for s, t in outs.values()],
            in_specs=[any_spec] * len(ins) + [pl.BlockSpec(memory_space=pltpu.VMEM)] * 3,
            out_specs=[any_spec] * len(outs),
            scratch_shapes=list(scratch.values()),
            name="layer",
            cost_estimate=pl.CostEstimate(
                flops=6 * S * D * (4 * L + 2 * F), bytes_accessed=150 << 20, transcendentals=0
            ),
            compiler_params=pltpu.CompilerParams(
                collective_id=0, has_side_effects=True, vmem_limit_bytes=60 << 20
            ),
        )(*ins.values(), *tables.values())
        got = types.SimpleNamespace(**dict(zip(outs, got)))

        def total(own, parts, split):
            bits = [b for b in (2, 4, 8, 16, 32) if b < n_dp]
            here = [0]
            for i in range(len(bits) - 1):
                here.append(here[-1] + 2 ** (len(bits) - 1 - i))
            arrived = sum(parts[:, p].astype(f32) for p in here)
            arrived = jnp.concatenate([arrived[0], arrived[1]], split)
            return own[NC - 1].astype(f32) + arrived

        sums = jnp.sum(got.small_dp, 0)

        def mine(values, axis, size):
            return lax.dynamic_slice_in_dim(values, me * size, size, axis)

        bias = mine(sums[2], 0, CD)
        return (
            got.layer_out,
            got.grad_tokens,
            mine(sums[0], 0, CD),
            mine(sums[1], 0, CD),
            total(got.gw_qkv, got.rb_qkv, 1).transpose(1, 0, 2),
            mine(sums[3, : 3 * L].reshape(3, heads, HD), 2, share),
            total(got.gw_out, got.rb_out, 0),
            bias,
            total(got.gw_up, got.rb_up, 0),
            mine(sums[4, :F].reshape(F // HD, HD), 1, share),
            total(got.gw_down, got.rb_down, 0),
            bias,
        )

    return body


def solution(mesh):
    n_dp, n_mp = mesh.shape["dp"], mesh.shape["mp"]
    weights_in = (
        P("dp"),
        P("dp"),
        P("dp", None, "mp"),
        P(None, "mp", "dp"),
        P("mp", "dp"),
        P("dp"),
        P("dp", "mp"),
        P("mp", "dp"),
        P("mp", "dp"),
        P("dp"),
    )
    rows = P(("dp", "mp"), None)
    return jax.shard_map(
        make_body(n_dp, n_mp),
        mesh=mesh,
        in_specs=(rows,) + weights_in + (rows,),
        out_specs=(rows, rows) + weights_in,
        check_vma=False,
    )
```

```python
import types

import jax
import jax.numpy as jnp
import numpy as np
from jax import lax
from jax.experimental import pallas as pl
from jax.experimental.pallas import tpu as pltpu
from jax.sharding import PartitionSpec as P

D = 2048
HD = 64
ROT = 32
EPS = 1e-05
BQ = 256
LB = 32
VB = 512
MESH = pl.DeviceIdType.MESH
NN = (((1,), (0,)), ((), ()))
NT = (((1,), (1,)), ((), ()))
TN = (((0,), (0,)), ((), ()))
bf16 = jnp.bfloat16
f32 = jnp.float32


def mm(left, right, dims):
    return lax.dot_general(left, right, dims, preferred_element_type=f32)


def flip(index, mask):
    bit = 1
    while bit <= mask:
        if mask & bit:
            index = index + bit * (1 - 2 * lax.rem(lax.div(index, bit), 2))
        bit *= 2
    return index


def span(bits):
    found = [0]
    for bit in bits:
        found = found + [m + bit for m in found]
    return found


def maybe_static(pred, act):
    if isinstance(pred, bool):
        if pred:
            act()
    else:
        pl.when(pred)(act)


def maybe(pred, act):
    if pred is None:
        act()
    else:
        pl.when(pred)(act)


class Sent:
    def __init__(self, out, into, pred_out, pred_into):
        self.out, self.into, self.pred_out, self.pred_into = out, into, pred_out, pred_into
        self.came, self.left = False, False

    def start(self):
        maybe(self.pred_out, self.out.start)

    def arrive(self):
        if not self.came:
            self.came = True
            maybe(self.pred_into, self.into.wait_recv)

    def finish(self):
        if not self.left:
            self.left = True
            maybe(self.pred_out, self.out.wait_send)


class Wire:
    def __init__(self, sems, count):
        self.sems, self.count, self.used, self.open = sems, count, 0, []

    def sem(self):
        assert self.used < self.count
        self.used += 1
        return self.sems.at[self.used - 1]

    def sems_of(self, n):
        assert self.used + n <= self.count
        self.used += n
        base = self.used - n
        return lambda j: self.sems.at[base + j]

    def send(self, src, dst, got, dev, pred_out=None, pred_into=None):
        s, r = self.sem(), self.sem()
        out = pltpu.make_async_remote_copy(src, dst, s, r, dev, MESH)
        into = pltpu.make_async_remote_copy(got, got, s, r, dev, MESH)
        one = Sent(out, into, pred_out, pred_into)
        one.start()
        self.open.append(one)
        return one

    def local(self, src, dst):
        copy = pltpu.make_async_copy(src, dst, self.sem())
        copy.start()
        return copy

    def finish(self):
        for one in self.open:
            one.finish()


def make_kernel(n_dp, n_mp, R, F, L, names, n_sems):
    S = R * n_mp
    CD = D // n_dp
    NC = n_dp // 2
    T = min(512, F)
    TD = 512
    HS = S // 2
    NH = n_mp // 2
    bits = [b for b in (2, 4, 8, 16, 32) if b < n_dp]
    orders = [bits, bits[1:] + bits[:1]]
    masks = sorted(span(bits), key=lambda m: -bin(m).count("1"))
    place = {m: n for n, m in enumerate(masks)}
    RB = min(BQ, S)

    def kernel(*refs):
        ref = types.SimpleNamespace(**dict(zip(names, refs)))
        me = lax.axis_index("dp")
        z = lax.axis_index("mp")
        wire = Wire(ref.sems, n_sems)
        slot_sems = ref.slot_sems
        mate = (flip(me, 1), z)
        up_dev = (me, jnp.minimum(z + 1, n_mp - 1))
        down_dev = (me, jnp.maximum(z - 1, 0))
        mine_half = lax.div(z, NH)
        barrier = pltpu.get_barrier_semaphore()
        for m in range(1, n_dp):
            pl.semaphore_signal(barrier, inc=1, device_id=(flip(me, m), z), device_id_type=MESH)
        for k in range(1, n_mp):
            pl.semaphore_signal(
                barrier, inc=1, device_id=(me, lax.rem(z + k, n_mp)), device_id_type=MESH
            )
        pl.semaphore_wait(barrier, n_dp - 1 + n_mp - 1)

        def ds(k, size):
            return pl.ds(pl.multiple_of(k * size, size), size)

        def run(copies):
            for c in copies:
                c.start()
            for c in copies:
                c.wait()

        def pieces_of(full, rows, kind):
            half = rows // 2

            def piece(k, h):
                if kind == "rows":
                    if h is None:
                        return full.at[ds(k, rows), :]
                    return full.at[pl.ds(pl.multiple_of(k * rows + h * half, half), half), :]
                if kind == "cube":
                    if h is None:
                        return full.at[:, ds(k, rows), :]
                    return full.at[:, pl.ds(pl.multiple_of(k * rows + h * half, half), half), :]
                if h is None:
                    return full.at[:, ds(k, CD)]
                return full.at[pl.ds(h * half, half), ds(k, CD)]

            return piece

        def half_rows_of(array, n, h, cube):
            if cube:
                return array.at[:, pl.ds(h * n, n), :]
            return array.at[pl.ds(h * n, n), :]

        weights = {
            "up": (ref.w_up, pieces_of(ref.full_up, CD, "rows"), CD // 2, ref.st_up.at[0]),
            "qkv": (ref.w_qkv, pieces_of(ref.full_qkv, CD, "cube"), CD // 2, ref.st_up.at[1]),
            "down": (ref.w_down, pieces_of(ref.full_down, F, "cols"), F // 2, ref.st_down.at[0]),
            "out": (ref.w_out, pieces_of(ref.full_out, L, "cols"), L // 2, ref.st_down.at[1, pl.ds(0, L)]),
        }
        order = ["up", "qkv", "down", "out"]
        arrivals = {w: [[] for _ in bits] for w in order}

        mates = {w: [] for w in order}

        def to_mate(w, j):
            piece = weights[w][1]
            for h in range(2):
                way = orders[h]
                for sub in span(way[:j]):
                    k = flip(flip(me, sub), way[j])
                    got = piece(flip(k, 1), h)
                    mates[w].append(wire.send(piece(k, h), piece(k, h), got, mate))

        def gather_step(w, j):
            own, piece, n, _ = weights[w]
            if j > 0:
                for one in arrivals[w][j - 1]:
                    one.arrive()
            for h in range(2):
                way = orders[h]
                for sub in span(way[:j]):
                    k = flip(me, sub)
                    src = half_rows_of(own, n, h, w == "qkv") if sub == 0 else piece(k, h)
                    got = piece(flip(k, way[j]), h)
                    arrivals[w][j].append(wire.send(src, piece(k, h), got, (flip(me, way[j]), z)))
            if j > 0:
                to_mate(w, j - 1)
            else:
                got = piece(flip(me, 1), None)
                mates[w].append(wire.send(own, piece(me, None), got, mate))

        def gather_mate(w):
            for one in arrivals[w][-1]:
                one.arrive()
            to_mate(w, len(bits) - 1)

        def gathered(w):
            for one in mates[w]:
                one.arrive()

        def moves(w, far, near, base, out):
            pairs = [(far, near)]
            if w == "qkv":
                pairs = [(far.at[j], near.at[:, pl.ds(j * L, L)]) for j in range(3)]
            return [
                pltpu.make_async_copy(*(p[::-1] if out else p), slot_sems.at[base + n])
                for n, p in enumerate(pairs)
            ]

        hr = R // 2

        def line_step(own, full, s, hh, log):
            rows = pl.ds(hh * hr, hr)
            if s > 1:
                for one in log[(s - 1, hh)]:
                    one.arrive()
            up, down = z - (s - 1), z + (s - 1)
            first = own.at[rows, :] if s == 1 else None
            one = wire.send(
                first if s == 1 else full.at[jnp.maximum(up, 0), rows, :],
                full.at[jnp.maximum(up, 0), rows, :],
                full.at[jnp.maximum(z - s, 0), rows, :],
                up_dev,
                jnp.logical_and(z + 1 < n_mp, up >= 0),
                z - s >= 0,
            )
            two = wire.send(
                first if s == 1 else full.at[jnp.minimum(down, n_mp - 1), rows, :],
                full.at[jnp.minimum(down, n_mp - 1), rows, :],
                full.at[jnp.minimum(z + s, n_mp - 1), rows, :],
                down_dev,
                jnp.logical_and(z >= 1, down < n_mp),
                z + s < n_mp,
            )
            log[(s, hh)] = [one, two]

        def line_arrive(log, s):
            for hh in range(2):
                for one in log[(s, hh)]:
                    one.arrive()

        class Loads:
            def __init__(self):
                self.open = []

            def rows(self, full, near, s):
                for c, pred in ((z - s, z - s >= 0), (z + s, z + s < n_mp)):
                    safe = jnp.clip(c, 0, n_mp - 1)
                    copy = pltpu.make_async_copy(full.at[safe], near.at[ds(safe, R), :], wire.sem())
                    maybe(pred, copy.start)
                    self.open.append((copy, pred))

            def wait(self):
                for copy, pred in self.open:
                    maybe(pred, copy.wait)
                self.open = []

        def add_rows(out, terms, count, block, wide):
            @pl.loop(0, count // block)
            def _(i):
                rows = pl.ds(pl.multiple_of(i * block, block), block)
                total = terms[0][rows, 0:wide].astype(f32)
                for term in terms[1:]:
                    total = total + term[rows, 0:wide].astype(f32)
                out[rows, 0:wide] = total.astype(out.dtype)

        class LineSum:
            def __init__(self, part, from_below, from_above):
                self.part, self.below, self.above = part, from_below, from_above
                self.us, self.ur = wire.sems_of(n_mp), wire.sems_of(n_mp)
                self.ds, self.dr = wire.sems_of(n_mp), wire.sems_of(n_mp)

            def up(self, j):
                return pltpu.make_async_remote_copy(
                    self.part.at[j], self.below.at[j], self.us(j), self.ur(j), up_dev, MESH
                )

            def down(self, j):
                return pltpu.make_async_remote_copy(
                    self.part.at[j], self.above.at[j], self.ds(j), self.dr(j), down_dev, MESH
                )

            def begin(self, near):
                @pl.when(z == 0)
                def _():
                    for j in range(n_mp - 1, 0, -1):
                        if (j < NH) == near:
                            self.up(j).start()

                @pl.when(z == n_mp - 1)
                def _():
                    for j in range(n_mp - 1):
                        if (j >= NH) == near:
                            self.down(j).start()

            def merge(self, j, got):
                a, b = ref.zs.at[0], ref.zs.at[1]
                one = pltpu.make_async_copy(self.part.at[j], a, slot_sems.at[4])
                two = pltpu.make_async_copy(got.at[j], b, slot_sems.at[5])
                run([one, two])
                add_rows(a, [a, b], R, LB, D)
                run([pltpu.make_async_copy(a, self.part.at[j], slot_sems.at[4])])

            def step(self, tau):
                j = n_mp - 1 - tau + z

                @pl.when(jnp.logical_and(z > 0, jnp.logical_and(j < n_mp, tau >= z)))
                def _():
                    self.up(j).wait_recv()
                    self.merge(j, self.below)
                    self.up(j).start()

                i = tau - (n_mp - 1 - z)

                @pl.when(jnp.logical_and(z < n_mp - 1, i >= 0))
                def _():
                    self.down(i).wait_recv()
                    self.merge(i, self.above)
                    self.down(i).start()

            def arrive(self):
                @pl.when(z > 0)
                def _():
                    self.up(z).wait_recv()

                @pl.when(z < n_mp - 1)
                def _():
                    self.down(z).wait_recv()

            def load(self, out):
                home = pltpu.make_async_copy(self.part.at[z], out.at[0], slot_sems.at[4])
                home.start()

                @pl.when(z > 0)
                def _():
                    run([pltpu.make_async_copy(self.below.at[z], out.at[1], slot_sems.at[5])])

                @pl.when(z == 0)
                def _():
                    out[1] = jnp.zeros((R, D), bf16)

                @pl.when(z < n_mp - 1)
                def _():
                    run([pltpu.make_async_copy(self.above.at[z], out.at[2], slot_sems.at[6])])

                @pl.when(z == n_mp - 1)
                def _():
                    out[2] = jnp.zeros((R, D), bf16)

                home.wait()

            def finish(self):
                for j in range(n_mp):

                    @pl.when(j > z)
                    def _():
                        self.up(j).wait_send()

                    @pl.when(j < z)
                    def _():
                        self.down(j).wait_send()

        class Ring:
            def __init__(self, slots, first_sem):
                self.slots, self.first_sem, self.base, self.primed = slots, first_sem, 0, 0

            def tile(self, copies, i, slot):
                return [
                    pltpu.make_async_copy(src, dst, slot_sems.at[self.first_sem + self.slots * n + slot])
                    for n, (src, dst) in enumerate(copies(i, slot))
                ]

            def start(self, copies, i, slot):
                for c in self.tile(copies, i, slot):
                    c.start()

            def fill(self, copies):
                for d in range(self.slots - 1):
                    self.start(copies, d, (self.base + d) % self.slots)

            def prime(self, copies):
                if not self.primed:
                    self.fill(copies)
                self.primed = self.slots - 1

            def step(self, count, copies, then, i):
                slot = lax.rem(self.base + i, self.slots)
                ahead = i + self.slots - 1

                def next_tile(slot):
                    maybe_static(ahead < count, lambda: self.start(copies, ahead, slot))
                    if then is not None:
                        for d in range(self.slots - 1):
                            maybe_static(ahead == count + d, lambda: self.start(then, d, slot))

                next_tile(lax.rem(self.base + ahead, self.slots))
                for c in self.tile(copies, i, slot):
                    c.wait()
                return slot

            def turned(self, count, then):
                self.base = (self.base + count) % self.slots
                self.primed = 0 if then is None else self.slots - 1

            def run(self, count, copies, work, then=None):
                self.prime(copies)

                @pl.loop(0, count)
                def _(i):
                    work(i, self.step(count, copies, then, i))

                self.turned(count, then)

        tall_ring, wide_ring = Ring(3, 18), Ring(2, 22)

        normed, pulled = ref.full_normed, ref.full_pulled
        pulled_log, normed_log = {}, {}
        Nv, Gv, Av, Hv = ref.Nv, ref.Gv, ref.Av, ref.Hv
        own_rows = ds(z, R)
        vec_a, vec_b, vrow = ref.vec_a_all, ref.vec_b_all, ref.vrow
        vec_sent = []
        for m in range(1, n_dp):
            k = flip(me, m)
            vec_sent.append(wire.send(ref.vec_a, vec_a.at[me], vec_a.at[k], (k, z)))
        own_vec = [wire.local(ref.vec_a, vec_a.at[me]), wire.local(ref.vec_b, vec_b.at[me])]
        tok_copy = wire.local(ref.tokens, ref.tok)
        line_step(ref.cotangent, pulled, 1, 0, pulled_log)
        gather_step("up", 0)
        vec_b_sent = []
        for m in range(1, n_dp):
            k = flip(me, m)
            vec_b_sent.append(wire.send(ref.vec_b, vec_b.at[me], vec_b.at[k], (k, z)))
        gather_step("qkv", 0)
        own_loads = [
            c for n, w in enumerate(order) for c in moves(w, weights[w][0], weights[w][3], 3 * n, False)
        ]
        for c in own_loads:
            c.start()
        cot_copy = wire.local(ref.cotangent, Gv.at[own_rows, :])
        tables = [
            wire.local(a, b)
            for a, b in ((ref.rope_c, ref.tc), (ref.rope_s, ref.ts))
        ]

        for one in vec_sent:
            one.arrive()
        for c in own_vec:
            c.wait()
        for k in range(n_dp):
            vrow[0:3, k * CD : (k + 1) * CD] = vec_a[k, 0:3, :]
        tok_copy.wait()
        tok = ref.tok

        def stats(rows):
            x = tok[rows, :].astype(f32)
            centre = jnp.mean(x, -1, keepdims=True)
            offset = x - centre
            spread = jnp.mean(offset * offset, -1, keepdims=True)
            scale = lax.rsqrt(spread + EPS)
            return x, offset * scale, scale


        @pl.loop(0, R // LB)
        def _(i):
            _, xhat, _ = stats(ds(i, LB))
            v = (xhat * vrow[0:1, :] + vrow[1:2, :]).astype(bf16)
            Nv[pl.ds(pl.multiple_of(z * R + i * LB, LB), LB), :] = v

        own_normed = Nv.at[own_rows, :]
        for hh in range(2):
            line_step(own_normed, normed, 1, hh, normed_log)

        for c in own_loads:
            c.wait()
        own_stores = [
            c
            for n, w in enumerate(order)
            for c in moves(w, weights[w][1](me, None), weights[w][3], 3 * n, True)
        ]
        for c in own_stores:
            c.start()
        for j in range(1, len(bits)):
            gather_step("up", j)
        gather_step("down", 0)
        for j in range(1, len(bits)):
            gather_step("qkv", j)
        gather_step("out", 0)
        for c in own_stores:
            c.wait()
        for c in tables:
            c.wait()
        for one in vec_b_sent:
            one.arrive()
        total = vec_b[0]
        for k in range(1, n_dp):
            total = total + vec_b[k]
        nq, nu = -(-3 * L // VB), F // VB
        for n in range(nq):
            vrow[3:4, n * VB : (n + 1) * VB] = total[n : n + 1, :]
        for n in range(nu):
            vrow[4:5, n * VB : (n + 1) * VB] = total[nq + n : nq + n + 1, :]

        loads = Loads()
        line_step(own_normed, normed, 2, 0, normed_log)
        line_step(own_normed, normed, 2, 1, normed_log)
        gather_mate("up")
        loads.rows(normed, Nv, 1)
        for s in range(2, NH):
            for hh in range(2):
                line_step(own_normed, normed, s + 1, hh, normed_log)
            loads.rows(normed, Nv, s)
        gathered("up")
        loads.wait()

        wa, wb = ref.wa, ref.wb
        WT = min(1024, F)
        C0, C1 = 0.7978845608028654, 0.044715

        def sequence_half(other, quarter=None):
            which = 1 - mine_half if other else mine_half
            if quarter is None:
                return ds(which, HS)
            return pl.ds(pl.multiple_of(which * HS + quarter * (HS // 2), HS // 2), HS // 2)

        own_quarters = [sequence_half(False, q) for q in range(2)]
        near_quarter = [ds(1 + lax.rem(1 + mine_half, 2), HS // 2)]
        far_quarter = [ds(3 - 3 * mine_half, HS // 2)]

        def tall(full, rows, i, slot, width):
            return [(full.at[:, ds(i, width)], wa.at[slot, pl.ds(0, rows), pl.ds(0, width)])]

        def tall_value(slot, rows, width):
            return wa[slot, 0:rows, 0:width]

        def wide_slot(slot):
            return pl.ds(pl.multiple_of(slot * T, T), T)

        def up_copies(i, slot):
            return tall(ref.full_up, D, i, slot, T)

        def hidden(parts, then=None):
            def work(i, slot):
                cols = ds(i, T)
                w = tall_value(slot, D, T)
                for rows in parts:
                    v = mm(Nv[rows, :], w, NN) + vrow[4:5, cols]
                    v2 = v * v
                    a = 0.5 * jnp.tanh(v * ((C0 * C1) * v2 + C0)) + 0.5
                    act = v * a
                    Av[rows, cols] = act.astype(bf16)
                    Hv[rows, cols] = (a + act * (1.0 - a) * ((6 * C0 * C1) * v2 + 2 * C0)).astype(bf16)

            tall_ring.run(F // T, up_copies, work, then)

        QKV, ATv, LSE = ref.QKV, ref.ATv, ref.LSE
        tc, ts = ref.tc, ref.ts
        first_turn = lax.rem(lax.broadcasted_iota(jnp.int32, (1, 128), 1), HD) < ROT // 2

        def turn(u, rows, sign):
            left = pltpu.roll(u, 128 - ROT // 2, 1)
            right = pltpu.roll(u, ROT // 2, 1)
            return u * tc[rows, :] + sign * (jnp.where(first_turn, left, right) * ts[rows, :])

        def qkv_copies(j, slot):
            return [(ref.full_qkv.at[j], wa.at[slot, :, pl.ds(0, L)])]

        def mix(parts):
            tall_ring.prime(qkv_copies)
            for j in range(3):
                slot = tall_ring.step(3, qkv_copies, None, j)
                w = tall_value(slot, D, L)
                for rows in parts:
                    v = mm(Nv[rows, :], w, NN) + vrow[3:4, j * L : (j + 1) * L]
                    for c in range(L // 128):
                        u = v[:, c * 128 : (c + 1) * 128]
                        if j < 2:
                            u = turn(u, rows, 1.0)
                        u = u.astype(bf16)
                        if j == 0:
                            u = u * bf16(HD**-0.5)
                        QKV[j, rows, pl.ds(c * 128, 128)] = u
            tall_ring.turned(3, None)

        if NH < n_mp - 1:
            line_step(own_normed, normed, NH + 1, 0, normed_log)
        hidden(own_quarters)
        tall_ring.prime(up_copies)
        for j in range(1, len(bits)):
            gather_step("down", j)
        for s in range(NH, n_mp - 1):
            for hh in range(2):
                if (s + 1, hh) not in normed_log:
                    line_step(own_normed, normed, s + 1, hh, normed_log)
            loads.rows(normed, Nv, s)
        line_step(ref.cotangent, pulled, 1, 1, pulled_log)
        loads.wait()
        hidden(near_quarter)
        gather_mate("qkv")
        for j in range(1, len(bits)):
            gather_step("out", j)
        gathered("qkv")
        mix(own_quarters + near_quarter)
        tall_ring.prime(up_copies)
        line_arrive(normed_log, n_mp - 1)
        loads.rows(normed, Nv, n_mp - 1)
        loads.wait()
        line_step(ref.cotangent, pulled, 2, 0, pulled_log)
        normed_mate = wire.send(Nv, ref.mate_normed, ref.mate_normed, mate)
        hidden(far_quarter, qkv_copies)
        line_step(ref.cotangent, pulled, 2, 1, pulled_log)
        for s in range(3, n_mp - 1):
            for hh in range(2):
                line_step(ref.cotangent, pulled, s, hh, pulled_log)
        mix(far_quarter)
        act_mate = wire.send(Av, ref.mate_act, ref.mate_act, mate)

        corner = lax.broadcasted_iota(jnp.int32, (RB, RB), 0) <= lax.broadcasted_iota(
            jnp.int32, (RB, RB), 1
        )
        lane = lax.broadcasted_iota(jnp.int32, (1, 128), 1)
        pair_masks = [lane < HD, lane >= HD]

        def only(values, mask):
            return jnp.where(mask, values, jnp.zeros_like(values))

        wo = ref.wo
        wo_load = pltpu.make_async_copy(ref.full_out, wo, wire.sem())

        def out_copies(i, slot):
            return tall(ref.full_down, F, i, slot, TD)

        def down_copies(i, slot):
            return [(ref.full_down.at[ds(i, T), :], wb.at[wide_slot(slot), :])]


        flat = ref.flat
        units = [(i, e) for i in range(S // RB) for e in range(2)]

        def places(i):
            return pl.ds(i * RB, RB), pl.ds(0, i * RB)

        def staggered(*phases):
            for t in range(len(units) + len(phases) - 1):
                for lag, phase in enumerate(phases):
                    if 0 <= t - lag < len(units):
                        phase(*units[t - lag])

        def attend_pair(hp):
            lanes = ds(hp, 128)

            flat[...] = QKV[2, :, lanes].T
            scores, weighted, done = {}, {}, {}

            def score(i, e):
                rows, past = places(i)
                q = only(QKV[0, rows, lanes], pair_masks[e])
                own = mm(QKV[1, rows, lanes], q, NT)
                scores[i, e] = own, mm(QKV[1, past, lanes], q, NT) if i else None

            def soften(i, e):
                own, earlier = scores.pop((i, e))
                own = jnp.where(corner, own, -1e30)
                top = jnp.max(own, 0, keepdims=True)
                if i:
                    top = jnp.maximum(top, jnp.max(earlier, 0, keepdims=True))
                    earlier = jnp.exp(earlier - top)
                own = jnp.exp(own - top)
                mass = jnp.sum(own, 0, keepdims=True)
                if i:
                    mass = mass + jnp.sum(earlier, 0, keepdims=True)
                inverse = 1.0 / mass
                LSE[hp * 2 + e, :, places(i)[0]] = top + jnp.log(mass)
                own = (own * inverse).astype(bf16)
                weighted[i, e] = own, (earlier * inverse).astype(bf16) if i else None

            def attend(i, e):
                rows, past = places(i)
                own, earlier = weighted.pop((i, e))
                values = flat.at[pl.ds(e * HD, HD), :]
                total = mm(values[:, rows], own, NN)
                if i:
                    total = total + mm(values[:, past], earlier, NN)
                done[e] = total
                if e == 1:
                    ATv[rows, lanes] = jnp.concatenate([done[0], done[1]], 0).T.astype(bf16)

            staggered(score, soften, attend)

        pairs = L // 128
        pl.loop(0, pairs // 2)(attend_pair)
        gather_mate("down")
        gather_mate("out")

        @pl.loop(pairs // 2, pairs)
        def _(hp):
            @pl.when(hp == pairs - 1)
            def _():
                for one in mates["out"] + mates["down"]:
                    one.into.wait_recv()
                wo_load.start()
                tall_ring.fill(out_copies)
                wide_ring.fill(down_copies)

            attend_pair(hp)

        for one in mates["out"] + mates["down"]:
            one.came = True
        tall_ring.primed, wide_ring.primed = 2, 1

        att_mate = wire.send(ATv, ref.mate_att, ref.mate_att, mate)
        line_step(ref.cotangent, pulled, n_mp - 1, 0, pulled_log)
        wo_load.wait()

        ob = ref.ob
        out_sems = ref.out_sems

        def put(part, half, i, slot):
            return [
                pltpu.make_async_copy(
                    ob.at[slot, pl.ds(j * R, R), :],
                    part.at[half * NH + j, :, ds(i, TD)],
                    out_sems.at[slot, j],
                )
                for j in range(NH)
            ]

        def product_half(part, other, ring, copies, value, then):
            half = 1 - mine_half if other else mine_half

            def work(i, slot):
                place_out = lax.rem(i, 2)

                @pl.when(i >= 2)
                def _():
                    for c in put(part, half, i - 2, place_out):
                        c.wait()

                for quarter in range(2):
                    v = value(sequence_half(other, quarter), slot, i)
                    ob[place_out, pl.ds(quarter * (HS // 2), HS // 2), :] = v.astype(bf16)
                for c in put(part, half, i, place_out):
                    c.start()

            ring.run(D // TD, copies, work, then)
            for i in range(D // TD - 2, D // TD):
                for c in put(part, half, i, i % 2):
                    c.wait()

        def out_value(rows, slot, i):
            v = mm(Av[rows, :], tall_value(slot, F, TD), NN)
            return v + mm(ATv[rows, :], wo[:, ds(i, TD)], NN)

        sum1 = LineSum(ref.part1, ref.below1, ref.above1)
        product_half(ref.part1, True, tall_ring, out_copies, out_value, out_copies)
        sum1.begin(False)
        line_step(ref.cotangent, pulled, n_mp - 1, 1, pulled_log)
        product_half(ref.part1, False, tall_ring, out_copies, out_value, None)
        sum1.begin(True)

        pulled_loads = Loads()
        for s in range(1, NH):
            line_arrive(pulled_log, s)
            pulled_loads.rows(pulled, Gv, s)
        YP = ref.YP
        small = ref.small
        small[...] = jnp.zeros_like(small)
        act_mate.arrive()
        cot_copy.wait()
        pulled_loads.wait()
        half_a = sequence_half(False)
        half_b = sequence_half(True)

        def mate_half(half):
            return wire.send(
                Gv.at[half, :], ref.mate_pulled.at[half, :], ref.mate_pulled.at[half, :], mate
            )

        def load_mate_columns(source, rows):
            return [
                wire.local(source.at[rows, ds(flip(me, m), CD)], YP.at[n, rows, :])
                for n, m in enumerate(masks)
            ]

        pulled_a = mate_half(half_a)
        for s in range(NH, n_mp):
            line_arrive(pulled_log, s)
            pulled_loads.rows(pulled, Gv, s)

        def pushed_half(other, then):
            def work(i, slot):
                cols = ds(i, T)
                total = small[4:5, cols]
                for quarter in range(2):
                    rows = sequence_half(other, quarter)
                    d = mm(Gv[rows, :], wb[wide_slot(slot), :], NT) * Hv[rows, cols].astype(f32)
                    d = d.astype(bf16)
                    Hv[rows, cols] = d
                    total = total + jnp.sum(d.astype(f32), 0, keepdims=True)
                small[4:5, cols] = total

            wide_ring.run(F // T, down_copies, work, then)

        pushed_half(False, down_copies)
        pulled_a.arrive()
        mate_columns = load_mate_columns(ref.mate_pulled, half_a)
        pulled_loads.wait()
        pulled_b = mate_half(half_b)
        pushed_half(True, None)
        hid_mate = wire.send(Hv, ref.mate_hid, ref.mate_hid, mate)
        mate_tiles = [wire.local(ref.mate_act, wb.at[:, pl.ds(0, F)])]
        att_mate.arrive()
        mate_load = wire.local(ref.mate_att, wa.at[0, pl.ds(0, S), pl.ds(0, L)])
        pulled_b.arrive()
        mate_columns = mate_columns + load_mate_columns(ref.mate_pulled, half_b)
        DMv = ref.DMv
        for half in range(2):
            rows = pl.ds(half * HS, HS)
            ob[half, :, 0:L] = mm(Gv[rows, :], wo[...], NT).astype(bf16)
        for c in mate_tiles + mate_columns:
            c.wait()

        grad_info = {
            "down": (ref.gw_down, ref.rb_down, ref.st_down, ref.ta_down, F // 2, 128),
            "out": (ref.gw_out, ref.rb_out, ref.st_down.at[:, pl.ds(0, L)], ref.ta_down.at[:, :, pl.ds(0, L // 2)], L // 2, 128),
            "up": (ref.gw_up, ref.rb_up, ref.st_up, ref.ta_up, CD // 2, 16),
            "qkv": (ref.gw_qkv, ref.rb_qkv, ref.st_up, ref.ta_up, CD // 2, 16),
        }
        offset, position = 0, []
        for i in range(len(bits)):
            position.append(offset)
            offset += 2 ** (len(bits) - 1 - i)

        def half_of(w, chunk, h):
            return half_rows_of(chunk, grad_info[w][4], h, w == "qkv")

        came = {}

        def scatter_send(w, h, i, m):
            gw, rb = grad_info[w][:2]
            rest = span(orders[h][i + 1 :])
            keep = m - orders[h][i]
            got = half_of(w, rb.at[position[i] + rest.index(keep)], h)
            came[(w, h, i, keep)] = wire.send(
                half_of(w, gw.at[place[m]], h), got, got, (flip(me, orders[h][i]), z)
            )

        def scatter_first(w, m):
            for h in range(2):
                if m & orders[h][0]:
                    scatter_send(w, h, 0, m)

        def scatter_step(w, i):
            gw, rb, _, ta, n, block = grad_info[w]
            wide = 3 * L if w == "qkv" else ta.shape[-1]
            for k in range(2 ** (len(bits) - 1 - i)):
                work = []
                for h in range(2):
                    way = orders[h]
                    m = way[i] + span(way[i + 1 :])[k]
                    terms = []
                    for e in range(i):
                        came[(w, h, e, m)].arrive()
                        rest = span(way[e + 1 :])
                        terms.append(half_of(w, rb.at[position[e] + rest.index(m)], h))
                    home = half_of(w, gw.at[place[m]], h)
                    first = moves(w, home, ta.at[h, 0], 9 * h, False)
                    first = first + moves(w, terms[0], ta.at[h, 1], 9 * h + 3, False)
                    for c in first:
                        c.start()
                    work.append((h, m, home, terms, first))
                for h, m, home, terms, first in work:
                    for c in first:
                        c.wait()
                    add_rows(ta.at[h, 0], [ta.at[h, 0], ta.at[h, 1]], n, block, wide)
                    for term in terms[1:]:
                        run(moves(w, term, ta.at[h, 1], 9 * h + 3, False))
                        add_rows(ta.at[h, 0], [ta.at[h, 0], ta.at[h, 1]], n, block, wide)
                    for c in moves(w, home, ta.at[h, 0], 9 * h + 6, True):
                        c.start()
                for h, m, home, terms, first in work:
                    for c in moves(w, home, ta.at[h, 0], 9 * h + 6, True):
                        c.wait()
                    scatter_send(w, h, i, m)

        def scatter_done(w):
            for h in range(2):
                for i in range(len(bits)):
                    came[(w, h, i, 0)].arrive()

        finals = {
            "down": (ref.grad_down, ref.gs),
            "out": (ref.grad_out, ref.gs),
            "up": (ref.grad_up, ref.gt),
            "qkv": ([ref.grad_q, ref.grad_k, ref.grad_v], ref.gt),
        }

        def weight_sum(w):
            gw, rb, st, ta, n, _ = grad_info[w]
            out, staged = finals[w]
            scatter_done(w)
            near = [st.at[0], st.at[1]]
            far = [gw.at[place[0]]] + [rb.at[position[i]] for i in range(len(bits))]
            first = moves(w, far[0], near[0], 0, False) + moves(w, far[1], near[1], 3, False)
            for c in first:
                c.start()
            rest = []
            for q, source in enumerate(far[2:]):
                for h in range(2):
                    rest += moves(w, half_of(w, source, h), ta.at[h, q], 6 + 6 * q + 3 * h, False)
            for c in rest:
                c.start()
            for c in first + rest:
                c.wait()
            block = min(n, staged.shape[1])
            wide = 3 * L if w == "qkv" else gw.shape[-1]

            def out_of(h, i, slot):
                rows = pl.ds(pl.multiple_of(h * n + i * block, block), block)
                if w == "qkv":
                    return [
                        pltpu.make_async_copy(
                            staged.at[slot, pl.ds(0, block), pl.ds(j * L, L)],
                            out[j].at[rows, :],
                            slot_sems.at[18 + 3 * slot + j],
                        )
                        for j in range(3)
                    ]
                return [
                    pltpu.make_async_copy(
                        staged.at[slot, pl.ds(0, block), pl.ds(0, wide)],
                        out.at[rows, :],
                        slot_sems.at[18 + 3 * slot],
                    )
                ]

            count = n // block
            for h in range(2):

                @pl.loop(0, count)
                def _(i):
                    slot = lax.rem(h * count + i, 2)
                    rows = pl.ds(pl.multiple_of(h * n + i * block, block), block)
                    inner = pl.ds(pl.multiple_of(i * block, block), block)

                    def again():
                        for c in out_of(h, i, slot):
                            c.wait()

                    maybe_static(h * count + i >= 2, again)
                    total = st[0, rows, 0:wide].astype(f32) + st[1, rows, 0:wide].astype(f32)
                    for q in range(len(far) - 2):
                        total = total + ta[h, q, inner, 0:wide].astype(f32)
                    staged[slot, 0:block, 0:wide] = total
                    for c in out_of(h, i, slot):
                        c.start()

            for slot in range(min(2, 2 * count)):
                for c in out_of(0, 0, slot):
                    c.wait()

        def grad_chunks(*jobs, between=None):
            pending = []

            def settle():
                for w, m, copies in pending:
                    for c in copies:
                        c.wait()
                    scatter_first(w, m)
                pending.clear()

            for n, m in enumerate(masks):
                slot = n % 2
                fresh = []
                for number, (w, work, st) in enumerate(jobs):
                    gw = grad_info[w][0]
                    work(m, flip(me, m), st.at[slot])
                    copies = moves(w, gw.at[place[m]], st.at[slot], 6 * number + 3 * slot, True)
                    for c in copies:
                        c.start()
                    if number == 0:
                        settle()
                    fresh.append((w, m, copies))
                pending.extend(fresh)
                if between is not None and n == len(masks) // 2:
                    between()
            settle()

        def grad_down(m, k, st):
            @pl.loop(0, F // T)
            def _(i):
                v = mm(Av[:, ds(i, T)], Gv[:, ds(k, CD)], TN)
                v = v + mm(wb[:, ds(i, T)], YP[place[m]], TN)
                st[ds(i, T), :] = v.astype(bf16)


        def grad_out(m, k, st):
            v = mm(ATv[...], Gv[:, ds(k, CD)], TN)
            v = v + mm(wa[0, 0:S, 0:L], YP[place[m]], TN)
            st[...] = v.astype(bf16)

        mate_load.wait()
        grad_chunks(
            ("down", grad_down, ref.st_down), ("out", grad_out, ref.ta_down.at[:, 1, pl.ds(0, L)])
        )
        sum1.step(1)
        def back_copies(i, slot):
            rows = ds(i, TD)
            return [(ref.full_up.at[rows, :], wb.at[wide_slot(slot), pl.ds(0, F)])] + [
                (ref.full_qkv.at[j, rows, :], wa.at[slot, pl.ds(j * TD, TD), pl.ds(0, L)])
                for j in range(3)
            ]

        def back_value(rows, slot, i):
            v = mm(Hv[rows, :], wb[wide_slot(slot), 0:F], NT)
            for j in range(3):
                w = wa[slot, j * TD : (j + 1) * TD, 0:L]
                v = v + mm(DMv[rows, j * L : (j + 1) * L], w, NT)
            return v

        back_ring = Ring(2, 24)
        back_ring.prime(back_copies)
        dk, dv = ref.dk, ref.dv

        @pl.loop(0, L // 128)
        def _(hp):
            lanes = ds(hp, 128)
            flat[...] = QKV[1, :, lanes].T
            dk[...] = jnp.zeros_like(dk)
            dv[...] = jnp.zeros_like(dv)
            scores, slopes, done = {}, {}, {}

            def score(i, e):
                rows, past = places(i)
                q = only(QKV[0, rows, lanes], pair_masks[e])
                do = ob[i * RB // HS, i * RB % HS : i * RB % HS + RB, lanes]
                do = only(do, pair_masks[e])
                found = [q, do]
                for where in [rows, past][: 1 + (i > 0)]:
                    found += [mm(QKV[1, where, lanes], q, NT), mm(QKV[2, where, lanes], do, NT)]
                scores[i, e] = found

            def slope(i, e):
                q, do, s, dp, *earlier = scores.pop((i, e))
                log_mass = LSE[hp * 2 + e, :, places(i)[0]]
                p = jnp.where(corner, jnp.exp(s - log_mass), 0.0)
                delta = jnp.sum(p * dp, 0, keepdims=True)
                if i:
                    s2, dp2 = earlier
                    p2 = jnp.exp(s2 - log_mass)
                    delta = delta + jnp.sum(p2 * dp2, 0, keepdims=True)
                found = [q, do, (p * (dp - delta)).astype(bf16), p.astype(bf16)]
                if i:
                    found += [(p2 * (dp2 - delta)).astype(bf16), p2.astype(bf16)]
                slopes[i, e] = found

            def push(i, e):
                rows, past = places(i)
                q, do, s, p, *earlier = slopes.pop((i, e))
                keys = flat.at[pl.ds(e * HD, HD), :]
                dk[rows, :] += mm(s, q, NN)
                dv[rows, :] += mm(p, do, NN)
                dq = mm(keys[:, rows], s, NN)
                if i:
                    s2, p2 = earlier
                    dk[past, :] += mm(s2, q, NN)
                    dv[past, :] += mm(p2, do, NN)
                    dq = dq + mm(keys[:, past], s2, NN)
                done[e] = dq
                if e == 1:
                    dq = jnp.concatenate([done[0], done[1]], 0).T * HD**-0.5
                    DMv[rows, lanes] = turn(dq, rows, -1.0).astype(bf16)

            staggered(score, slope, push)
            DMv[:, ds(hp + L // 128, 128)] = turn(dk[...], pl.ds(0, S), -1.0).astype(bf16)
            DMv[:, ds(hp + 2 * (L // 128), 128)] = dv[...].astype(bf16)

        mix_mate = wire.send(DMv, ref.mate_mix, ref.mate_mix, mate)
        for i in range(1, len(bits)):
            scatter_step("down", i)

        sum2 = LineSum(ref.part2, ref.below2, ref.above2)
        product_half(ref.part2, True, back_ring, back_copies, back_value, None)
        sum2.begin(False)
        hid_mate.arrive()
        mate_tiles = [wire.local(ref.mate_hid, wb.at[:, pl.ds(0, F)])]

        normed_mate.arrive()
        mate_columns = load_mate_columns(ref.mate_normed, pl.ds(0, S))
        small[3:4, pl.ds(0, 3 * L)] = sum_rows_of(DMv, S)
        for tau in range(2, n_mp - 1):
            sum1.step(tau)
        for c in mate_tiles + mate_columns:
            c.wait()

        def grad_up(m, k, st):
            @pl.loop(0, F // WT)
            def _(i):
                v = mm(Nv[:, ds(k, CD)], Hv[:, ds(i, WT)], TN)
                v = v + mm(YP[place[m]], wb[:, ds(i, WT)], TN)
                st[:, ds(i, WT)] = v.astype(bf16)

        grad_chunks(("up", grad_up, ref.st_up))
        back_ring.prime(back_copies)

        small_b, small_b_all = ref.small_b, ref.small_b_all
        for n in range(nq):
            small_b[n : n + 1, :] = small[3:4, n * VB : (n + 1) * VB]
        for n in range(nu):
            small_b[nq + n : nq + n + 1, :] = small[4:5, n * VB : (n + 1) * VB]
        for n in range(nq + nu, 8):
            small_b[n : n + 1, :] = jnp.zeros((1, VB), f32)
        biases = []
        for m in range(1, n_dp):
            k = flip(me, m)
            biases.append(wire.send(small_b, small_b_all.at[me], small_b_all.at[k], (k, z)))
        product_half(ref.part2, False, back_ring, back_copies, back_value, None)
        sum2.begin(True)

        sum2.step(1)
        mix_mate.arrive()
        loads_mix = [wire.local(ref.mate_mix, wb.at[:, pl.ds(0, 3 * L)])]
        for i in range(1, len(bits)):
            scatter_step("out", i)
        for c in loads_mix:
            c.wait()

        def grad_qkv(m, k, st):
            v = mm(Nv[:, ds(k, CD)], DMv[...], TN)
            v = v + mm(YP[place[m]], wb[:, 0 : 3 * L], TN)
            st[:, 0 : 3 * L] = v.astype(bf16)

        grad_chunks(("qkv", grad_qkv, ref.st_up))

        zs = ref.zs
        sum1.arrive()
        sum1.load(zs)
        @pl.loop(0, R // LB)
        def _(i):
            rows = ds(i, LB)
            v = tok[rows, :].astype(f32) + vrow[2:3, :]
            v = v + zs[0, rows, :].astype(f32)
            v = v + zs[1, rows, :].astype(f32) + zs[2, rows, :].astype(f32)
            zs[0, rows, :] = v.astype(bf16)

        lo_copy = wire.local(zs.at[0], ref.layer_out)
        small[2:3, :] = sum_rows_of(Gv, S)
        lo_copy.wait()


        for i in range(1, len(bits)):
            scatter_step("up", i)
        for tau in range(2, n_mp - 1):
            sum2.step(tau)
        for i in range(1, len(bits)):
            scatter_step("qkv", i)
        for w in ("down", "out"):
            weight_sum(w)
        for one in biases:
            one.arrive()
        total = small_b[...]
        for m in range(1, n_dp):
            total = total + small_b_all[flip(me, m)]
        ref.bias_sums[...] = total

        weight_sum("up")
        sum2.arrive()
        sum2.load(zs)
        gt = ref.gt

        def gt_copy(i, slot):
            return pltpu.make_async_copy(
                gt.at[slot], ref.grad_tokens.at[ds(i, LB), :], slot_sems.at[slot]
            )

        @pl.loop(0, R // LB)
        def _(i):
            slot = lax.rem(i, 2)
            rows = ds(i, LB)
            _, xhat, scale = stats(rows)
            d = zs[0, rows, :].astype(f32) + zs[1, rows, :].astype(f32)
            d = d + zs[2, rows, :].astype(f32)
            small[0:1, :] += jnp.sum(d * xhat, 0, keepdims=True)
            small[1:2, :] += jnp.sum(d, 0, keepdims=True)
            e = d * vrow[0:1, :]
            centre = jnp.mean(e, -1, keepdims=True)
            along = jnp.mean(e * xhat, -1, keepdims=True)

            @pl.when(i >= 2)
            def _():
                gt_copy(i - 2, slot).wait()

            own = Gv[pl.ds(pl.multiple_of(z * R + i * LB, LB), LB), :].astype(f32)
            gt[slot] = own + scale * (e - centre - xhat * along)
            gt_copy(i, slot).start()

        for i in range(max(0, R // LB - 2), R // LB):
            gt_copy(i, i % 2).wait()
        small_k, small_all = ref.small_k, ref.small_all
        for k in range(n_dp):
            small_k[k] = small[:, k * CD : (k + 1) * CD]
        across = []
        for m in range(1, n_dp):
            k = flip(me, m)
            across.append(wire.send(small_k.at[k], small_all.at[me], small_all.at[k], (k, z)))
        weight_sum("qkv")
        for one in across:
            one.arrive()
        total = small_k[me]
        for m in range(1, n_dp):
            total = total + small_all[flip(me, m)]
        small_own, small_mp = ref.small_own, ref.small_mp
        small_own[...] = total
        across = []
        for k in range(1, n_mp):
            to = lax.rem(z + k, n_mp)
            across.append(wire.send(small_own, small_mp.at[k], small_mp.at[k], (me, to)))
        for one in across:
            one.arrive()
        others = small_mp[1]
        for k in range(2, n_mp):
            others = others + small_mp[k]
        first_two = lax.broadcasted_iota(jnp.int32, (8, 1), 0) < 2
        ref.row_sums[...] = total + jnp.where(first_two, others, 0.0)
        sum1.finish()
        sum2.finish()
        wire.finish()

    return kernel


def sum_rows_of(array, rows):
    total = None
    for i in range(rows // 128):
        part = jnp.sum(array[pl.ds(i * 128, 128), :].astype(f32), 0, keepdims=True)
        total = part if total is None else total + part
    return total


def rope_tables(length):
    places = np.arange(length, dtype=np.float64)
    inverse = 10000.0 ** (-np.arange(0, ROT, 2, dtype=np.float64) / ROT)
    angles = places[:, None] * inverse[None, :]
    cosine, sine = np.cos(angles), np.sin(angles)
    rest = np.zeros((length, HD - ROT))
    c = np.concatenate([cosine, cosine, rest + 1.0], -1)
    s = np.concatenate([-sine, sine, rest], -1)
    return [np.concatenate([t, t], -1).astype(np.float32) for t in (c, s)]


def make_body(n_dp, n_mp):
    def body(
        tokens, ln_gain, ln_bias, w_qkv, b_qkv, w_out, b_out, w_up, b_up, w_down, b_down, cotangent
    ):
        me = lax.axis_index("dp")
        R = tokens.shape[0]
        S = R * n_mp
        CD = D // n_dp
        NC = n_dp // 2
        F = w_up.shape[1]
        L = w_qkv.shape[2]
        heads = b_qkv.shape[1]
        share = HD // n_dp
        T = min(512, F)
        TD = 512
        nq, nu = -(-3 * L // VB), F // VB

        def spread(shape, own, axis, rows):
            whole = lax.dynamic_update_slice_in_dim(
                jnp.zeros(shape, f32), own.astype(f32), me * share, axis
            ).reshape(-1)
            return jnp.pad(whole, (0, rows * VB - whole.shape[0])).reshape(rows, VB)

        vec_a = jnp.stack(
            [ln_gain.astype(f32), ln_bias.astype(f32), b_out.astype(f32) + b_down.astype(f32)]
        )
        vec_a = jnp.pad(vec_a, ((0, 5), (0, 0)))
        vec_b = jnp.concatenate(
            [
                spread((3, heads, HD), b_qkv, 2, nq),
                spread((F // HD, HD), b_up, 1, nu),
                jnp.zeros((8 - nq - nu, VB), f32),
            ],
            0,
        )
        rope_c, rope_s = rope_tables(S)
        ins = dict(
            tokens=tokens,
            cotangent=cotangent,
            vec_a=vec_a,
            vec_b=vec_b,
            w_up=w_up,
            w_qkv=w_qkv.transpose(1, 0, 2),
            w_down=w_down,
            w_out=w_out,
            rope_c=jnp.asarray(rope_c),
            rope_s=jnp.asarray(rope_s),
        )
        any_spec = pl.BlockSpec(memory_space=pl.ANY)
        vmem_spec = pl.BlockSpec(memory_space=pltpu.VMEM)
        outs = dict(
            layer_out=((R, D), bf16),
            grad_tokens=((R, D), f32),
            row_sums=((8, CD), f32),
            bias_sums=((8, VB), f32),
            grad_up=((CD, F), f32),
            grad_q=((CD, L), f32),
            grad_k=((CD, L), f32),
            grad_v=((CD, L), f32),
            grad_down=((F, CD), f32),
            grad_out=((L, CD), f32),
            gw_up=((NC, CD, F), bf16),
            gw_qkv=((NC, 3, CD, L), bf16),
            gw_down=((NC, F, CD), bf16),
            gw_out=((NC, L, CD), bf16),
            rb_up=((NC - 1, CD, F), bf16),
            rb_qkv=((NC - 1, 3, CD, L), bf16),
            rb_down=((NC - 1, F, CD), bf16),
            rb_out=((NC - 1, L, CD), bf16),
            full_up=((D, F), bf16),
            full_qkv=((3, D, L), bf16),
            full_down=((F, D), bf16),
            full_out=((L, D), bf16),
            full_normed=((n_mp, R, D), bf16),
            full_pulled=((n_mp, R, D), bf16),
            mate_normed=((S, D), bf16),
            mate_pulled=((S, D), bf16),
            mate_act=((S, F), bf16),
            mate_hid=((S, F), bf16),
            mate_att=((S, L), bf16),
            mate_mix=((S, 3 * L), bf16),
            part1=((n_mp, R, D), bf16),
            below1=((n_mp, R, D), bf16),
            above1=((n_mp, R, D), bf16),
            part2=((n_mp, R, D), bf16),
            below2=((n_mp, R, D), bf16),
            above2=((n_mp, R, D), bf16),
        )
        n_sems = 33 * (n_dp + n_mp)
        scratch = dict(
            vec_a_all=pltpu.VMEM((n_dp, 8, CD), f32),
            vec_b_all=pltpu.VMEM((n_dp, 8, VB), f32),
            vrow=pltpu.VMEM((8, D), f32),
            small=pltpu.VMEM((8, D), f32),
            small_k=pltpu.VMEM((n_dp, 8, CD), f32),
            small_all=pltpu.VMEM((n_dp, 8, CD), f32),
            small_own=pltpu.VMEM((8, CD), f32),
            small_mp=pltpu.VMEM((n_mp, 8, CD), f32),
            small_b=pltpu.VMEM((8, VB), f32),
            small_b_all=pltpu.VMEM((n_dp, 8, VB), f32),
            tok=pltpu.VMEM((R, D), bf16),
            gt=pltpu.VMEM((2, LB, D), f32),
            gs=pltpu.VMEM((2, min(256, L // 2), CD), f32),
            tc=pltpu.VMEM((S, 128), f32),
            ts=pltpu.VMEM((S, 128), f32),
            Nv=pltpu.VMEM((S, D), bf16),
            Gv=pltpu.VMEM((S, D), bf16),
            Av=pltpu.VMEM((S, F), bf16),
            Hv=pltpu.VMEM((S, F), bf16),
            QKV=pltpu.VMEM((3, S, L), bf16),
            ATv=pltpu.VMEM((S, L), bf16),
            flat=pltpu.VMEM((128, S), bf16),
            DMv=pltpu.VMEM((S, 3 * L), bf16),
            LSE=pltpu.VMEM((heads, 1, S), f32),
            dk=pltpu.VMEM((S, 128), f32),
            dv=pltpu.VMEM((S, 128), f32),
            wa=pltpu.VMEM((3, D, T), bf16),
            wb=pltpu.VMEM((2 * T, D), bf16),
            wo=pltpu.VMEM((L, D), bf16),
            ob=pltpu.VMEM((2, S // 2, TD), bf16),
            YP=pltpu.VMEM((NC, S, CD), bf16),
            zs=pltpu.VMEM((3, R, D), bf16),
            st_up=pltpu.VMEM((2, CD, F), bf16),
            st_down=pltpu.VMEM((2, F, CD), bf16),
            ta_up=pltpu.VMEM((2, 2, CD // 2, F), bf16),
            ta_down=pltpu.VMEM((2, 2, F // 2, CD), bf16),
            sems=pltpu.SemaphoreType.DMA((n_sems,)),
            slot_sems=pltpu.SemaphoreType.DMA((32,)),
            out_sems=pltpu.SemaphoreType.DMA((2, n_mp)),
        )
        names = list(ins) + list(outs) + list(scratch)
        got = pl.pallas_call(
            make_kernel(n_dp, n_mp, R, F, L, names, n_sems),
            out_shape=[jax.ShapeDtypeStruct(s, t) for s, t in outs.values()],
            in_specs=[any_spec] * len(ins),
            out_specs=[vmem_spec if n.endswith("_sums") else any_spec for n in outs],
            scratch_shapes=list(scratch.values()),
            name="layer",
            cost_estimate=pl.CostEstimate(
                flops=6 * S * D * (4 * L + 2 * F), bytes_accessed=150 << 20, transcendentals=0
            ),
            compiler_params=pltpu.CompilerParams(
                collective_id=0, has_side_effects=True, vmem_limit_bytes=62 << 20
            ),
        )(*ins.values())
        got = types.SimpleNamespace(**dict(zip(outs, got)))

        def mine(values, axis):
            return lax.dynamic_slice_in_dim(values, me * share, share, axis)

        sums = got.bias_sums.reshape(-1)
        bias = got.row_sums[2]
        return (
            got.layer_out,
            got.grad_tokens,
            got.row_sums[0],
            got.row_sums[1],
            jnp.stack([got.grad_q, got.grad_k, got.grad_v], 1),
            mine(sums[: 3 * L].reshape(3, heads, HD), 2),
            got.grad_out,
            bias,
            got.grad_up,
            mine(sums[nq * VB : nq * VB + F].reshape(F // HD, HD), 1),
            got.grad_down,
            bias,
        )

    return body


def solution(mesh):
    n_dp, n_mp = mesh.shape["dp"], mesh.shape["mp"]
    weights_in = (
        P("dp"),
        P("dp"),
        P("dp", None, "mp"),
        P(None, "mp", "dp"),
        P("mp", "dp"),
        P("dp"),
        P("dp", "mp"),
        P("mp", "dp"),
        P("mp", "dp"),
        P("dp"),
    )
    rows = P(("dp", "mp"), None)
    return jax.shard_map(
        make_body(n_dp, n_mp),
        mesh=mesh,
        in_specs=(rows,) + weights_in + (rows,),
        out_specs=(rows, rows) + weights_in,
        check_vma=False,
    )
```

```python
import types

import jax
import jax.numpy as jnp
import numpy as np
from jax import lax
from jax.experimental import pallas as pl
from jax.experimental.pallas import tpu as pltpu
from jax.sharding import PartitionSpec as P

D = 2048
HD = 64
ROT = 32
EPS = 1e-05
BQ = 256
LB = 32
VB = 512
MESH = pl.DeviceIdType.MESH
NN = (((1,), (0,)), ((), ()))
NT = (((1,), (1,)), ((), ()))
TN = (((0,), (0,)), ((), ()))
bf16 = jnp.bfloat16
f32 = jnp.float32


def mm(left, right, dims):
    return lax.dot_general(left, right, dims, preferred_element_type=f32)


def flip(index, mask):
    bit = 1
    while bit <= mask:
        if mask & bit:
            index = index + bit * (1 - 2 * lax.rem(lax.div(index, bit), 2))
        bit *= 2
    return index


def span(bits):
    found = [0]
    for bit in bits:
        found = found + [m + bit for m in found]
    return found


def maybe_static(pred, act):
    if isinstance(pred, bool):
        if pred:
            act()
    else:
        pl.when(pred)(act)


def maybe(pred, act):
    if pred is None:
        act()
    else:
        pl.when(pred)(act)


class Sent:
    def __init__(self, out, into, pred_out, pred_into):
        self.out, self.into, self.pred_out, self.pred_into = out, into, pred_out, pred_into
        self.came, self.left = False, False

    def start(self):
        maybe(self.pred_out, self.out.start)

    def arrive(self):
        if not self.came:
            self.came = True
            maybe(self.pred_into, self.into.wait_recv)

    def finish(self):
        if not self.left:
            self.left = True
            maybe(self.pred_out, self.out.wait_send)


class Wire:
    def __init__(self, sems, count):
        self.sems, self.count, self.used, self.open = sems, count, 0, []

    def sem(self):
        assert self.used < self.count
        self.used += 1
        return self.sems.at[self.used - 1]

    def sems_of(self, n):
        assert self.used + n <= self.count
        self.used += n
        base = self.used - n
        return lambda j: self.sems.at[base + j]

    def send(self, src, dst, got, dev, pred_out=None, pred_into=None):
        s, r = self.sem(), self.sem()
        out = pltpu.make_async_remote_copy(src, dst, s, r, dev, MESH)
        into = pltpu.make_async_remote_copy(got, got, s, r, dev, MESH)
        one = Sent(out, into, pred_out, pred_into)
        one.start()
        self.open.append(one)
        return one

    def local(self, src, dst):
        copy = pltpu.make_async_copy(src, dst, self.sem())
        copy.start()
        return copy

    def finish(self):
        for one in self.open:
            one.finish()


def make_kernel(n_dp, n_mp, R, F, L, names, n_sems):
    S = R * n_mp
    CD = D // n_dp
    NC = n_dp // 2
    T = min(512, F)
    TD = 512
    HS = S // 2
    NH = n_mp // 2
    bits = [b for b in (2, 4, 8, 16, 32) if b < n_dp]
    orders = [bits, bits[1:] + bits[:1]]
    masks = sorted(span(bits), key=lambda m: -bin(m).count("1"))
    place = {m: n for n, m in enumerate(masks)}
    RB = min(BQ, S)

    def kernel(*refs):
        ref = types.SimpleNamespace(**dict(zip(names, refs)))
        me = lax.axis_index("dp")
        z = lax.axis_index("mp")
        wire = Wire(ref.sems, n_sems)
        slot_sems = ref.slot_sems
        mate = (flip(me, 1), z)
        up_dev = (me, jnp.minimum(z + 1, n_mp - 1))
        down_dev = (me, jnp.maximum(z - 1, 0))
        mine_half = lax.div(z, NH)
        barrier = pltpu.get_barrier_semaphore()
        for m in range(1, n_dp):
            pl.semaphore_signal(barrier, inc=1, device_id=(flip(me, m), z), device_id_type=MESH)
        for k in range(1, n_mp):
            pl.semaphore_signal(
                barrier, inc=1, device_id=(me, lax.rem(z + k, n_mp)), device_id_type=MESH
            )
        pl.semaphore_wait(barrier, n_dp - 1 + n_mp - 1)

        def ds(k, size):
            return pl.ds(pl.multiple_of(k * size, size), size)

        def run(copies):
            for c in copies:
                c.start()
            for c in copies:
                c.wait()

        def pieces_of(full, rows, kind):
            half = rows // 2

            def piece(k, h):
                if kind == "rows":
                    if h is None:
                        return full.at[ds(k, rows), :]
                    return full.at[pl.ds(pl.multiple_of(k * rows + h * half, half), half), :]
                if kind == "cube":
                    if h is None:
                        return full.at[:, ds(k, rows), :]
                    return full.at[:, pl.ds(pl.multiple_of(k * rows + h * half, half), half), :]
                if h is None:
                    return full.at[:, ds(k, CD)]
                return full.at[pl.ds(h * half, half), ds(k, CD)]

            return piece

        def half_rows_of(array, n, h, cube):
            if cube:
                return array.at[:, pl.ds(h * n, n), :]
            return array.at[pl.ds(h * n, n), :]

        weights = {
            "up": (ref.w_up, pieces_of(ref.full_up, CD, "rows"), CD // 2, ref.st_up.at[0]),
            "qkv": (ref.w_qkv, pieces_of(ref.full_qkv, CD, "cube"), CD // 2, ref.st_up.at[1]),
            "down": (ref.w_down, pieces_of(ref.full_down, F, "cols"), F // 2, ref.st_down.at[0]),
            "out": (ref.w_out, pieces_of(ref.full_out, L, "cols"), L // 2, ref.st_down.at[1, pl.ds(0, L)]),
        }
        order = ["up", "qkv", "down", "out"]
        arrivals = {w: [[] for _ in bits] for w in order}

        mates = {w: [] for w in order}

        def to_mate(w, j):
            piece = weights[w][1]
            for h in range(2):
                way = orders[h]
                for sub in span(way[:j]):
                    k = flip(flip(me, sub), way[j])
                    got = piece(flip(k, 1), h)
                    mates[w].append(wire.send(piece(k, h), piece(k, h), got, mate))

        def gather_step(w, j):
            own, piece, n, _ = weights[w]
            if j > 0:
                for one in arrivals[w][j - 1]:
                    one.arrive()
            for h in range(2):
                way = orders[h]
                for sub in span(way[:j]):
                    k = flip(me, sub)
                    src = half_rows_of(own, n, h, w == "qkv") if sub == 0 else piece(k, h)
                    got = piece(flip(k, way[j]), h)
                    arrivals[w][j].append(wire.send(src, piece(k, h), got, (flip(me, way[j]), z)))
            if j > 0:
                to_mate(w, j - 1)
            else:
                got = piece(flip(me, 1), None)
                mates[w].append(wire.send(own, piece(me, None), got, mate))

        def gather_mate(w):
            for one in arrivals[w][-1]:
                one.arrive()
            to_mate(w, len(bits) - 1)

        def gathered(w):
            for one in mates[w]:
                one.arrive()

        def moves(w, far, near, base, out):
            pairs = [(far, near)]
            if w == "qkv":
                pairs = [(far.at[j], near.at[:, pl.ds(j * L, L)]) for j in range(3)]
            return [
                pltpu.make_async_copy(*(p[::-1] if out else p), slot_sems.at[base + n])
                for n, p in enumerate(pairs)
            ]

        hr = R // 2

        def line_step(own, full, s, hh, log):
            rows = pl.ds(hh * hr, hr)
            if s > 1:
                for one in log[(s - 1, hh)]:
                    one.arrive()
            up, down = z - (s - 1), z + (s - 1)
            first = own.at[rows, :] if s == 1 else None
            one = wire.send(
                first if s == 1 else full.at[jnp.maximum(up, 0), rows, :],
                full.at[jnp.maximum(up, 0), rows, :],
                full.at[jnp.maximum(z - s, 0), rows, :],
                up_dev,
                jnp.logical_and(z + 1 < n_mp, up >= 0),
                z - s >= 0,
            )
            two = wire.send(
                first if s == 1 else full.at[jnp.minimum(down, n_mp - 1), rows, :],
                full.at[jnp.minimum(down, n_mp - 1), rows, :],
                full.at[jnp.minimum(z + s, n_mp - 1), rows, :],
                down_dev,
                jnp.logical_and(z >= 1, down < n_mp),
                z + s < n_mp,
            )
            log[(s, hh)] = [one, two]

        def line_arrive(log, s):
            for hh in range(2):
                for one in log[(s, hh)]:
                    one.arrive()

        class Loads:
            def __init__(self):
                self.open = []

            def rows(self, full, near, s):
                for c, pred in ((z - s, z - s >= 0), (z + s, z + s < n_mp)):
                    safe = jnp.clip(c, 0, n_mp - 1)
                    copy = pltpu.make_async_copy(full.at[safe], near.at[ds(safe, R), :], wire.sem())
                    maybe(pred, copy.start)
                    self.open.append((copy, pred))

            def wait(self):
                for copy, pred in self.open:
                    maybe(pred, copy.wait)
                self.open = []

        def add_rows(out, terms, count, block, wide):
            @pl.loop(0, count // block)
            def _(i):
                rows = pl.ds(pl.multiple_of(i * block, block), block)
                total = terms[0][rows, 0:wide].astype(f32)
                for term in terms[1:]:
                    total = total + term[rows, 0:wide].astype(f32)
                out[rows, 0:wide] = total.astype(out.dtype)

        class LineSum:
            def __init__(self, part, from_below, from_above):
                self.part, self.below, self.above = part, from_below, from_above
                self.us, self.ur = wire.sems_of(n_mp), wire.sems_of(n_mp)
                self.ds, self.dr = wire.sems_of(n_mp), wire.sems_of(n_mp)

            def up(self, j):
                return pltpu.make_async_remote_copy(
                    self.part.at[j], self.below.at[j], self.us(j), self.ur(j), up_dev, MESH
                )

            def down(self, j):
                return pltpu.make_async_remote_copy(
                    self.part.at[j], self.above.at[j], self.ds(j), self.dr(j), down_dev, MESH
                )

            def begin(self, near):
                @pl.when(z == 0)
                def _():
                    for j in range(n_mp - 1, 0, -1):
                        if (j < NH) == near:
                            self.up(j).start()

                @pl.when(z == n_mp - 1)
                def _():
                    for j in range(n_mp - 1):
                        if (j >= NH) == near:
                            self.down(j).start()

            def merge(self, j, got):
                a, b = ref.zs.at[0], ref.zs.at[1]
                one = pltpu.make_async_copy(self.part.at[j], a, slot_sems.at[4])
                two = pltpu.make_async_copy(got.at[j], b, slot_sems.at[5])
                run([one, two])
                add_rows(a, [a, b], R, LB, D)
                run([pltpu.make_async_copy(a, self.part.at[j], slot_sems.at[4])])

            def step(self, tau):
                j = n_mp - 1 - tau + z

                @pl.when(jnp.logical_and(z > 0, jnp.logical_and(j < n_mp, tau >= z)))
                def _():
                    self.up(j).wait_recv()
                    self.merge(j, self.below)
                    self.up(j).start()

                i = tau - (n_mp - 1 - z)

                @pl.when(jnp.logical_and(z < n_mp - 1, i >= 0))
                def _():
                    self.down(i).wait_recv()
                    self.merge(i, self.above)
                    self.down(i).start()

            def arrive(self):
                @pl.when(z > 0)
                def _():
                    self.up(z).wait_recv()

                @pl.when(z < n_mp - 1)
                def _():
                    self.down(z).wait_recv()

            def load(self, out):
                home = pltpu.make_async_copy(self.part.at[z], out.at[0], slot_sems.at[4])
                home.start()

                @pl.when(z > 0)
                def _():
                    run([pltpu.make_async_copy(self.below.at[z], out.at[1], slot_sems.at[5])])

                @pl.when(z == 0)
                def _():
                    out[1] = jnp.zeros((R, D), bf16)

                @pl.when(z < n_mp - 1)
                def _():
                    run([pltpu.make_async_copy(self.above.at[z], out.at[2], slot_sems.at[6])])

                @pl.when(z == n_mp - 1)
                def _():
                    out[2] = jnp.zeros((R, D), bf16)

                home.wait()

            def finish(self):
                for j in range(n_mp):

                    @pl.when(j > z)
                    def _():
                        self.up(j).wait_send()

                    @pl.when(j < z)
                    def _():
                        self.down(j).wait_send()

        class Ring:
            def __init__(self, slots, first_sem):
                self.slots, self.first_sem, self.base, self.primed = slots, first_sem, 0, 0

            def tile(self, copies, i, slot):
                return [
                    pltpu.make_async_copy(src, dst, slot_sems.at[self.first_sem + self.slots * n + slot])
                    for n, (src, dst) in enumerate(copies(i, slot))
                ]

            def start(self, copies, i, slot):
                for c in self.tile(copies, i, slot):
                    c.start()

            def fill(self, copies):
                for d in range(self.slots - 1):
                    self.start(copies, d, (self.base + d) % self.slots)

            def prime(self, copies):
                if not self.primed:
                    self.fill(copies)
                self.primed = self.slots - 1

            def step(self, count, copies, then, i):
                slot = lax.rem(self.base + i, self.slots)
                ahead = i + self.slots - 1

                def next_tile(slot):
                    maybe_static(ahead < count, lambda: self.start(copies, ahead, slot))
                    if then is not None:
                        for d in range(self.slots - 1):
                            maybe_static(ahead == count + d, lambda: self.start(then, d, slot))

                next_tile(lax.rem(self.base + ahead, self.slots))
                for c in self.tile(copies, i, slot):
                    c.wait()
                return slot

            def turned(self, count, then):
                self.base = (self.base + count) % self.slots
                self.primed = 0 if then is None else self.slots - 1

            def run(self, count, copies, work, then=None):
                self.prime(copies)

                @pl.loop(0, count)
                def _(i):
                    work(i, self.step(count, copies, then, i))

                self.turned(count, then)

        tall_ring, wide_ring = Ring(3, 18), Ring(2, 22)

        normed, pulled = ref.full_normed, ref.full_pulled
        pulled_log, normed_log = {}, {}
        Nv, Gv, Av, Hv = ref.Nv, ref.Gv, ref.Av, ref.Hv
        own_rows = ds(z, R)
        vec_a, vec_b, vrow = ref.vec_a_all, ref.vec_b_all, ref.vrow
        vec_sent = []
        for m in range(1, n_dp):
            k = flip(me, m)
            vec_sent.append(wire.send(ref.vec_a, vec_a.at[me], vec_a.at[k], (k, z)))
        own_vec = [wire.local(ref.vec_a, vec_a.at[me]), wire.local(ref.vec_b, vec_b.at[me])]
        tok_copy = wire.local(ref.tokens, ref.tok)
        line_step(ref.cotangent, pulled, 1, 0, pulled_log)
        gather_step("up", 0)
        vec_b_sent = []
        for m in range(1, n_dp):
            k = flip(me, m)
            vec_b_sent.append(wire.send(ref.vec_b, vec_b.at[me], vec_b.at[k], (k, z)))
        gather_step("qkv", 0)
        own_loads = [
            c for n, w in enumerate(order) for c in moves(w, weights[w][0], weights[w][3], 3 * n, False)
        ]
        for c in own_loads:
            c.start()
        cot_copy = wire.local(ref.cotangent, Gv.at[own_rows, :])
        tables = [
            wire.local(a, b)
            for a, b in ((ref.rope_c, ref.tc), (ref.rope_s, ref.ts))
        ]

        for one in vec_sent:
            one.arrive()
        for c in own_vec:
            c.wait()
        for k in range(n_dp):
            for n in range(CD // 128):
                lanes = pl.ds(k * CD + n * 128, 128)
                for row in range(2):
                    at = row * (CD // 128) + n
                    vrow[row : row + 1, lanes] = vec_a[k, at : at + 1, :]
                one, two = 2 * (CD // 128) + n, 3 * (CD // 128) + n
                vrow[2:3, lanes] = vec_a[k, one : one + 1, :] + vec_a[k, two : two + 1, :]
        tok_copy.wait()
        tok = ref.tok

        def stats(rows):
            x = tok[rows, :].astype(f32)
            centre = jnp.mean(x, -1, keepdims=True)
            offset = x - centre
            spread = jnp.mean(offset * offset, -1, keepdims=True)
            scale = lax.rsqrt(spread + EPS)
            return x, offset * scale, scale


        @pl.loop(0, R // LB)
        def _(i):
            _, xhat, _ = stats(ds(i, LB))
            v = (xhat * vrow[0:1, :] + vrow[1:2, :]).astype(bf16)
            Nv[pl.ds(pl.multiple_of(z * R + i * LB, LB), LB), :] = v

        own_normed = Nv.at[own_rows, :]
        for hh in range(2):
            line_step(own_normed, normed, 1, hh, normed_log)

        for c in own_loads:
            c.wait()
        own_stores = [
            c
            for n, w in enumerate(order)
            for c in moves(w, weights[w][1](me, None), weights[w][3], 3 * n, True)
        ]
        for c in own_stores:
            c.start()
        for j in range(1, len(bits)):
            gather_step("up", j)
        gather_step("down", 0)
        for j in range(1, len(bits)):
            gather_step("qkv", j)
        gather_step("out", 0)
        for c in own_stores:
            c.wait()
        for c in tables:
            c.wait()
        for one in vec_b_sent:
            one.arrive()
        total = vec_b[0]
        for k in range(1, n_dp):
            total = total + vec_b[k]
        nq, nu = -(-3 * L // VB), F // VB
        for n in range(nq):
            vrow[3:4, n * VB : (n + 1) * VB] = total[n : n + 1, :]
        for n in range(nu):
            vrow[4:5, n * VB : (n + 1) * VB] = total[nq + n : nq + n + 1, :]

        loads = Loads()
        line_step(own_normed, normed, 2, 0, normed_log)
        line_step(own_normed, normed, 2, 1, normed_log)
        gather_mate("up")
        loads.rows(normed, Nv, 1)
        for s in range(2, NH):
            for hh in range(2):
                line_step(own_normed, normed, s + 1, hh, normed_log)
            loads.rows(normed, Nv, s)
        gathered("up")
        loads.wait()

        wa, wb = ref.wa, ref.wb
        WT = min(1024, F)
        C0, C1 = 0.7978845608028654, 0.044715

        def sequence_half(other, quarter=None):
            which = 1 - mine_half if other else mine_half
            if quarter is None:
                return ds(which, HS)
            return pl.ds(pl.multiple_of(which * HS + quarter * (HS // 2), HS // 2), HS // 2)

        own_quarters = [sequence_half(False, q) for q in range(2)]
        near_quarter = [ds(1 + lax.rem(1 + mine_half, 2), HS // 2)]
        far_quarter = [ds(3 - 3 * mine_half, HS // 2)]

        def tall(full, rows, i, slot, width):
            return [(full.at[:, ds(i, width)], wa.at[slot, pl.ds(0, rows), pl.ds(0, width)])]

        def tall_value(slot, rows, width):
            return wa[slot, 0:rows, 0:width]

        def wide_slot(slot):
            return pl.ds(pl.multiple_of(slot * T, T), T)

        def up_copies(i, slot):
            return tall(ref.full_up, D, i, slot, T)

        def hidden(parts, then=None):
            def work(i, slot):
                cols = ds(i, T)
                w = tall_value(slot, D, T)
                for rows in parts:
                    v = mm(Nv[rows, :], w, NN) + vrow[4:5, cols]
                    v2 = v * v
                    a = 0.5 * jnp.tanh(v * ((C0 * C1) * v2 + C0)) + 0.5
                    act = v * a
                    Av[rows, cols] = act.astype(bf16)
                    Hv[rows, cols] = (a + act * (1.0 - a) * ((6 * C0 * C1) * v2 + 2 * C0)).astype(bf16)

            tall_ring.run(F // T, up_copies, work, then)

        QKV, ATv, LSE = ref.QKV, ref.ATv, ref.LSE
        tc, ts = ref.tc, ref.ts
        first_turn = lax.rem(lax.broadcasted_iota(jnp.int32, (1, 128), 1), HD) < ROT // 2

        def turn(u, rows, sign):
            left = pltpu.roll(u, 128 - ROT // 2, 1)
            right = pltpu.roll(u, ROT // 2, 1)
            return u * tc[rows, :] + sign * (jnp.where(first_turn, left, right) * ts[rows, :])

        def qkv_copies(j, slot):
            return [(ref.full_qkv.at[j], wa.at[slot, :, pl.ds(0, L)])]

        def mix(parts):
            tall_ring.prime(qkv_copies)
            for j in range(3):
                slot = tall_ring.step(3, qkv_copies, None, j)
                w = tall_value(slot, D, L)
                for rows in parts:
                    v = mm(Nv[rows, :], w, NN) + vrow[3:4, j * L : (j + 1) * L]
                    for c in range(L // 128):
                        u = v[:, c * 128 : (c + 1) * 128]
                        if j < 2:
                            u = turn(u, rows, 1.0)
                        u = u.astype(bf16)
                        if j == 0:
                            u = u * bf16(HD**-0.5)
                        QKV[j, rows, pl.ds(c * 128, 128)] = u
            tall_ring.turned(3, None)

        if NH < n_mp - 1:
            line_step(own_normed, normed, NH + 1, 0, normed_log)
        hidden(own_quarters)
        tall_ring.prime(up_copies)
        for j in range(1, len(bits)):
            gather_step("down", j)
        for s in range(NH, n_mp - 1):
            for hh in range(2):
                if (s + 1, hh) not in normed_log:
                    line_step(own_normed, normed, s + 1, hh, normed_log)
            loads.rows(normed, Nv, s)
        line_step(ref.cotangent, pulled, 1, 1, pulled_log)
        loads.wait()
        hidden(near_quarter)
        gather_mate("qkv")
        for j in range(1, len(bits)):
            gather_step("out", j)
        gathered("qkv")
        mix(own_quarters + near_quarter)
        tall_ring.prime(up_copies)
        line_arrive(normed_log, n_mp - 1)
        loads.rows(normed, Nv, n_mp - 1)
        loads.wait()
        line_step(ref.cotangent, pulled, 2, 0, pulled_log)
        normed_mate = wire.send(Nv, ref.mate_normed, ref.mate_normed, mate)
        hidden(far_quarter, qkv_copies)
        line_step(ref.cotangent, pulled, 2, 1, pulled_log)
        for s in range(3, n_mp - 1):
            for hh in range(2):
                line_step(ref.cotangent, pulled, s, hh, pulled_log)
        mix(far_quarter)
        act_mate = wire.send(Av, ref.mate_act, ref.mate_act, mate)

        corner = lax.broadcasted_iota(jnp.int32, (RB, RB), 0) <= lax.broadcasted_iota(
            jnp.int32, (RB, RB), 1
        )
        lane = lax.broadcasted_iota(jnp.int32, (1, 128), 1)
        pair_masks = [lane < HD, lane >= HD]

        def only(values, mask):
            return jnp.where(mask, values, jnp.zeros_like(values))

        wo = ref.wo
        wo_load = pltpu.make_async_copy(ref.full_out, wo, wire.sem())

        def out_copies(i, slot):
            return tall(ref.full_down, F, i, slot, TD)

        def down_copies(i, slot):
            return [(ref.full_down.at[ds(i, T), :], wb.at[wide_slot(slot), :])]


        flat = ref.flat
        units = [(i, e) for i in range(S // RB) for e in range(2)]

        def places(i):
            return pl.ds(i * RB, RB), pl.ds(0, i * RB)

        def staggered(*phases):
            for t in range(len(units) + len(phases) - 1):
                for lag, phase in enumerate(phases):
                    if 0 <= t - lag < len(units):
                        phase(*units[t - lag])

        def attend_pair(hp):
            lanes = ds(hp, 128)

            flat[...] = QKV[2, :, lanes].T
            scores, weighted, done = {}, {}, {}

            def score(i, e):
                rows, past = places(i)
                q = only(QKV[0, rows, lanes], pair_masks[e])
                own = mm(QKV[1, rows, lanes], q, NT)
                scores[i, e] = own, mm(QKV[1, past, lanes], q, NT) if i else None

            def soften(i, e):
                own, earlier = scores.pop((i, e))
                own = jnp.where(corner, own, -1e30)
                top = jnp.max(own, 0, keepdims=True)
                if i:
                    top = jnp.maximum(top, jnp.max(earlier, 0, keepdims=True))
                    earlier = jnp.exp(earlier - top)
                own = jnp.exp(own - top)
                mass = jnp.sum(own, 0, keepdims=True)
                if i:
                    mass = mass + jnp.sum(earlier, 0, keepdims=True)
                inverse = 1.0 / mass
                LSE[hp * 2 + e, :, places(i)[0]] = top + jnp.log(mass)
                own = (own * inverse).astype(bf16)
                weighted[i, e] = own, (earlier * inverse).astype(bf16) if i else None

            def attend(i, e):
                rows, past = places(i)
                own, earlier = weighted.pop((i, e))
                values = flat.at[pl.ds(e * HD, HD), :]
                total = mm(values[:, rows], own, NN)
                if i:
                    total = total + mm(values[:, past], earlier, NN)
                done[e] = total
                if e == 1:
                    ATv[rows, lanes] = jnp.concatenate([done[0], done[1]], 0).T.astype(bf16)

            staggered(score, soften, attend)

        pairs = L // 128
        pl.loop(0, pairs // 2)(attend_pair)
        gather_mate("down")
        gather_mate("out")

        @pl.loop(pairs // 2, pairs)
        def _(hp):
            @pl.when(hp == pairs - 1)
            def _():
                for one in mates["out"] + mates["down"]:
                    one.into.wait_recv()
                wo_load.start()
                tall_ring.fill(out_copies)
                wide_ring.fill(down_copies)

            attend_pair(hp)

        for one in mates["out"] + mates["down"]:
            one.came = True
        tall_ring.primed, wide_ring.primed = 2, 1

        att_mate = wire.send(ATv, ref.mate_att, ref.mate_att, mate)
        line_step(ref.cotangent, pulled, n_mp - 1, 0, pulled_log)
        wo_load.wait()

        ob = ref.ob
        out_sems = ref.out_sems

        def put(part, half, i, slot):
            return [
                pltpu.make_async_copy(
                    ob.at[slot, pl.ds(j * R, R), :],
                    part.at[half * NH + j, :, ds(i, TD)],
                    out_sems.at[slot, j],
                )
                for j in range(NH)
            ]

        def product_half(part, other, ring, copies, value, then):
            half = 1 - mine_half if other else mine_half

            def work(i, slot):
                place_out = lax.rem(i, 2)

                @pl.when(i >= 2)
                def _():
                    for c in put(part, half, i - 2, place_out):
                        c.wait()

                for quarter in range(2):
                    v = value(sequence_half(other, quarter), slot, i)
                    ob[place_out, pl.ds(quarter * (HS // 2), HS // 2), :] = v.astype(bf16)
                for c in put(part, half, i, place_out):
                    c.start()

            ring.run(D // TD, copies, work, then)
            for i in range(D // TD - 2, D // TD):
                for c in put(part, half, i, i % 2):
                    c.wait()

        def out_value(rows, slot, i):
            v = mm(Av[rows, :], tall_value(slot, F, TD), NN)
            return v + mm(ATv[rows, :], wo[:, ds(i, TD)], NN)

        sum1 = LineSum(ref.part1, ref.below1, ref.above1)
        product_half(ref.part1, True, tall_ring, out_copies, out_value, out_copies)
        sum1.begin(False)
        line_step(ref.cotangent, pulled, n_mp - 1, 1, pulled_log)
        product_half(ref.part1, False, tall_ring, out_copies, out_value, None)
        sum1.begin(True)

        pulled_loads = Loads()
        last = n_mp - n_mp // 4
        for s in range(1, last):
            line_arrive(pulled_log, s)
            pulled_loads.rows(pulled, Gv, s)
        YP = ref.YP
        small = ref.small
        small[...] = jnp.zeros_like(small)
        act_mate.arrive()
        cot_copy.wait()
        pulled_loads.wait()
        half_a = sequence_half(False)
        half_b = sequence_half(True)

        def mate_half(half):
            return wire.send(
                Gv.at[half, :], ref.mate_pulled.at[half, :], ref.mate_pulled.at[half, :], mate
            )

        def load_mate_columns(source, rows):
            return [
                wire.local(source.at[rows, ds(flip(me, m), CD)], YP.at[n, rows, :])
                for n, m in enumerate(masks)
            ]

        pulled_a = mate_half(half_a)

        def push_hidden(parts, then):
            def work(i, slot):
                cols = ds(i, T)
                total = small[4:5, cols]
                for rows in parts:
                    d = mm(Gv[rows, :], wb[wide_slot(slot), :], NT) * Hv[rows, cols].astype(f32)
                    d = d.astype(bf16)
                    Hv[rows, cols] = d
                    total = total + jnp.sum(d.astype(f32), 0, keepdims=True)
                small[4:5, cols] = total

            wide_ring.run(F // T, down_copies, work, then)

        push_hidden(own_quarters + near_quarter, down_copies)
        pulled_a.arrive()
        mate_columns = load_mate_columns(ref.mate_pulled, half_a)
        for s in range(last, n_mp):
            line_arrive(pulled_log, s)
            pulled_loads.rows(pulled, Gv, s)
        pulled_loads.wait()
        pulled_b = mate_half(half_b)
        push_hidden(far_quarter, None)
        hid_mate = wire.send(Hv, ref.mate_hid, ref.mate_hid, mate)
        mate_tiles = [wire.local(ref.mate_act, wb.at[:, pl.ds(0, F)])]
        att_mate.arrive()
        mate_load = wire.local(ref.mate_att, wa.at[0, pl.ds(0, S), pl.ds(0, L)])
        pulled_b.arrive()
        mate_columns = mate_columns + load_mate_columns(ref.mate_pulled, half_b)
        DMv = ref.DMv
        for half in range(2):
            rows = pl.ds(half * HS, HS)
            ob[half, :, 0:L] = mm(Gv[rows, :], wo[...], NT).astype(bf16)
        for c in mate_tiles + mate_columns:
            c.wait()

        grad_info = {
            "down": (ref.gw_down, ref.rb_down, ref.st_down, ref.ta_down, F // 2, 128),
            "out": (ref.gw_out, ref.rb_out, ref.st_down.at[:, pl.ds(0, L)], ref.ta_down.at[:, :, pl.ds(0, L // 2)], L // 2, 128),
            "up": (ref.gw_up, ref.rb_up, ref.st_up, ref.ta_up, CD // 2, 16),
            "qkv": (ref.gw_qkv, ref.rb_qkv, ref.st_up, ref.ta_up, CD // 2, 16),
        }
        offset, position = 0, []
        for i in range(len(bits)):
            position.append(offset)
            offset += 2 ** (len(bits) - 1 - i)

        def half_of(w, chunk, h):
            return half_rows_of(chunk, grad_info[w][4], h, w == "qkv")

        came = {}

        def scatter_send(w, h, i, m):
            gw, rb = grad_info[w][:2]
            rest = span(orders[h][i + 1 :])
            keep = m - orders[h][i]
            got = half_of(w, rb.at[position[i] + rest.index(keep)], h)
            came[(w, h, i, keep)] = wire.send(
                half_of(w, gw.at[place[m]], h), got, got, (flip(me, orders[h][i]), z)
            )

        def scatter_first(w, m):
            for h in range(2):
                if m & orders[h][0]:
                    scatter_send(w, h, 0, m)

        def scatter_step(w, i):
            gw, rb, _, ta, n, block = grad_info[w]
            wide = 3 * L if w == "qkv" else ta.shape[-1]
            for k in range(2 ** (len(bits) - 1 - i)):
                work = []
                for h in range(2):
                    way = orders[h]
                    m = way[i] + span(way[i + 1 :])[k]
                    terms = []
                    for e in range(i):
                        came[(w, h, e, m)].arrive()
                        rest = span(way[e + 1 :])
                        terms.append(half_of(w, rb.at[position[e] + rest.index(m)], h))
                    home = half_of(w, gw.at[place[m]], h)
                    first = moves(w, home, ta.at[h, 0], 9 * h, False)
                    first = first + moves(w, terms[0], ta.at[h, 1], 9 * h + 3, False)
                    for c in first:
                        c.start()
                    work.append((h, m, home, terms, first))
                for h, m, home, terms, first in work:
                    for c in first:
                        c.wait()
                    add_rows(ta.at[h, 0], [ta.at[h, 0], ta.at[h, 1]], n, block, wide)
                    for term in terms[1:]:
                        run(moves(w, term, ta.at[h, 1], 9 * h + 3, False))
                        add_rows(ta.at[h, 0], [ta.at[h, 0], ta.at[h, 1]], n, block, wide)
                    for c in moves(w, home, ta.at[h, 0], 9 * h + 6, True):
                        c.start()
                for h, m, home, terms, first in work:
                    for c in moves(w, home, ta.at[h, 0], 9 * h + 6, True):
                        c.wait()
                    scatter_send(w, h, i, m)

        def scatter_done(w):
            for h in range(2):
                for i in range(len(bits)):
                    came[(w, h, i, 0)].arrive()

        finals = {
            "down": (ref.grad_down, ref.gs),
            "out": (ref.grad_out, ref.gs),
            "up": (ref.grad_up, ref.gt),
            "qkv": ([ref.grad_q, ref.grad_k, ref.grad_v], ref.gt),
        }

        def weight_sum(w):
            gw, rb, st, ta, n, _ = grad_info[w]
            out, staged = finals[w]
            scatter_done(w)
            near = [st.at[0], st.at[1]]
            far = [gw.at[place[0]]] + [rb.at[position[i]] for i in range(len(bits))]
            first = moves(w, far[0], near[0], 0, False) + moves(w, far[1], near[1], 3, False)
            for c in first:
                c.start()
            rest = []
            for q, source in enumerate(far[2:]):
                for h in range(2):
                    rest += moves(w, half_of(w, source, h), ta.at[h, q], 6 + 6 * q + 3 * h, False)
            for c in rest:
                c.start()
            for c in first + rest:
                c.wait()
            block = min(n, staged.shape[1])
            wide = 3 * L if w == "qkv" else gw.shape[-1]

            def out_of(h, i, slot):
                rows = pl.ds(pl.multiple_of(h * n + i * block, block), block)
                if w == "qkv":
                    return [
                        pltpu.make_async_copy(
                            staged.at[slot, pl.ds(0, block), pl.ds(j * L, L)],
                            out[j].at[rows, :],
                            slot_sems.at[18 + 3 * slot + j],
                        )
                        for j in range(3)
                    ]
                return [
                    pltpu.make_async_copy(
                        staged.at[slot, pl.ds(0, block), pl.ds(0, wide)],
                        out.at[rows, :],
                        slot_sems.at[18 + 3 * slot],
                    )
                ]

            count = n // block
            for h in range(2):

                @pl.loop(0, count)
                def _(i):
                    slot = lax.rem(h * count + i, 2)
                    rows = pl.ds(pl.multiple_of(h * n + i * block, block), block)
                    inner = pl.ds(pl.multiple_of(i * block, block), block)

                    def again():
                        for c in out_of(h, i, slot):
                            c.wait()

                    maybe_static(h * count + i >= 2, again)
                    total = st[0, rows, 0:wide].astype(f32) + st[1, rows, 0:wide].astype(f32)
                    for q in range(len(far) - 2):
                        total = total + ta[h, q, inner, 0:wide].astype(f32)
                    staged[slot, 0:block, 0:wide] = total
                    for c in out_of(h, i, slot):
                        c.start()

            for slot in range(min(2, 2 * count)):
                for c in out_of(0, 0, slot):
                    c.wait()

        def grad_chunks(*jobs, chosen=masks):
            pending = []

            def settle():
                for w, m, copies in pending:
                    for c in copies:
                        c.wait()
                    scatter_first(w, m)
                pending.clear()

            for n, m in enumerate(chosen):
                slot = n % 2
                fresh = []
                for number, (w, work, st) in enumerate(jobs):
                    gw = grad_info[w][0]
                    work(m, flip(me, m), st.at[slot])
                    copies = moves(w, gw.at[place[m]], st.at[slot], 6 * number + 3 * slot, True)
                    for c in copies:
                        c.start()
                    if number == 0:
                        settle()
                    fresh.append((w, m, copies))
                pending.extend(fresh)
            settle()

        def grad_down(m, k, st):
            @pl.loop(0, F // T)
            def _(i):
                v = mm(Av[:, ds(i, T)], Gv[:, ds(k, CD)], TN)
                v = v + mm(wb[:, ds(i, T)], YP[place[m]], TN)
                st[ds(i, T), :] = v.astype(bf16)


        def grad_out(m, k, st):
            v = mm(ATv[...], Gv[:, ds(k, CD)], TN)
            v = v + mm(wa[0, 0:S, 0:L], YP[place[m]], TN)
            st[...] = v.astype(bf16)

        mate_load.wait()
        out_place = ref.ta_down.at[:, 1, pl.ds(0, L)]
        branch_jobs = ("down", grad_down, ref.st_down), ("out", grad_out, out_place)
        grad_chunks(*branch_jobs, chosen=masks[:-1])
        sum1.step(1)
        def back_copies(i, slot):
            rows = ds(i, TD)
            return [(ref.full_up.at[rows, :], wb.at[wide_slot(slot), pl.ds(0, F)])] + [
                (ref.full_qkv.at[j, rows, :], wa.at[slot, pl.ds(j * TD, TD), pl.ds(0, L)])
                for j in range(3)
            ]

        def back_value(rows, slot, i):
            v = mm(Hv[rows, :], wb[wide_slot(slot), 0:F], NT)
            for j in range(3):
                w = wa[slot, j * TD : (j + 1) * TD, 0:L]
                v = v + mm(DMv[rows, j * L : (j + 1) * L], w, NT)
            return v

        back_ring = Ring(2, 24)
        back_ring.prime(back_copies)
        dk, dv = ref.dk, ref.dv

        @pl.loop(0, L // 128)
        def _(hp):
            lanes = ds(hp, 128)
            flat[...] = QKV[1, :, lanes].T
            dk[...] = jnp.zeros_like(dk)
            dv[...] = jnp.zeros_like(dv)
            scores, slopes, done = {}, {}, {}

            def score(i, e):
                rows, past = places(i)
                q = only(QKV[0, rows, lanes], pair_masks[e])
                do = ob[i * RB // HS, i * RB % HS : i * RB % HS + RB, lanes]
                do = only(do, pair_masks[e])
                found = [q, do]
                for where in [rows, past][: 1 + (i > 0)]:
                    found += [mm(QKV[1, where, lanes], q, NT), mm(QKV[2, where, lanes], do, NT)]
                scores[i, e] = found

            def slope(i, e):
                q, do, s, dp, *earlier = scores.pop((i, e))
                log_mass = LSE[hp * 2 + e, :, places(i)[0]]
                p = jnp.where(corner, jnp.exp(s - log_mass), 0.0)
                delta = jnp.sum(p * dp, 0, keepdims=True)
                if i:
                    s2, dp2 = earlier
                    p2 = jnp.exp(s2 - log_mass)
                    delta = delta + jnp.sum(p2 * dp2, 0, keepdims=True)
                found = [q, do, (p * (dp - delta)).astype(bf16), p.astype(bf16)]
                if i:
                    found += [(p2 * (dp2 - delta)).astype(bf16), p2.astype(bf16)]
                slopes[i, e] = found

            def push(i, e):
                rows, past = places(i)
                q, do, s, p, *earlier = slopes.pop((i, e))
                keys = flat.at[pl.ds(e * HD, HD), :]
                dk[rows, :] += mm(s, q, NN)
                dv[rows, :] += mm(p, do, NN)
                dq = mm(keys[:, rows], s, NN)
                if i:
                    s2, p2 = earlier
                    dk[past, :] += mm(s2, q, NN)
                    dv[past, :] += mm(p2, do, NN)
                    dq = dq + mm(keys[:, past], s2, NN)
                done[e] = dq
                if e == 1:
                    dq = jnp.concatenate([done[0], done[1]], 0).T * HD**-0.5
                    DMv[rows, lanes] = turn(dq, rows, -1.0).astype(bf16)

            staggered(score, slope, push)
            DMv[:, ds(hp + L // 128, 128)] = turn(dk[...], pl.ds(0, S), -1.0).astype(bf16)
            DMv[:, ds(hp + 2 * (L // 128), 128)] = dv[...].astype(bf16)

        mix_mate = wire.send(DMv, ref.mate_mix, ref.mate_mix, mate)
        sum2 = LineSum(ref.part2, ref.below2, ref.above2)
        product_half(ref.part2, True, back_ring, back_copies, back_value, None)
        sum2.begin(False)
        hid_mate.arrive()
        mate_tiles = [wire.local(ref.mate_hid, wb.at[:, pl.ds(0, F)])]

        normed_mate.arrive()
        mate_columns = load_mate_columns(ref.mate_normed, pl.ds(0, S))
        small[3:4, pl.ds(0, 3 * L)] = sum_rows_of(DMv, S)
        for i in range(1, len(bits)):
            scatter_step("down", i)

        for tau in range(2, n_mp - 1):
            sum1.step(tau)
        for c in mate_tiles + mate_columns:
            c.wait()

        def grad_up(m, k, st):
            @pl.loop(0, F // WT)
            def _(i):
                v = mm(Nv[:, ds(k, CD)], Hv[:, ds(i, WT)], TN)
                v = v + mm(YP[place[m]], wb[:, ds(i, WT)], TN)
                st[:, ds(i, WT)] = v.astype(bf16)

        grad_chunks(("up", grad_up, ref.st_up))
        back_ring.prime(back_copies)
        sum2.step(1)

        small_b, small_b_all = ref.small_b, ref.small_b_all
        for n in range(nq):
            small_b[n : n + 1, :] = small[3:4, n * VB : (n + 1) * VB]
        for n in range(nu):
            small_b[nq + n : nq + n + 1, :] = small[4:5, n * VB : (n + 1) * VB]
        for n in range(nq + nu, 8):
            small_b[n : n + 1, :] = jnp.zeros((1, VB), f32)
        biases = []
        for m in range(1, n_dp):
            k = flip(me, m)
            biases.append(wire.send(small_b, small_b_all.at[me], small_b_all.at[k], (k, z)))
        product_half(ref.part2, False, back_ring, back_copies, back_value, None)
        sum2.begin(True)

        mix_mate.arrive()
        loads_mix = [wire.local(ref.mate_mix, wb.at[:, pl.ds(0, 3 * L)])]
        for i in range(1, len(bits)):
            scatter_step("up", i)
        for i in range(1, len(bits)):
            scatter_step("out", i)
        for c in loads_mix:
            c.wait()

        def grad_qkv(m, k, st):
            v = mm(Nv[:, ds(k, CD)], DMv[...], TN)
            v = v + mm(YP[place[m]], wb[:, 0 : 3 * L], TN)
            st[:, 0 : 3 * L] = v.astype(bf16)

        grad_chunks(("qkv", grad_qkv, ref.st_up))

        for tau in range(2, n_mp - 1):
            sum2.step(tau)
        zs = ref.zs
        sum1.arrive()
        sum1.load(zs)
        @pl.loop(0, R // LB)
        def _(i):
            rows = ds(i, LB)
            v = tok[rows, :].astype(f32) + vrow[2:3, :]
            v = v + zs[0, rows, :].astype(f32)
            v = v + zs[1, rows, :].astype(f32) + zs[2, rows, :].astype(f32)
            zs[0, rows, :] = v.astype(bf16)

        lo_copy = wire.local(zs.at[0], ref.layer_out)
        small[2:3, :] = sum_rows_of(Gv, S)
        lo_copy.wait()


        own_loads = [
            wire.local(ref.mate_act, wb.at[:, pl.ds(0, F)]),
            wire.local(ref.mate_att, wa.at[0, pl.ds(0, S), pl.ds(0, L)]),
            wire.local(ref.mate_pulled.at[:, ds(me, CD)], YP.at[NC - 1]),
        ]
        for c in own_loads:
            c.wait()
        grad_chunks(*branch_jobs, chosen=masks[-1:])
        for i in range(1, len(bits)):
            scatter_step("qkv", i)
        for w in ("down", "out"):
            weight_sum(w)
        for one in biases:
            one.arrive()
        total = small_b[...]
        for m in range(1, n_dp):
            total = total + small_b_all[flip(me, m)]
        ref.bias_sums[...] = total

        sum2.arrive()
        sum2.load(zs)
        gt = ref.gt

        def gt_copy(i, slot):
            return pltpu.make_async_copy(
                gt.at[slot], ref.grad_tokens.at[ds(i, LB), :], slot_sems.at[slot]
            )

        @pl.loop(0, R // LB)
        def _(i):
            slot = lax.rem(i, 2)
            rows = ds(i, LB)
            _, xhat, scale = stats(rows)
            d = zs[0, rows, :].astype(f32) + zs[1, rows, :].astype(f32)
            d = d + zs[2, rows, :].astype(f32)
            small[0:1, :] += jnp.sum(d * xhat, 0, keepdims=True)
            small[1:2, :] += jnp.sum(d, 0, keepdims=True)
            e = d * vrow[0:1, :]
            centre = jnp.mean(e, -1, keepdims=True)
            along = jnp.mean(e * xhat, -1, keepdims=True)

            @pl.when(i >= 2)
            def _():
                gt_copy(i - 2, slot).wait()

            own = Gv[pl.ds(pl.multiple_of(z * R + i * LB, LB), LB), :].astype(f32)
            gt[slot] = own + scale * (e - centre - xhat * along)
            gt_copy(i, slot).start()

        for i in range(max(0, R // LB - 2), R // LB):
            gt_copy(i, i % 2).wait()
        small_k, small_all = ref.small_k, ref.small_all
        for k in range(n_dp):
            small_k[k] = small[:, k * CD : (k + 1) * CD]
        across = []
        for m in range(1, n_dp):
            k = flip(me, m)
            across.append(wire.send(small_k.at[k], small_all.at[me], small_all.at[k], (k, z)))
        weight_sum("up")
        for one in across:
            one.arrive()
        total = small_k[me]
        for m in range(1, n_dp):
            total = total + small_all[flip(me, m)]
        small_own, small_mp = ref.small_own, ref.small_mp
        small_own[...] = total
        across = []
        for k in range(1, n_mp):
            to = lax.rem(z + k, n_mp)
            across.append(wire.send(small_own, small_mp.at[k], small_mp.at[k], (me, to)))
        weight_sum("qkv")
        for one in across:
            one.arrive()
        others = small_mp[1]
        for k in range(2, n_mp):
            others = others + small_mp[k]
        first_two = lax.broadcasted_iota(jnp.int32, (8, 1), 0) < 2
        ref.row_sums[...] = total + jnp.where(first_two, others, 0.0)
        sum1.finish()
        sum2.finish()
        wire.finish()

    return kernel


def sum_rows_of(array, rows):
    total = None
    for i in range(rows // 128):
        part = jnp.sum(array[pl.ds(i * 128, 128), :].astype(f32), 0, keepdims=True)
        total = part if total is None else total + part
    return total


def rope_tables(length):
    places = np.arange(length, dtype=np.float64)
    inverse = 10000.0 ** (-np.arange(0, ROT, 2, dtype=np.float64) / ROT)
    angles = places[:, None] * inverse[None, :]
    cosine, sine = np.cos(angles), np.sin(angles)
    rest = np.zeros((length, HD - ROT))
    c = np.concatenate([cosine, cosine, rest + 1.0], -1)
    s = np.concatenate([-sine, sine, rest], -1)
    return [np.concatenate([t, t], -1).astype(np.float32) for t in (c, s)]


def make_body(n_dp, n_mp):
    def body(
        tokens, ln_gain, ln_bias, w_qkv, b_qkv, w_out, b_out, w_up, b_up, w_down, b_down, cotangent
    ):
        me = lax.axis_index("dp")
        R = tokens.shape[0]
        S = R * n_mp
        CD = D // n_dp
        NC = n_dp // 2
        F = w_up.shape[1]
        L = w_qkv.shape[2]
        heads = b_qkv.shape[1]
        share = HD // n_dp
        T = min(512, F)
        TD = 512
        nq, nu = -(-3 * L // VB), F // VB

        def spread(shape, own, axis, rows):
            whole = lax.dynamic_update_slice_in_dim(
                jnp.zeros(shape, f32), own.astype(f32), me * share, axis
            ).reshape(-1)
            return jnp.pad(whole, (0, rows * VB - whole.shape[0])).reshape(rows, VB)

        vec_a = jnp.concatenate([ln_gain, ln_bias, b_out, b_down]).astype(f32)
        vec_a = jnp.pad(vec_a, (0, 1024 - 4 * CD)).reshape(8, 128)
        vec_b = jnp.concatenate(
            [
                spread((3, heads, HD), b_qkv, 2, nq),
                spread((F // HD, HD), b_up, 1, nu),
                jnp.zeros((8 - nq - nu, VB), f32),
            ],
            0,
        )
        rope_c, rope_s = rope_tables(S)
        ins = dict(
            tokens=tokens,
            cotangent=cotangent,
            vec_a=vec_a,
            vec_b=vec_b,
            w_up=w_up,
            w_qkv=w_qkv.transpose(1, 0, 2),
            w_down=w_down,
            w_out=w_out,
            rope_c=jnp.asarray(rope_c),
            rope_s=jnp.asarray(rope_s),
        )
        any_spec = pl.BlockSpec(memory_space=pl.ANY)
        vmem_spec = pl.BlockSpec(memory_space=pltpu.VMEM)
        outs = dict(
            layer_out=((R, D), bf16),
            grad_tokens=((R, D), f32),
            row_sums=((8, CD), f32),
            bias_sums=((8, VB), f32),
            grad_up=((CD, F), f32),
            grad_q=((CD, L), f32),
            grad_k=((CD, L), f32),
            grad_v=((CD, L), f32),
            grad_down=((F, CD), f32),
            grad_out=((L, CD), f32),
            gw_up=((NC, CD, F), bf16),
            gw_qkv=((NC, 3, CD, L), bf16),
            gw_down=((NC, F, CD), bf16),
            gw_out=((NC, L, CD), bf16),
            rb_up=((NC - 1, CD, F), bf16),
            rb_qkv=((NC - 1, 3, CD, L), bf16),
            rb_down=((NC - 1, F, CD), bf16),
            rb_out=((NC - 1, L, CD), bf16),
            full_up=((D, F), bf16),
            full_qkv=((3, D, L), bf16),
            full_down=((F, D), bf16),
            full_out=((L, D), bf16),
            full_normed=((n_mp, R, D), bf16),
            full_pulled=((n_mp, R, D), bf16),
            mate_normed=((S, D), bf16),
            mate_pulled=((S, D), bf16),
            mate_act=((S, F), bf16),
            mate_hid=((S, F), bf16),
            mate_att=((S, L), bf16),
            mate_mix=((S, 3 * L), bf16),
            part1=((n_mp, R, D), bf16),
            below1=((n_mp, R, D), bf16),
            above1=((n_mp, R, D), bf16),
            part2=((n_mp, R, D), bf16),
            below2=((n_mp, R, D), bf16),
            above2=((n_mp, R, D), bf16),
        )
        n_sems = 33 * (n_dp + n_mp)
        scratch = dict(
            vec_a_all=pltpu.VMEM((n_dp, 8, 128), f32),
            vec_b_all=pltpu.VMEM((n_dp, 8, VB), f32),
            vrow=pltpu.VMEM((8, D), f32),
            small=pltpu.VMEM((8, D), f32),
            small_k=pltpu.VMEM((n_dp, 8, CD), f32),
            small_all=pltpu.VMEM((n_dp, 8, CD), f32),
            small_own=pltpu.VMEM((8, CD), f32),
            small_mp=pltpu.VMEM((n_mp, 8, CD), f32),
            small_b=pltpu.VMEM((8, VB), f32),
            small_b_all=pltpu.VMEM((n_dp, 8, VB), f32),
            tok=pltpu.VMEM((R, D), bf16),
            gt=pltpu.VMEM((2, LB, D), f32),
            gs=pltpu.VMEM((2, min(256, L // 2), CD), f32),
            tc=pltpu.VMEM((S, 128), f32),
            ts=pltpu.VMEM((S, 128), f32),
            Nv=pltpu.VMEM((S, D), bf16),
            Gv=pltpu.VMEM((S, D), bf16),
            Av=pltpu.VMEM((S, F), bf16),
            Hv=pltpu.VMEM((S, F), bf16),
            QKV=pltpu.VMEM((3, S, L), bf16),
            ATv=pltpu.VMEM((S, L), bf16),
            flat=pltpu.VMEM((128, S), bf16),
            DMv=pltpu.VMEM((S, 3 * L), bf16),
            LSE=pltpu.VMEM((heads, 1, S), f32),
            dk=pltpu.VMEM((S, 128), f32),
            dv=pltpu.VMEM((S, 128), f32),
            wa=pltpu.VMEM((3, D, T), bf16),
            wb=pltpu.VMEM((2 * T, D), bf16),
            wo=pltpu.VMEM((L, D), bf16),
            ob=pltpu.VMEM((2, S // 2, TD), bf16),
            YP=pltpu.VMEM((NC, S, CD), bf16),
            zs=pltpu.VMEM((3, R, D), bf16),
            st_up=pltpu.VMEM((2, CD, F), bf16),
            st_down=pltpu.VMEM((2, F, CD), bf16),
            ta_up=pltpu.VMEM((2, 2, CD // 2, F), bf16),
            ta_down=pltpu.VMEM((2, 2, F // 2, CD), bf16),
            sems=pltpu.SemaphoreType.DMA((n_sems,)),
            slot_sems=pltpu.SemaphoreType.DMA((32,)),
            out_sems=pltpu.SemaphoreType.DMA((2, n_mp)),
        )
        names = list(ins) + list(outs) + list(scratch)
        got = pl.pallas_call(
            make_kernel(n_dp, n_mp, R, F, L, names, n_sems),
            out_shape=[jax.ShapeDtypeStruct(s, t) for s, t in outs.values()],
            in_specs=[any_spec] * len(ins),
            out_specs=[vmem_spec if n.endswith("_sums") else any_spec for n in outs],
            scratch_shapes=list(scratch.values()),
            name="layer",
            cost_estimate=pl.CostEstimate(
                flops=6 * S * D * (4 * L + 2 * F), bytes_accessed=150 << 20, transcendentals=0
            ),
            compiler_params=pltpu.CompilerParams(
                collective_id=0, has_side_effects=True, vmem_limit_bytes=62 << 20
            ),
        )(*ins.values())
        got = types.SimpleNamespace(**dict(zip(outs, got)))

        def mine(values, axis):
            return lax.dynamic_slice_in_dim(values, me * share, share, axis)

        sums = got.bias_sums.reshape(-1)
        bias = got.row_sums[2]
        return (
            got.layer_out,
            got.grad_tokens,
            got.row_sums[0],
            got.row_sums[1],
            jnp.stack([got.grad_q, got.grad_k, got.grad_v], 1),
            mine(sums[: 3 * L].reshape(3, heads, HD), 2),
            got.grad_out,
            bias,
            got.grad_up,
            mine(sums[nq * VB : nq * VB + F].reshape(F // HD, HD), 1),
            got.grad_down,
            bias,
        )

    return body


def solution(mesh):
    n_dp, n_mp = mesh.shape["dp"], mesh.shape["mp"]
    weights_in = (
        P("dp"),
        P("dp"),
        P("dp", None, "mp"),
        P(None, "mp", "dp"),
        P("mp", "dp"),
        P("dp"),
        P("dp", "mp"),
        P("mp", "dp"),
        P("mp", "dp"),
        P("dp"),
    )
    rows = P(("dp", "mp"), None)
    return jax.shard_map(
        make_body(n_dp, n_mp),
        mesh=mesh,
        in_specs=(rows,) + weights_in + (rows,),
        out_specs=(rows, rows) + weights_in,
        check_vma=False,
    )
```

```python
import types

import jax
import jax.numpy as jnp
import numpy as np
from jax import lax
from jax.experimental import pallas as pl
from jax.experimental.pallas import tpu as pltpu
from jax.sharding import PartitionSpec as P

D = 2048
HD = 64
ROT = 32
EPS = 1e-05
BQ = 256
LB = 32
VB = 512
MESH = pl.DeviceIdType.MESH
NN = (((1,), (0,)), ((), ()))
NT = (((1,), (1,)), ((), ()))
TN = (((0,), (0,)), ((), ()))
bf16 = jnp.bfloat16
f32 = jnp.float32


def mm(left, right, dims):
    return lax.dot_general(left, right, dims, preferred_element_type=f32)


def flip(index, mask):
    bit = 1
    while bit <= mask:
        if mask & bit:
            index = index + bit * (1 - 2 * lax.rem(lax.div(index, bit), 2))
        bit *= 2
    return index


def span(bits):
    found = [0]
    for bit in bits:
        found = found + [m + bit for m in found]
    return found


def maybe_static(pred, act):
    if isinstance(pred, bool):
        if pred:
            act()
    else:
        pl.when(pred)(act)


def maybe(pred, act):
    if pred is None:
        act()
    else:
        pl.when(pred)(act)


class Sent:
    def __init__(self, out, into, pred_out, pred_into):
        self.out, self.into, self.pred_out, self.pred_into = out, into, pred_out, pred_into
        self.came, self.left = False, False

    def start(self):
        maybe(self.pred_out, self.out.start)

    def arrive(self):
        if not self.came:
            self.came = True
            maybe(self.pred_into, self.into.wait_recv)

    def finish(self):
        if not self.left:
            self.left = True
            maybe(self.pred_out, self.out.wait_send)


class Wire:
    def __init__(self, sems, count):
        self.sems, self.count, self.used, self.open = sems, count, 0, []

    def sem(self):
        assert self.used < self.count
        self.used += 1
        return self.sems.at[self.used - 1]

    def sems_of(self, n):
        assert self.used + n <= self.count
        self.used += n
        base = self.used - n
        return lambda j: self.sems.at[base + j]

    def send(self, src, dst, got, dev, pred_out=None, pred_into=None):
        s, r = self.sem(), self.sem()
        out = pltpu.make_async_remote_copy(src, dst, s, r, dev, MESH)
        into = pltpu.make_async_remote_copy(got, got, s, r, dev, MESH)
        one = Sent(out, into, pred_out, pred_into)
        one.start()
        self.open.append(one)
        return one

    def local(self, src, dst):
        copy = pltpu.make_async_copy(src, dst, self.sem())
        copy.start()
        return copy

    def finish(self):
        for one in self.open:
            one.finish()


def make_kernel(n_dp, n_mp, R, F, L, names, n_sems):
    S = R * n_mp
    CD = D // n_dp
    NC = n_dp // 2
    T = min(512, F)
    TD = 512
    HS = S // 2
    NH = n_mp // 2
    bits = [b for b in (2, 4, 8, 16, 32) if b < n_dp]
    orders = [bits, bits[1:] + bits[:1]]
    masks = sorted(span(bits), key=lambda m: -bin(m).count("1"))
    place = {m: n for n, m in enumerate(masks)}
    RB = min(BQ, S)

    def kernel(*refs):
        ref = types.SimpleNamespace(**dict(zip(names, refs)))
        me = lax.axis_index("dp")
        z = lax.axis_index("mp")
        wire = Wire(ref.sems, n_sems)
        slot_sems = ref.slot_sems
        mate = (flip(me, 1), z)
        up_dev = (me, jnp.minimum(z + 1, n_mp - 1))
        down_dev = (me, jnp.maximum(z - 1, 0))
        mine_half = lax.div(z, NH)
        barrier = pltpu.get_barrier_semaphore()
        for m in range(1, n_dp):
            pl.semaphore_signal(barrier, inc=1, device_id=(flip(me, m), z), device_id_type=MESH)
        for k in range(1, n_mp):
            pl.semaphore_signal(
                barrier, inc=1, device_id=(me, lax.rem(z + k, n_mp)), device_id_type=MESH
            )
        pl.semaphore_wait(barrier, n_dp - 1 + n_mp - 1)

        def ds(k, size):
            return pl.ds(pl.multiple_of(k * size, size), size)

        def run(copies):
            for c in copies:
                c.start()
            for c in copies:
                c.wait()

        def pieces_of(full, rows, kind):
            half = rows // 2

            def piece(k, h):
                if kind == "rows":
                    if h is None:
                        return full.at[ds(k, rows), :]
                    return full.at[pl.ds(pl.multiple_of(k * rows + h * half, half), half), :]
                if kind == "cube":
                    if h is None:
                        return full.at[:, ds(k, rows), :]
                    return full.at[:, pl.ds(pl.multiple_of(k * rows + h * half, half), half), :]
                if h is None:
                    return full.at[:, ds(k, CD)]
                return full.at[pl.ds(h * half, half), ds(k, CD)]

            return piece

        def half_rows_of(array, n, h, cube):
            if cube:
                return array.at[:, pl.ds(h * n, n), :]
            return array.at[pl.ds(h * n, n), :]

        weights = {
            "up": (ref.w_up, pieces_of(ref.full_up, CD, "rows"), CD // 2, ref.st_up.at[0]),
            "qkv": (ref.w_qkv, pieces_of(ref.full_qkv, CD, "cube"), CD // 2, ref.st_up.at[1]),
            "down": (ref.w_down, pieces_of(ref.full_down, F, "cols"), F // 2, ref.st_down.at[0]),
            "out": (ref.w_out, pieces_of(ref.full_out, L, "cols"), L // 2, ref.st_down.at[1, pl.ds(0, L)]),
        }
        order = ["up", "qkv", "down", "out"]
        arrivals = {w: [[] for _ in bits] for w in order}

        mates = {w: [] for w in order}

        def to_mate(w, j):
            piece = weights[w][1]
            for h in range(2):
                way = orders[h]
                for sub in span(way[:j]):
                    k = flip(flip(me, sub), way[j])
                    got = piece(flip(k, 1), h)
                    mates[w].append(wire.send(piece(k, h), piece(k, h), got, mate))

        def gather_step(w, j):
            own, piece, n, _ = weights[w]
            if j > 0:
                for one in arrivals[w][j - 1]:
                    one.arrive()
            for h in range(2):
                way = orders[h]
                for sub in span(way[:j]):
                    k = flip(me, sub)
                    src = half_rows_of(own, n, h, w == "qkv") if sub == 0 else piece(k, h)
                    got = piece(flip(k, way[j]), h)
                    arrivals[w][j].append(wire.send(src, piece(k, h), got, (flip(me, way[j]), z)))
            if j > 0:
                to_mate(w, j - 1)
            else:
                got = piece(flip(me, 1), None)
                mates[w].append(wire.send(own, piece(me, None), got, mate))

        def gather_mate(w):
            for one in arrivals[w][-1]:
                one.arrive()
            to_mate(w, len(bits) - 1)

        def gathered(w):
            for one in mates[w]:
                one.arrive()

        def moves(w, far, near, base, out):
            pairs = [(far, near)]
            if w == "qkv":
                pairs = [(far.at[j], near.at[:, pl.ds(j * L, L)]) for j in range(3)]
            return [
                pltpu.make_async_copy(*(p[::-1] if out else p), slot_sems.at[base + n])
                for n, p in enumerate(pairs)
            ]

        hr = R // 2

        def line_step(own, full, s, hh, log):
            rows = pl.ds(hh * hr, hr)
            if s > 1:
                for one in log[(s - 1, hh)]:
                    one.arrive()
            up, down = z - (s - 1), z + (s - 1)
            first = own.at[rows, :] if s == 1 else None
            one = wire.send(
                first if s == 1 else full.at[jnp.maximum(up, 0), rows, :],
                full.at[jnp.maximum(up, 0), rows, :],
                full.at[jnp.maximum(z - s, 0), rows, :],
                up_dev,
                jnp.logical_and(z + 1 < n_mp, up >= 0),
                z - s >= 0,
            )
            two = wire.send(
                first if s == 1 else full.at[jnp.minimum(down, n_mp - 1), rows, :],
                full.at[jnp.minimum(down, n_mp - 1), rows, :],
                full.at[jnp.minimum(z + s, n_mp - 1), rows, :],
                down_dev,
                jnp.logical_and(z >= 1, down < n_mp),
                z + s < n_mp,
            )
            log[(s, hh)] = [one, two]

        def line_arrive(log, s):
            for hh in range(2):
                for one in log[(s, hh)]:
                    one.arrive()

        class Loads:
            def __init__(self):
                self.open = []

            def rows(self, full, near, s):
                for c, pred in ((z - s, z - s >= 0), (z + s, z + s < n_mp)):
                    safe = jnp.clip(c, 0, n_mp - 1)
                    copy = pltpu.make_async_copy(full.at[safe], near.at[ds(safe, R), :], wire.sem())
                    maybe(pred, copy.start)
                    self.open.append((copy, pred))

            def wait(self):
                for copy, pred in self.open:
                    maybe(pred, copy.wait)
                self.open = []

        def add_rows(out, terms, count, block, wide):
            @pl.loop(0, count // block)
            def _(i):
                rows = pl.ds(pl.multiple_of(i * block, block), block)
                total = terms[0][rows, 0:wide].astype(f32)
                for term in terms[1:]:
                    total = total + term[rows, 0:wide].astype(f32)
                out[rows, 0:wide] = total.astype(out.dtype)

        class LineSum:
            def __init__(self, part, from_below, from_above):
                self.part, self.below, self.above = part, from_below, from_above
                self.us, self.ur = wire.sems_of(n_mp), wire.sems_of(n_mp)
                self.ds, self.dr = wire.sems_of(n_mp), wire.sems_of(n_mp)

            def up(self, j):
                return pltpu.make_async_remote_copy(
                    self.part.at[j], self.below.at[j], self.us(j), self.ur(j), up_dev, MESH
                )

            def down(self, j):
                return pltpu.make_async_remote_copy(
                    self.part.at[j], self.above.at[j], self.ds(j), self.dr(j), down_dev, MESH
                )

            def begin(self, near):
                @pl.when(z == 0)
                def _():
                    for j in range(n_mp - 1, 0, -1):
                        if (j < NH) == near:
                            self.up(j).start()

                @pl.when(z == n_mp - 1)
                def _():
                    for j in range(n_mp - 1):
                        if (j >= NH) == near:
                            self.down(j).start()

            def merge(self, j, got):
                a, b = ref.zs.at[0], ref.zs.at[1]
                one = pltpu.make_async_copy(self.part.at[j], a, slot_sems.at[4])
                two = pltpu.make_async_copy(got.at[j], b, slot_sems.at[5])
                run([one, two])
                add_rows(a, [a, b], R, LB, D)
                run([pltpu.make_async_copy(a, self.part.at[j], slot_sems.at[4])])

            def step(self, tau):
                j = n_mp - 1 - tau + z

                @pl.when(jnp.logical_and(z > 0, jnp.logical_and(j < n_mp, tau >= z)))
                def _():
                    self.up(j).wait_recv()
                    self.merge(j, self.below)
                    self.up(j).start()

                i = tau - (n_mp - 1 - z)

                @pl.when(jnp.logical_and(z < n_mp - 1, i >= 0))
                def _():
                    self.down(i).wait_recv()
                    self.merge(i, self.above)
                    self.down(i).start()

            def arrive(self):
                @pl.when(z > 0)
                def _():
                    self.up(z).wait_recv()

                @pl.when(z < n_mp - 1)
                def _():
                    self.down(z).wait_recv()

            def load(self, out):
                home = pltpu.make_async_copy(self.part.at[z], out.at[0], slot_sems.at[4])
                home.start()

                @pl.when(z > 0)
                def _():
                    run([pltpu.make_async_copy(self.below.at[z], out.at[1], slot_sems.at[5])])

                @pl.when(z == 0)
                def _():
                    out[1] = jnp.zeros((R, D), bf16)

                @pl.when(z < n_mp - 1)
                def _():
                    run([pltpu.make_async_copy(self.above.at[z], out.at[2], slot_sems.at[6])])

                @pl.when(z == n_mp - 1)
                def _():
                    out[2] = jnp.zeros((R, D), bf16)

                home.wait()

            def finish(self):
                for j in range(n_mp):

                    @pl.when(j > z)
                    def _():
                        self.up(j).wait_send()

                    @pl.when(j < z)
                    def _():
                        self.down(j).wait_send()

        class Ring:
            def __init__(self, slots, first_sem):
                self.slots, self.first_sem, self.base, self.primed = slots, first_sem, 0, 0

            def tile(self, copies, i, slot):
                return [
                    pltpu.make_async_copy(src, dst, slot_sems.at[self.first_sem + self.slots * n + slot])
                    for n, (src, dst) in enumerate(copies(i, slot))
                ]

            def start(self, copies, i, slot):
                for c in self.tile(copies, i, slot):
                    c.start()

            def fill(self, copies):
                for d in range(self.slots - 1):
                    self.start(copies, d, (self.base + d) % self.slots)

            def prime(self, copies):
                if not self.primed:
                    self.fill(copies)
                self.primed = self.slots - 1

            def step(self, count, copies, then, i):
                slot = lax.rem(self.base + i, self.slots)
                ahead = i + self.slots - 1

                def next_tile(slot):
                    maybe_static(ahead < count, lambda: self.start(copies, ahead, slot))
                    if then is not None:
                        for d in range(self.slots - 1):
                            maybe_static(ahead == count + d, lambda: self.start(then, d, slot))

                next_tile(lax.rem(self.base + ahead, self.slots))
                for c in self.tile(copies, i, slot):
                    c.wait()
                return slot

            def turned(self, count, then):
                self.base = (self.base + count) % self.slots
                self.primed = 0 if then is None else self.slots - 1

            def run(self, count, copies, work, then=None):
                self.prime(copies)

                @pl.loop(0, count)
                def _(i):
                    work(i, self.step(count, copies, then, i))

                self.turned(count, then)

        tall_ring, wide_ring = Ring(3, 18), Ring(2, 22)

        normed, pulled = ref.full_normed, ref.full_pulled
        pulled_log, normed_log = {}, {}
        Nv, Gv, Av, Hv = ref.Nv, ref.Gv, ref.Av, ref.Hv
        own_rows = ds(z, R)
        vec_a, vec_b, vrow = ref.vec_a_all, ref.vec_b_all, ref.vrow
        vec_sent = []
        for m in range(1, n_dp):
            k = flip(me, m)
            vec_sent.append(wire.send(ref.vec_a, vec_a.at[me], vec_a.at[k], (k, z)))
        own_vec = [wire.local(ref.vec_a, vec_a.at[me]), wire.local(ref.vec_b, vec_b.at[me])]
        tok_copy = wire.local(ref.tokens, ref.tok)
        line_step(ref.cotangent, pulled, 1, 0, pulled_log)
        gather_step("up", 0)
        vec_b_sent = []
        for m in range(1, n_dp):
            k = flip(me, m)
            vec_b_sent.append(wire.send(ref.vec_b, vec_b.at[me], vec_b.at[k], (k, z)))
        gather_step("qkv", 0)
        own_loads = [
            c for n, w in enumerate(order) for c in moves(w, weights[w][0], weights[w][3], 3 * n, False)
        ]
        for c in own_loads:
            c.start()
        cot_copy = wire.local(ref.cotangent, Gv.at[own_rows, :])
        tables = [
            wire.local(a, b)
            for a, b in ((ref.rope_c, ref.tc), (ref.rope_s, ref.ts))
        ]

        for one in vec_sent:
            one.arrive()
        for c in own_vec:
            c.wait()
        for k in range(n_dp):
            for n in range(CD // 128):
                lanes = pl.ds(k * CD + n * 128, 128)
                for row in range(2):
                    at = row * (CD // 128) + n
                    vrow[row : row + 1, lanes] = vec_a[k, at : at + 1, :]
                one, two = 2 * (CD // 128) + n, 3 * (CD // 128) + n
                vrow[2:3, lanes] = vec_a[k, one : one + 1, :] + vec_a[k, two : two + 1, :]
        tok_copy.wait()
        tok = ref.tok

        def stats(rows):
            x = tok[rows, :].astype(f32)
            centre = jnp.mean(x, -1, keepdims=True)
            offset = x - centre
            spread = jnp.mean(offset * offset, -1, keepdims=True)
            scale = lax.rsqrt(spread + EPS)
            return x, offset * scale, scale


        @pl.loop(0, R // LB)
        def _(i):
            _, xhat, _ = stats(ds(i, LB))
            v = (xhat * vrow[0:1, :] + vrow[1:2, :]).astype(bf16)
            Nv[pl.ds(pl.multiple_of(z * R + i * LB, LB), LB), :] = v

        own_normed = Nv.at[own_rows, :]
        for hh in range(2):
            line_step(own_normed, normed, 1, hh, normed_log)

        for c in own_loads:
            c.wait()
        own_stores = [
            c
            for n, w in enumerate(order)
            for c in moves(w, weights[w][1](me, None), weights[w][3], 3 * n, True)
        ]
        for c in own_stores:
            c.start()
        for j in range(1, len(bits)):
            gather_step("up", j)
        gather_step("down", 0)
        for j in range(1, len(bits)):
            gather_step("qkv", j)
        gather_step("out", 0)
        for c in own_stores:
            c.wait()
        for c in tables:
            c.wait()
        for one in vec_b_sent:
            one.arrive()
        total = vec_b[0]
        for k in range(1, n_dp):
            total = total + vec_b[k]
        nq, nu = -(-3 * L // VB), F // VB
        for n in range(nq):
            vrow[3:4, n * VB : (n + 1) * VB] = total[n : n + 1, :]
        for n in range(nu):
            vrow[4:5, n * VB : (n + 1) * VB] = total[nq + n : nq + n + 1, :]

        loads = Loads()
        line_step(own_normed, normed, 2, 0, normed_log)
        line_step(own_normed, normed, 2, 1, normed_log)
        gather_mate("up")
        loads.rows(normed, Nv, 1)
        for s in range(2, NH):
            for hh in range(2):
                line_step(own_normed, normed, s + 1, hh, normed_log)
            loads.rows(normed, Nv, s)
        gathered("up")
        loads.wait()

        wa, wb = ref.wa, ref.wb
        WT = min(1024, F)
        C0, C1 = 0.7978845608028654, 0.044715

        def sequence_half(other, quarter=None):
            which = 1 - mine_half if other else mine_half
            if quarter is None:
                return ds(which, HS)
            return pl.ds(pl.multiple_of(which * HS + quarter * (HS // 2), HS // 2), HS // 2)

        own_quarters = [sequence_half(False, q) for q in range(2)]
        near_quarter = [ds(1 + lax.rem(1 + mine_half, 2), HS // 2)]
        far_quarter = [ds(3 - 3 * mine_half, HS // 2)]

        def tall(full, rows, i, slot, width):
            return [(full.at[:, ds(i, width)], wa.at[slot, pl.ds(0, rows), pl.ds(0, width)])]

        def tall_value(slot, rows, width):
            return wa[slot, 0:rows, 0:width]

        def wide_slot(slot):
            return pl.ds(pl.multiple_of(slot * T, T), T)

        def up_copies(i, slot):
            return tall(ref.full_up, D, i, slot, T)

        def hidden(parts, then=None):
            def work(i, slot):
                cols = ds(i, T)
                w = tall_value(slot, D, T)
                for rows in parts:
                    v = mm(Nv[rows, :], w, NN) + vrow[4:5, cols]
                    v2 = v * v
                    a = 0.5 * jnp.tanh(v * ((C0 * C1) * v2 + C0)) + 0.5
                    act = v * a
                    Av[rows, cols] = act.astype(bf16)
                    Hv[rows, cols] = (a + act * (1.0 - a) * ((6 * C0 * C1) * v2 + 2 * C0)).astype(bf16)

            tall_ring.run(F // T, up_copies, work, then)

        QKV, ATv, LSE = ref.QKV, ref.ATv, ref.LSE
        tc, ts = ref.tc, ref.ts
        first_turn = lax.rem(lax.broadcasted_iota(jnp.int32, (1, 128), 1), HD) < ROT // 2

        def turn(u, rows, sign):
            left = pltpu.roll(u, 128 - ROT // 2, 1)
            right = pltpu.roll(u, ROT // 2, 1)
            return u * tc[rows, :] + sign * (jnp.where(first_turn, left, right) * ts[rows, :])

        def qkv_copies(j, slot):
            return [(ref.full_qkv.at[j], wa.at[slot, :, pl.ds(0, L)])]

        def mix(parts):
            tall_ring.prime(qkv_copies)
            for j in range(3):
                slot = tall_ring.step(3, qkv_copies, None, j)
                w = tall_value(slot, D, L)
                for rows in parts:
                    v = mm(Nv[rows, :], w, NN) + vrow[3:4, j * L : (j + 1) * L]
                    for c in range(L // 128):
                        u = v[:, c * 128 : (c + 1) * 128]
                        if j < 2:
                            u = turn(u, rows, 1.0)
                        u = u.astype(bf16)
                        if j == 0:
                            u = u * bf16(HD**-0.5)
                        QKV[j, rows, pl.ds(c * 128, 128)] = u
            tall_ring.turned(3, None)

        if NH < n_mp - 1:
            line_step(own_normed, normed, NH + 1, 0, normed_log)
        hidden(own_quarters)
        tall_ring.prime(up_copies)
        for j in range(1, len(bits)):
            gather_step("down", j)
        for s in range(NH, n_mp - 1):
            for hh in range(2):
                if (s + 1, hh) not in normed_log:
                    line_step(own_normed, normed, s + 1, hh, normed_log)
            loads.rows(normed, Nv, s)
        line_step(ref.cotangent, pulled, 1, 1, pulled_log)
        loads.wait()
        hidden(near_quarter)
        gather_mate("qkv")
        for j in range(1, len(bits)):
            gather_step("out", j)
        gathered("qkv")
        mix(own_quarters + near_quarter)
        tall_ring.prime(up_copies)
        line_arrive(normed_log, n_mp - 1)
        loads.rows(normed, Nv, n_mp - 1)
        loads.wait()
        line_step(ref.cotangent, pulled, 2, 0, pulled_log)
        normed_mate = wire.send(Nv, ref.mate_normed, ref.mate_normed, mate)
        hidden(far_quarter, qkv_copies)
        line_step(ref.cotangent, pulled, 2, 1, pulled_log)
        for s in range(3, n_mp - 1):
            for hh in range(2):
                line_step(ref.cotangent, pulled, s, hh, pulled_log)
        mix(far_quarter)
        act_mate = wire.send(Av, ref.mate_act, ref.mate_act, mate)

        corner = lax.broadcasted_iota(jnp.int32, (RB, RB), 0) <= lax.broadcasted_iota(
            jnp.int32, (RB, RB), 1
        )
        lane = lax.broadcasted_iota(jnp.int32, (1, 128), 1)
        pair_masks = [lane < HD, lane >= HD]

        def only(values, mask):
            return jnp.where(mask, values, jnp.zeros_like(values))

        wo = ref.wo
        wo_load = pltpu.make_async_copy(ref.full_out, wo, wire.sem())

        def out_copies(i, slot):
            return tall(ref.full_down, F, i, slot, TD)

        def down_copies(i, slot):
            return [(ref.full_down.at[ds(i, T), :], wb.at[wide_slot(slot), :])]


        flat = ref.flat
        units = [(i, e) for i in range(S // RB) for e in range(2)]

        def places(i):
            return pl.ds(i * RB, RB), pl.ds(0, i * RB)

        def staggered(*phases):
            for t in range(len(units) + len(phases) - 1):
                for lag, phase in enumerate(phases):
                    if 0 <= t - lag < len(units):
                        phase(*units[t - lag])

        def attend_pair(hp):
            lanes = ds(hp, 128)

            flat[...] = QKV[2, :, lanes].T
            scores, weighted, done = {}, {}, {}

            def score(i, e):
                rows, past = places(i)
                q = only(QKV[0, rows, lanes], pair_masks[e])
                own = mm(QKV[1, rows, lanes], q, NT)
                scores[i, e] = own, mm(QKV[1, past, lanes], q, NT) if i else None

            def soften(i, e):
                own, earlier = scores.pop((i, e))
                own = jnp.where(corner, own, -1e30)
                top = jnp.max(own, 0, keepdims=True)
                if i:
                    top = jnp.maximum(top, jnp.max(earlier, 0, keepdims=True))
                    earlier = jnp.exp(earlier - top)
                own = jnp.exp(own - top)
                mass = jnp.sum(own, 0, keepdims=True)
                if i:
                    mass = mass + jnp.sum(earlier, 0, keepdims=True)
                inverse = 1.0 / mass
                LSE[hp * 2 + e, :, places(i)[0]] = top + jnp.log(mass)
                own = (own * inverse).astype(bf16)
                weighted[i, e] = own, (earlier * inverse).astype(bf16) if i else None

            def attend(i, e):
                rows, past = places(i)
                own, earlier = weighted.pop((i, e))
                values = flat.at[pl.ds(e * HD, HD), :]
                total = mm(values[:, rows], own, NN)
                if i:
                    total = total + mm(values[:, past], earlier, NN)
                done[e] = total
                if e == 1:
                    ATv[rows, lanes] = jnp.concatenate([done[0], done[1]], 0).T.astype(bf16)

            staggered(score, soften, attend)

        pairs = L // 128
        pl.loop(0, pairs // 2)(attend_pair)
        gather_mate("down")
        gather_mate("out")

        @pl.loop(pairs // 2, pairs)
        def _(hp):
            @pl.when(hp == pairs - 1)
            def _():
                for one in mates["out"] + mates["down"]:
                    one.into.wait_recv()
                wo_load.start()
                tall_ring.fill(out_copies)
                wide_ring.fill(down_copies)

            attend_pair(hp)

        for one in mates["out"] + mates["down"]:
            one.came = True
        tall_ring.primed, wide_ring.primed = 2, 1

        att_mate = wire.send(ATv, ref.mate_att, ref.mate_att, mate)
        line_step(ref.cotangent, pulled, n_mp - 1, 0, pulled_log)
        wo_load.wait()

        ob = ref.ob
        out_sems = ref.out_sems

        def put(part, half, i, slot):
            return [
                pltpu.make_async_copy(
                    ob.at[slot, pl.ds(j * R, R), :],
                    part.at[half * NH + j, :, ds(i, TD)],
                    out_sems.at[slot, j],
                )
                for j in range(NH)
            ]

        def product_half(part, other, ring, copies, value, then):
            half = 1 - mine_half if other else mine_half

            def work(i, slot):
                place_out = lax.rem(i, 2)

                @pl.when(i >= 2)
                def _():
                    for c in put(part, half, i - 2, place_out):
                        c.wait()

                for quarter in range(2):
                    v = value(sequence_half(other, quarter), slot, i)
                    ob[place_out, pl.ds(quarter * (HS // 2), HS // 2), :] = v.astype(bf16)
                for c in put(part, half, i, place_out):
                    c.start()

            ring.run(D // TD, copies, work, then)
            for i in range(D // TD - 2, D // TD):
                for c in put(part, half, i, i % 2):
                    c.wait()

        def out_value(rows, slot, i):
            v = mm(Av[rows, :], tall_value(slot, F, TD), NN)
            return v + mm(ATv[rows, :], wo[:, ds(i, TD)], NN)

        sum1 = LineSum(ref.part1, ref.below1, ref.above1)
        product_half(ref.part1, True, tall_ring, out_copies, out_value, out_copies)
        sum1.begin(False)
        line_step(ref.cotangent, pulled, n_mp - 1, 1, pulled_log)
        product_half(ref.part1, False, tall_ring, out_copies, out_value, None)
        sum1.begin(True)

        pulled_loads = Loads()
        last = n_mp - n_mp // 4
        for s in range(1, last):
            line_arrive(pulled_log, s)
            pulled_loads.rows(pulled, Gv, s)
        YP = ref.YP
        small = ref.small
        small[...] = jnp.zeros_like(small)
        act_mate.arrive()
        cot_copy.wait()
        pulled_loads.wait()
        half_a = sequence_half(False)
        half_b = sequence_half(True)

        def mate_half(half):
            return wire.send(
                Gv.at[half, :], ref.mate_pulled.at[half, :], ref.mate_pulled.at[half, :], mate
            )

        def load_mate_columns(source, rows):
            return [
                wire.local(source.at[rows, ds(flip(me, m), CD)], YP.at[n, rows, :])
                for n, m in enumerate(masks)
            ]

        pulled_a = mate_half(half_a)

        def push_hidden(parts, then):
            def work(i, slot):
                cols = ds(i, T)
                total = small[4:5, cols]
                for rows in parts:
                    d = mm(Gv[rows, :], wb[wide_slot(slot), :], NT) * Hv[rows, cols].astype(f32)
                    d = d.astype(bf16)
                    Hv[rows, cols] = d
                    total = total + jnp.sum(d.astype(f32), 0, keepdims=True)
                small[4:5, cols] = total

            wide_ring.run(F // T, down_copies, work, then)

        push_hidden(own_quarters + near_quarter, down_copies)
        pulled_a.arrive()
        mate_columns = load_mate_columns(ref.mate_pulled, half_a)
        for s in range(last, n_mp):
            line_arrive(pulled_log, s)
            pulled_loads.rows(pulled, Gv, s)
        pulled_loads.wait()
        pulled_b = mate_half(half_b)
        push_hidden(far_quarter, None)
        hid_mate = wire.send(Hv, ref.mate_hid, ref.mate_hid, mate)
        mate_tiles = [wire.local(ref.mate_act, wb.at[:, pl.ds(0, F)])]
        att_mate.arrive()
        mate_load = wire.local(ref.mate_att, wa.at[0, pl.ds(0, S), pl.ds(0, L)])
        pulled_b.arrive()
        mate_columns = mate_columns + load_mate_columns(ref.mate_pulled, half_b)
        DMv = ref.DMv
        for half in range(2):
            rows = pl.ds(half * HS, HS)
            ob[half, :, 0:L] = mm(Gv[rows, :], wo[...], NT).astype(bf16)
        for c in mate_tiles + mate_columns:
            c.wait()

        grad_info = {
            "down": (ref.gw_down, ref.rb_down, ref.st_down, ref.ta_down, F // 2, 128),
            "out": (ref.gw_out, ref.rb_out, ref.st_down.at[:, pl.ds(0, L)], ref.ta_down.at[:, :, pl.ds(0, L // 2)], L // 2, 128),
            "up": (ref.gw_up, ref.rb_up, ref.st_up, ref.ta_up, CD // 2, 16),
            "qkv": (ref.gw_qkv, ref.rb_qkv, ref.st_up, ref.ta_up, CD // 2, 16),
        }
        offset, position = 0, []
        for i in range(len(bits)):
            position.append(offset)
            offset += 2 ** (len(bits) - 1 - i)

        def half_of(w, chunk, h):
            return half_rows_of(chunk, grad_info[w][4], h, w == "qkv")

        came = {}

        def scatter_send(w, h, i, m):
            gw, rb = grad_info[w][:2]
            rest = span(orders[h][i + 1 :])
            keep = m - orders[h][i]
            got = half_of(w, rb.at[position[i] + rest.index(keep)], h)
            came[(w, h, i, keep)] = wire.send(
                half_of(w, gw.at[place[m]], h), got, got, (flip(me, orders[h][i]), z)
            )

        def scatter_first(w, m):
            for h in range(2):
                if m & orders[h][0]:
                    scatter_send(w, h, 0, m)

        def scatter_step(w, i):
            gw, rb, _, ta, n, block = grad_info[w]
            wide = 3 * L if w == "qkv" else ta.shape[-1]
            for k in range(2 ** (len(bits) - 1 - i)):
                work = []
                for h in range(2):
                    way = orders[h]
                    m = way[i] + span(way[i + 1 :])[k]
                    terms = []
                    for e in range(i):
                        came[(w, h, e, m)].arrive()
                        rest = span(way[e + 1 :])
                        terms.append(half_of(w, rb.at[position[e] + rest.index(m)], h))
                    home = half_of(w, gw.at[place[m]], h)
                    first = moves(w, home, ta.at[h, 0], 9 * h, False)
                    first = first + moves(w, terms[0], ta.at[h, 1], 9 * h + 3, False)
                    for c in first:
                        c.start()
                    work.append((h, m, home, terms, first))
                for h, m, home, terms, first in work:
                    for c in first:
                        c.wait()
                    add_rows(ta.at[h, 0], [ta.at[h, 0], ta.at[h, 1]], n, block, wide)
                    for term in terms[1:]:
                        run(moves(w, term, ta.at[h, 1], 9 * h + 3, False))
                        add_rows(ta.at[h, 0], [ta.at[h, 0], ta.at[h, 1]], n, block, wide)
                    for c in moves(w, home, ta.at[h, 0], 9 * h + 6, True):
                        c.start()
                for h, m, home, terms, first in work:
                    for c in moves(w, home, ta.at[h, 0], 9 * h + 6, True):
                        c.wait()
                    scatter_send(w, h, i, m)

        def scatter_done(w):
            for h in range(2):
                for i in range(len(bits)):
                    came[(w, h, i, 0)].arrive()

        finals = {
            "down": (ref.grad_down, ref.gs),
            "out": (ref.grad_out, ref.gs),
            "up": (ref.grad_up, ref.gt),
            "qkv": ([ref.grad_q, ref.grad_k, ref.grad_v], ref.gt),
        }

        def weight_sum(w):
            gw, rb, st, ta, n, _ = grad_info[w]
            out, staged = finals[w]
            scatter_done(w)
            near = [st.at[0], st.at[1]]
            far = [gw.at[place[0]]] + [rb.at[position[i]] for i in range(len(bits))]
            first = moves(w, far[0], near[0], 0, False) + moves(w, far[1], near[1], 3, False)
            for c in first:
                c.start()
            rest = []
            for q, source in enumerate(far[2:]):
                for h in range(2):
                    rest += moves(w, half_of(w, source, h), ta.at[h, q], 6 + 6 * q + 3 * h, False)
            for c in rest:
                c.start()
            for c in first + rest:
                c.wait()
            block = min(n, staged.shape[1])
            wide = 3 * L if w == "qkv" else gw.shape[-1]

            def out_of(h, i, slot):
                rows = pl.ds(pl.multiple_of(h * n + i * block, block), block)
                if w == "qkv":
                    return [
                        pltpu.make_async_copy(
                            staged.at[slot, pl.ds(0, block), pl.ds(j * L, L)],
                            out[j].at[rows, :],
                            slot_sems.at[18 + 3 * slot + j],
                        )
                        for j in range(3)
                    ]
                return [
                    pltpu.make_async_copy(
                        staged.at[slot, pl.ds(0, block), pl.ds(0, wide)],
                        out.at[rows, :],
                        slot_sems.at[18 + 3 * slot],
                    )
                ]

            count = n // block
            for h in range(2):

                @pl.loop(0, count)
                def _(i):
                    slot = lax.rem(h * count + i, 2)
                    rows = pl.ds(pl.multiple_of(h * n + i * block, block), block)
                    inner = pl.ds(pl.multiple_of(i * block, block), block)

                    def again():
                        for c in out_of(h, i, slot):
                            c.wait()

                    maybe_static(h * count + i >= 2, again)
                    total = st[0, rows, 0:wide].astype(f32) + st[1, rows, 0:wide].astype(f32)
                    for q in range(len(far) - 2):
                        total = total + ta[h, q, inner, 0:wide].astype(f32)
                    staged[slot, 0:block, 0:wide] = total
                    for c in out_of(h, i, slot):
                        c.start()

            for slot in range(min(2, 2 * count)):
                for c in out_of(0, 0, slot):
                    c.wait()

        def grad_chunks(*jobs, chosen=masks):
            pending = []

            def settle():
                for w, m, copies in pending:
                    for c in copies:
                        c.wait()
                    scatter_first(w, m)
                pending.clear()

            for n, m in enumerate(chosen):
                slot = n % 2
                fresh = []
                for number, (w, work, st) in enumerate(jobs):
                    gw = grad_info[w][0]
                    work(m, flip(me, m), st.at[slot])
                    copies = moves(w, gw.at[place[m]], st.at[slot], 6 * number + 3 * slot, True)
                    for c in copies:
                        c.start()
                    if number == 0:
                        settle()
                    fresh.append((w, m, copies))
                pending.extend(fresh)
            settle()

        def grad_down(m, k, st):
            @pl.loop(0, F // WT)
            def _(i):
                v = mm(Av[:, ds(i, WT)], Gv[:, ds(k, CD)], TN)
                v = v + mm(wb[:, ds(i, WT)], YP[place[m]], TN)
                st[ds(i, WT), :] = v.astype(bf16)


        def grad_out(m, k, st):
            v = mm(ATv[...], Gv[:, ds(k, CD)], TN)
            v = v + mm(wa[0, 0:S, 0:L], YP[place[m]], TN)
            st[...] = v.astype(bf16)

        mate_load.wait()
        out_place = ref.ta_down.at[:, 1, pl.ds(0, L)]
        branch_jobs = ("down", grad_down, ref.st_down), ("out", grad_out, out_place)
        grad_chunks(*branch_jobs, chosen=masks[:-1])
        sum1.step(1)
        def back_copies(i, slot):
            rows = ds(i, TD)
            return [(ref.full_up.at[rows, :], wb.at[wide_slot(slot), pl.ds(0, F)])] + [
                (ref.full_qkv.at[j, rows, :], wa.at[slot, pl.ds(j * TD, TD), pl.ds(0, L)])
                for j in range(3)
            ]

        def back_value(rows, slot, i):
            v = mm(Hv[rows, :], wb[wide_slot(slot), 0:F], NT)
            for j in range(3):
                w = wa[slot, j * TD : (j + 1) * TD, 0:L]
                v = v + mm(DMv[rows, j * L : (j + 1) * L], w, NT)
            return v

        back_ring = Ring(2, 24)
        back_ring.prime(back_copies)
        dk, dv = ref.dk, ref.dv

        @pl.loop(0, L // 128)
        def _(hp):
            lanes = ds(hp, 128)
            flat[...] = QKV[1, :, lanes].T
            dk[...] = jnp.zeros_like(dk)
            dv[...] = jnp.zeros_like(dv)
            scores, slopes, done = {}, {}, {}

            def score(i, e):
                rows, past = places(i)
                q = only(QKV[0, rows, lanes], pair_masks[e])
                do = ob[i * RB // HS, i * RB % HS : i * RB % HS + RB, lanes]
                do = only(do, pair_masks[e])
                found = [q, do]
                for where in [rows, past][: 1 + (i > 0)]:
                    found += [mm(QKV[1, where, lanes], q, NT), mm(QKV[2, where, lanes], do, NT)]
                scores[i, e] = found

            def slope(i, e):
                q, do, s, dp, *earlier = scores.pop((i, e))
                log_mass = LSE[hp * 2 + e, :, places(i)[0]]
                p = jnp.where(corner, jnp.exp(s - log_mass), 0.0)
                delta = jnp.sum(p * dp, 0, keepdims=True)
                if i:
                    s2, dp2 = earlier
                    p2 = jnp.exp(s2 - log_mass)
                    delta = delta + jnp.sum(p2 * dp2, 0, keepdims=True)
                found = [q, do, (p * (dp - delta)).astype(bf16), p.astype(bf16)]
                if i:
                    found += [(p2 * (dp2 - delta)).astype(bf16), p2.astype(bf16)]
                slopes[i, e] = found

            def push(i, e):
                rows, past = places(i)
                q, do, s, p, *earlier = slopes.pop((i, e))
                keys = flat.at[pl.ds(e * HD, HD), :]
                dk[rows, :] += mm(s, q, NN)
                dv[rows, :] += mm(p, do, NN)
                dq = mm(keys[:, rows], s, NN)
                if i:
                    s2, p2 = earlier
                    dk[past, :] += mm(s2, q, NN)
                    dv[past, :] += mm(p2, do, NN)
                    dq = dq + mm(keys[:, past], s2, NN)
                done[e] = dq
                if e == 1:
                    dq = jnp.concatenate([done[0], done[1]], 0).T * HD**-0.5
                    DMv[rows, lanes] = turn(dq, rows, -1.0).astype(bf16)

            staggered(score, slope, push)
            DMv[:, ds(hp + L // 128, 128)] = turn(dk[...], pl.ds(0, S), -1.0).astype(bf16)
            DMv[:, ds(hp + 2 * (L // 128), 128)] = dv[...].astype(bf16)

        mix_mate = wire.send(DMv, ref.mate_mix, ref.mate_mix, mate)
        sum2 = LineSum(ref.part2, ref.below2, ref.above2)
        product_half(ref.part2, True, back_ring, back_copies, back_value, None)
        sum2.begin(False)
        hid_mate.arrive()
        mate_tiles = [wire.local(ref.mate_hid, wb.at[:, pl.ds(0, F)])]

        normed_mate.arrive()
        mate_columns = load_mate_columns(ref.mate_normed, pl.ds(0, S))
        small[3:4, pl.ds(0, 3 * L)] = sum_rows_of(DMv, S)
        for i in range(1, len(bits)):
            scatter_step("down", i)

        for tau in range(2, n_mp - 1):
            sum1.step(tau)
        for c in mate_tiles + mate_columns:
            c.wait()

        def grad_up(m, k, st):
            @pl.loop(0, F // WT)
            def _(i):
                v = mm(Nv[:, ds(k, CD)], Hv[:, ds(i, WT)], TN)
                v = v + mm(YP[place[m]], wb[:, ds(i, WT)], TN)
                st[:, ds(i, WT)] = v.astype(bf16)

        grad_chunks(("up", grad_up, ref.st_up))
        back_ring.prime(back_copies)
        sum2.step(1)

        small_b, small_b_all = ref.small_b, ref.small_b_all
        for n in range(nq):
            small_b[n : n + 1, :] = small[3:4, n * VB : (n + 1) * VB]
        for n in range(nu):
            small_b[nq + n : nq + n + 1, :] = small[4:5, n * VB : (n + 1) * VB]
        for n in range(nq + nu, 8):
            small_b[n : n + 1, :] = jnp.zeros((1, VB), f32)
        biases = []
        for m in range(1, n_dp):
            k = flip(me, m)
            biases.append(wire.send(small_b, small_b_all.at[me], small_b_all.at[k], (k, z)))
        product_half(ref.part2, False, back_ring, back_copies, back_value, None)
        sum2.begin(True)

        mix_mate.arrive()
        loads_mix = [wire.local(ref.mate_mix, wb.at[:, pl.ds(0, 3 * L)])]
        for i in range(1, len(bits)):
            scatter_step("up", i)
        for i in range(1, len(bits)):
            scatter_step("out", i)
        for c in loads_mix:
            c.wait()

        def grad_qkv(m, k, st):
            v = mm(Nv[:, ds(k, CD)], DMv[...], TN)
            v = v + mm(YP[place[m]], wb[:, 0 : 3 * L], TN)
            st[:, 0 : 3 * L] = v.astype(bf16)

        grad_chunks(("qkv", grad_qkv, ref.st_up))
        own_loads = [
            wire.local(ref.mate_act, wb.at[:, pl.ds(0, F)]),
            wire.local(ref.mate_att, wa.at[0, pl.ds(0, S), pl.ds(0, L)]),
            wire.local(ref.mate_pulled.at[:, ds(me, CD)], YP.at[NC - 1]),
        ]

        for tau in range(2, n_mp - 1):
            sum2.step(tau)
        zs = ref.zs
        sum1.arrive()
        sum1.load(zs)
        @pl.loop(0, R // LB)
        def _(i):
            rows = ds(i, LB)
            v = tok[rows, :].astype(f32) + vrow[2:3, :]
            v = v + zs[0, rows, :].astype(f32)
            v = v + zs[1, rows, :].astype(f32) + zs[2, rows, :].astype(f32)
            zs[0, rows, :] = v.astype(bf16)

        lo_copy = wire.local(zs.at[0], ref.layer_out)
        small[2:3, :] = sum_rows_of(Gv, S)
        lo_copy.wait()


        for c in own_loads:
            c.wait()
        grad_chunks(*branch_jobs, chosen=masks[-1:])
        for w in ("down", "out"):
            weight_sum(w)
        for i in range(1, len(bits)):
            scatter_step("qkv", i)
        weight_sum("up")
        for one in biases:
            one.arrive()
        total = small_b[...]
        for m in range(1, n_dp):
            total = total + small_b_all[flip(me, m)]
        ref.bias_sums[...] = total

        sum2.arrive()
        sum2.load(zs)
        gt = ref.gt

        def gt_copy(i, slot):
            return pltpu.make_async_copy(
                gt.at[slot], ref.grad_tokens.at[ds(i, LB), :], slot_sems.at[slot]
            )

        @pl.loop(0, R // LB)
        def _(i):
            slot = lax.rem(i, 2)
            rows = ds(i, LB)
            _, xhat, scale = stats(rows)
            d = zs[0, rows, :].astype(f32) + zs[1, rows, :].astype(f32)
            d = d + zs[2, rows, :].astype(f32)
            small[0:1, :] += jnp.sum(d * xhat, 0, keepdims=True)
            small[1:2, :] += jnp.sum(d, 0, keepdims=True)
            e = d * vrow[0:1, :]
            centre = jnp.mean(e, -1, keepdims=True)
            along = jnp.mean(e * xhat, -1, keepdims=True)

            @pl.when(i >= 2)
            def _():
                gt_copy(i - 2, slot).wait()

            own = Gv[pl.ds(pl.multiple_of(z * R + i * LB, LB), LB), :].astype(f32)
            gt[slot] = own + scale * (e - centre - xhat * along)
            gt_copy(i, slot).start()

        for i in range(max(0, R // LB - 2), R // LB):
            gt_copy(i, i % 2).wait()
        small_k, small_all = ref.small_k, ref.small_all
        for k in range(n_dp):
            small_k[k] = small[:, k * CD : (k + 1) * CD]
        across = []
        for m in range(1, n_dp):
            k = flip(me, m)
            across.append(wire.send(small_k.at[k], small_all.at[me], small_all.at[k], (k, z)))
        for one in across:
            one.arrive()
        total = small_k[me]
        for m in range(1, n_dp):
            total = total + small_all[flip(me, m)]
        small_own, small_mp = ref.small_own, ref.small_mp
        small_own[...] = total
        across = []
        for k in range(1, n_mp):
            to = lax.rem(z + k, n_mp)
            across.append(wire.send(small_own, small_mp.at[k], small_mp.at[k], (me, to)))
        weight_sum("qkv")
        for one in across:
            one.arrive()
        others = small_mp[1]
        for k in range(2, n_mp):
            others = others + small_mp[k]
        first_two = lax.broadcasted_iota(jnp.int32, (8, 1), 0) < 2
        ref.row_sums[...] = total + jnp.where(first_two, others, 0.0)
        sum1.finish()
        sum2.finish()
        wire.finish()

    return kernel


def sum_rows_of(array, rows):
    total = None
    for i in range(rows // 128):
        part = jnp.sum(array[pl.ds(i * 128, 128), :].astype(f32), 0, keepdims=True)
        total = part if total is None else total + part
    return total


def rope_tables(length):
    places = np.arange(length, dtype=np.float64)
    inverse = 10000.0 ** (-np.arange(0, ROT, 2, dtype=np.float64) / ROT)
    angles = places[:, None] * inverse[None, :]
    cosine, sine = np.cos(angles), np.sin(angles)
    rest = np.zeros((length, HD - ROT))
    c = np.concatenate([cosine, cosine, rest + 1.0], -1)
    s = np.concatenate([-sine, sine, rest], -1)
    return [np.concatenate([t, t], -1).astype(np.float32) for t in (c, s)]


def make_body(n_dp, n_mp):
    def body(
        tokens, ln_gain, ln_bias, w_qkv, b_qkv, w_out, b_out, w_up, b_up, w_down, b_down, cotangent
    ):
        me = lax.axis_index("dp")
        R = tokens.shape[0]
        S = R * n_mp
        CD = D // n_dp
        NC = n_dp // 2
        F = w_up.shape[1]
        L = w_qkv.shape[2]
        heads = b_qkv.shape[1]
        share = HD // n_dp
        T = min(512, F)
        TD = 512
        nq, nu = -(-3 * L // VB), F // VB

        def spread(shape, own, axis, rows):
            whole = lax.dynamic_update_slice_in_dim(
                jnp.zeros(shape, f32), own.astype(f32), me * share, axis
            ).reshape(-1)
            return jnp.pad(whole, (0, rows * VB - whole.shape[0])).reshape(rows, VB)

        vec_a = jnp.concatenate([ln_gain, ln_bias, b_out, b_down]).astype(f32)
        vec_a = jnp.pad(vec_a, (0, 1024 - 4 * CD)).reshape(8, 128)
        vec_b = jnp.concatenate(
            [
                spread((3, heads, HD), b_qkv, 2, nq),
                spread((F // HD, HD), b_up, 1, nu),
                jnp.zeros((8 - nq - nu, VB), f32),
            ],
            0,
        )
        rope_c, rope_s = rope_tables(S)
        ins = dict(
            tokens=tokens,
            cotangent=cotangent,
            vec_a=vec_a,
            vec_b=vec_b,
            w_up=w_up,
            w_qkv=w_qkv.transpose(1, 0, 2),
            w_down=w_down,
            w_out=w_out,
            rope_c=jnp.asarray(rope_c),
            rope_s=jnp.asarray(rope_s),
        )
        any_spec = pl.BlockSpec(memory_space=pl.ANY)
        vmem_spec = pl.BlockSpec(memory_space=pltpu.VMEM)
        outs = dict(
            layer_out=((R, D), bf16),
            grad_tokens=((R, D), f32),
            row_sums=((8, CD), f32),
            bias_sums=((8, VB), f32),
            grad_up=((CD, F), f32),
            grad_q=((CD, L), f32),
            grad_k=((CD, L), f32),
            grad_v=((CD, L), f32),
            grad_down=((F, CD), f32),
            grad_out=((L, CD), f32),
            gw_up=((NC, CD, F), bf16),
            gw_qkv=((NC, 3, CD, L), bf16),
            gw_down=((NC, F, CD), bf16),
            gw_out=((NC, L, CD), bf16),
            rb_up=((NC - 1, CD, F), bf16),
            rb_qkv=((NC - 1, 3, CD, L), bf16),
            rb_down=((NC - 1, F, CD), bf16),
            rb_out=((NC - 1, L, CD), bf16),
            full_up=((D, F), bf16),
            full_qkv=((3, D, L), bf16),
            full_down=((F, D), bf16),
            full_out=((L, D), bf16),
            full_normed=((n_mp, R, D), bf16),
            full_pulled=((n_mp, R, D), bf16),
            mate_normed=((S, D), bf16),
            mate_pulled=((S, D), bf16),
            mate_act=((S, F), bf16),
            mate_hid=((S, F), bf16),
            mate_att=((S, L), bf16),
            mate_mix=((S, 3 * L), bf16),
            part1=((n_mp, R, D), bf16),
            below1=((n_mp, R, D), bf16),
            above1=((n_mp, R, D), bf16),
            part2=((n_mp, R, D), bf16),
            below2=((n_mp, R, D), bf16),
            above2=((n_mp, R, D), bf16),
        )
        n_sems = 33 * (n_dp + n_mp)
        scratch = dict(
            vec_a_all=pltpu.VMEM((n_dp, 8, 128), f32),
            vec_b_all=pltpu.VMEM((n_dp, 8, VB), f32),
            vrow=pltpu.VMEM((8, D), f32),
            small=pltpu.VMEM((8, D), f32),
            small_k=pltpu.VMEM((n_dp, 8, CD), f32),
            small_all=pltpu.VMEM((n_dp, 8, CD), f32),
            small_own=pltpu.VMEM((8, CD), f32),
            small_mp=pltpu.VMEM((n_mp, 8, CD), f32),
            small_b=pltpu.VMEM((8, VB), f32),
            small_b_all=pltpu.VMEM((n_dp, 8, VB), f32),
            tok=pltpu.VMEM((R, D), bf16),
            gt=pltpu.VMEM((2, LB, D), f32),
            gs=pltpu.VMEM((2, min(256, L // 2), CD), f32),
            tc=pltpu.VMEM((S, 128), f32),
            ts=pltpu.VMEM((S, 128), f32),
            Nv=pltpu.VMEM((S, D), bf16),
            Gv=pltpu.VMEM((S, D), bf16),
            Av=pltpu.VMEM((S, F), bf16),
            Hv=pltpu.VMEM((S, F), bf16),
            QKV=pltpu.VMEM((3, S, L), bf16),
            ATv=pltpu.VMEM((S, L), bf16),
            flat=pltpu.VMEM((128, S), bf16),
            DMv=pltpu.VMEM((S, 3 * L), bf16),
            LSE=pltpu.VMEM((heads, 1, S), f32),
            dk=pltpu.VMEM((S, 128), f32),
            dv=pltpu.VMEM((S, 128), f32),
            wa=pltpu.VMEM((3, D, T), bf16),
            wb=pltpu.VMEM((2 * T, D), bf16),
            wo=pltpu.VMEM((L, D), bf16),
            ob=pltpu.VMEM((2, S // 2, TD), bf16),
            YP=pltpu.VMEM((NC, S, CD), bf16),
            zs=pltpu.VMEM((3, R, D), bf16),
            st_up=pltpu.VMEM((2, CD, F), bf16),
            st_down=pltpu.VMEM((2, F, CD), bf16),
            ta_up=pltpu.VMEM((2, 2, CD // 2, F), bf16),
            ta_down=pltpu.VMEM((2, 2, F // 2, CD), bf16),
            sems=pltpu.SemaphoreType.DMA((n_sems,)),
            slot_sems=pltpu.SemaphoreType.DMA((32,)),
            out_sems=pltpu.SemaphoreType.DMA((2, n_mp)),
        )
        names = list(ins) + list(outs) + list(scratch)
        got = pl.pallas_call(
            make_kernel(n_dp, n_mp, R, F, L, names, n_sems),
            out_shape=[jax.ShapeDtypeStruct(s, t) for s, t in outs.values()],
            in_specs=[any_spec] * len(ins),
            out_specs=[vmem_spec if n.endswith("_sums") else any_spec for n in outs],
            scratch_shapes=list(scratch.values()),
            name="layer",
            cost_estimate=pl.CostEstimate(
                flops=6 * S * D * (4 * L + 2 * F), bytes_accessed=150 << 20, transcendentals=0
            ),
            compiler_params=pltpu.CompilerParams(
                collective_id=0, has_side_effects=True, vmem_limit_bytes=62 << 20
            ),
        )(*ins.values())
        got = types.SimpleNamespace(**dict(zip(outs, got)))

        def mine(values, axis):
            return lax.dynamic_slice_in_dim(values, me * share, share, axis)

        sums = got.bias_sums.reshape(-1)
        bias = got.row_sums[2]
        return (
            got.layer_out,
            got.grad_tokens,
            got.row_sums[0],
            got.row_sums[1],
            jnp.stack([got.grad_q, got.grad_k, got.grad_v], 1),
            mine(sums[: 3 * L].reshape(3, heads, HD), 2),
            got.grad_out,
            bias,
            got.grad_up,
            mine(sums[nq * VB : nq * VB + F].reshape(F // HD, HD), 1),
            got.grad_down,
            bias,
        )

    return body


def solution(mesh):
    n_dp, n_mp = mesh.shape["dp"], mesh.shape["mp"]
    weights_in = (
        P("dp"),
        P("dp"),
        P("dp", None, "mp"),
        P(None, "mp", "dp"),
        P("mp", "dp"),
        P("dp"),
        P("dp", "mp"),
        P("mp", "dp"),
        P("mp", "dp"),
        P("dp"),
    )
    rows = P(("dp", "mp"), None)
    return jax.shard_map(
        make_body(n_dp, n_mp),
        mesh=mesh,
        in_specs=(rows,) + weights_in + (rows,),
        out_specs=(rows, rows) + weights_in,
        check_vma=False,
    )
```

```python
import types

import jax
import jax.numpy as jnp
import numpy as np
from jax import lax
from jax.experimental import pallas as pl
from jax.experimental.pallas import tpu as pltpu
from jax.sharding import PartitionSpec as P

D = 2048
HD = 64
ROT = 32
EPS = 1e-05
BQ = 256
LB = 32
VB = 512
MESH = pl.DeviceIdType.MESH
NN = (((1,), (0,)), ((), ()))
NT = (((1,), (1,)), ((), ()))
TN = (((0,), (0,)), ((), ()))
bf16 = jnp.bfloat16
f32 = jnp.float32


def mm(left, right, dims):
    return lax.dot_general(left, right, dims, preferred_element_type=f32)


def flip(index, mask):
    bit = 1
    while bit <= mask:
        if mask & bit:
            index = index + bit * (1 - 2 * lax.rem(lax.div(index, bit), 2))
        bit *= 2
    return index


def span(bits):
    found = [0]
    for bit in bits:
        found = found + [m + bit for m in found]
    return found


def maybe_static(pred, act):
    if isinstance(pred, bool):
        if pred:
            act()
    else:
        pl.when(pred)(act)


def maybe(pred, act):
    if pred is None:
        act()
    else:
        pl.when(pred)(act)


class Sent:
    def __init__(self, out, into, pred_out, pred_into):
        self.out, self.into, self.pred_out, self.pred_into = out, into, pred_out, pred_into
        self.came, self.left = False, False

    def start(self):
        maybe(self.pred_out, self.out.start)

    def arrive(self):
        if not self.came:
            self.came = True
            maybe(self.pred_into, self.into.wait_recv)

    def finish(self):
        if not self.left:
            self.left = True
            maybe(self.pred_out, self.out.wait_send)


class Wire:
    def __init__(self, sems, count):
        self.sems, self.count, self.used, self.open = sems, count, 0, []

    def sem(self):
        assert self.used < self.count
        self.used += 1
        return self.sems.at[self.used - 1]

    def sems_of(self, n):
        assert self.used + n <= self.count
        self.used += n
        base = self.used - n
        return lambda j: self.sems.at[base + j]

    def send(self, src, dst, got, dev, pred_out=None, pred_into=None):
        s, r = self.sem(), self.sem()
        out = pltpu.make_async_remote_copy(src, dst, s, r, dev, MESH)
        into = pltpu.make_async_remote_copy(got, got, s, r, dev, MESH)
        one = Sent(out, into, pred_out, pred_into)
        one.start()
        self.open.append(one)
        return one

    def local(self, src, dst):
        copy = pltpu.make_async_copy(src, dst, self.sem())
        copy.start()
        return copy

    def finish(self):
        for one in self.open:
            one.finish()


def make_kernel(n_dp, n_mp, R, F, L, names, n_sems):
    S = R * n_mp
    CD = D // n_dp
    NC = n_dp // 2
    T = min(512, F)
    TD = 512
    HS = S // 2
    NH = n_mp // 2
    bits = [b for b in (2, 4, 8, 16, 32) if b < n_dp]
    orders = [bits, bits[1:] + bits[:1]]
    masks = sorted(span(bits), key=lambda m: -bin(m).count("1"))
    place = {m: n for n, m in enumerate(masks)}
    RB = min(BQ, S)

    def kernel(*refs):
        ref = types.SimpleNamespace(**dict(zip(names, refs)))
        me = lax.axis_index("dp")
        z = lax.axis_index("mp")
        wire = Wire(ref.sems, n_sems)
        slot_sems = ref.slot_sems
        mate = (flip(me, 1), z)
        up_dev = (me, jnp.minimum(z + 1, n_mp - 1))
        down_dev = (me, jnp.maximum(z - 1, 0))
        mine_half = lax.div(z, NH)
        barrier = pltpu.get_barrier_semaphore()
        for m in range(1, n_dp):
            pl.semaphore_signal(barrier, inc=1, device_id=(flip(me, m), z), device_id_type=MESH)
        for k in range(1, n_mp):
            pl.semaphore_signal(
                barrier, inc=1, device_id=(me, lax.rem(z + k, n_mp)), device_id_type=MESH
            )
        pl.semaphore_wait(barrier, n_dp - 1 + n_mp - 1)

        def ds(k, size):
            return pl.ds(pl.multiple_of(k * size, size), size)

        def run(copies):
            for c in copies:
                c.start()
            for c in copies:
                c.wait()

        def pieces_of(full, rows, kind):
            half = rows // 2

            def piece(k, h):
                if kind == "rows":
                    if h is None:
                        return full.at[ds(k, rows), :]
                    return full.at[pl.ds(pl.multiple_of(k * rows + h * half, half), half), :]
                if kind == "cube":
                    if h is None:
                        return full.at[:, ds(k, rows), :]
                    return full.at[:, pl.ds(pl.multiple_of(k * rows + h * half, half), half), :]
                if h is None:
                    return full.at[:, ds(k, CD)]
                return full.at[pl.ds(h * half, half), ds(k, CD)]

            return piece

        def half_rows_of(array, n, h, cube):
            if cube:
                return array.at[:, pl.ds(h * n, n), :]
            return array.at[pl.ds(h * n, n), :]

        weights = {
            "up": (ref.w_up, pieces_of(ref.full_up, CD, "rows"), CD // 2, ref.st_up.at[0]),
            "qkv": (ref.w_qkv, pieces_of(ref.full_qkv, CD, "cube"), CD // 2, ref.st_up.at[1]),
            "down": (ref.w_down, pieces_of(ref.full_down, F, "cols"), F // 2, ref.st_down.at[0]),
            "out": (ref.w_out, pieces_of(ref.full_out, L, "cols"), L // 2, ref.st_down.at[1, pl.ds(0, L)]),
        }
        order = ["up", "qkv", "down", "out"]
        arrivals = {w: [[] for _ in bits] for w in order}

        mates = {w: [] for w in order}

        def to_mate(w, j):
            piece = weights[w][1]
            for h in range(2):
                way = orders[h]
                for sub in span(way[:j]):
                    k = flip(flip(me, sub), way[j])
                    got = piece(flip(k, 1), h)
                    mates[w].append(wire.send(piece(k, h), piece(k, h), got, mate))

        def gather_step(w, j):
            own, piece, n, _ = weights[w]
            if j > 0:
                for one in arrivals[w][j - 1]:
                    one.arrive()
            for h in range(2):
                way = orders[h]
                for sub in span(way[:j]):
                    k = flip(me, sub)
                    src = half_rows_of(own, n, h, w == "qkv") if sub == 0 else piece(k, h)
                    got = piece(flip(k, way[j]), h)
                    arrivals[w][j].append(wire.send(src, piece(k, h), got, (flip(me, way[j]), z)))
            if j > 0:
                to_mate(w, j - 1)
            else:
                got = piece(flip(me, 1), None)
                mates[w].append(wire.send(own, piece(me, None), got, mate))

        def gather_mate(w):
            for one in arrivals[w][-1]:
                one.arrive()
            to_mate(w, len(bits) - 1)

        def gathered(w):
            for one in mates[w]:
                one.arrive()

        def moves(w, far, near, base, out):
            pairs = [(far, near)]
            if w == "qkv":
                pairs = [(far.at[j], near.at[:, pl.ds(j * L, L)]) for j in range(3)]
            return [
                pltpu.make_async_copy(*(p[::-1] if out else p), slot_sems.at[base + n])
                for n, p in enumerate(pairs)
            ]

        hr = R // 2

        def line_step(own, full, s, hh, log):
            rows = pl.ds(hh * hr, hr)
            if s > 1:
                for one in log[(s - 1, hh)]:
                    one.arrive()
            up, down = z - (s - 1), z + (s - 1)
            first = own.at[rows, :] if s == 1 else None
            one = wire.send(
                first if s == 1 else full.at[jnp.maximum(up, 0), rows, :],
                full.at[jnp.maximum(up, 0), rows, :],
                full.at[jnp.maximum(z - s, 0), rows, :],
                up_dev,
                jnp.logical_and(z + 1 < n_mp, up >= 0),
                z - s >= 0,
            )
            two = wire.send(
                first if s == 1 else full.at[jnp.minimum(down, n_mp - 1), rows, :],
                full.at[jnp.minimum(down, n_mp - 1), rows, :],
                full.at[jnp.minimum(z + s, n_mp - 1), rows, :],
                down_dev,
                jnp.logical_and(z >= 1, down < n_mp),
                z + s < n_mp,
            )
            log[(s, hh)] = [one, two]

        def line_arrive(log, s):
            for hh in range(2):
                for one in log[(s, hh)]:
                    one.arrive()

        class Loads:
            def __init__(self):
                self.open = []

            def rows(self, full, near, s):
                for c, pred in ((z - s, z - s >= 0), (z + s, z + s < n_mp)):
                    safe = jnp.clip(c, 0, n_mp - 1)
                    copy = pltpu.make_async_copy(full.at[safe], near.at[ds(safe, R), :], wire.sem())
                    maybe(pred, copy.start)
                    self.open.append((copy, pred))

            def wait(self):
                for copy, pred in self.open:
                    maybe(pred, copy.wait)
                self.open = []

        def add_rows(out, terms, count, block, wide):
            @pl.loop(0, count // block)
            def _(i):
                rows = pl.ds(pl.multiple_of(i * block, block), block)
                total = terms[0][rows, 0:wide].astype(f32)
                for term in terms[1:]:
                    total = total + term[rows, 0:wide].astype(f32)
                out[rows, 0:wide] = total.astype(out.dtype)

        class LineSum:
            def __init__(self, part, from_below, from_above):
                self.part, self.below, self.above = part, from_below, from_above
                self.us, self.ur = wire.sems_of(n_mp), wire.sems_of(n_mp)
                self.ds, self.dr = wire.sems_of(n_mp), wire.sems_of(n_mp)

            def up(self, j):
                return pltpu.make_async_remote_copy(
                    self.part.at[j], self.below.at[j], self.us(j), self.ur(j), up_dev, MESH
                )

            def down(self, j):
                return pltpu.make_async_remote_copy(
                    self.part.at[j], self.above.at[j], self.ds(j), self.dr(j), down_dev, MESH
                )

            def begin(self, near):
                @pl.when(z == 0)
                def _():
                    for j in range(n_mp - 1, 0, -1):
                        if (j < NH) == near:
                            self.up(j).start()

                @pl.when(z == n_mp - 1)
                def _():
                    for j in range(n_mp - 1):
                        if (j >= NH) == near:
                            self.down(j).start()

            def merge(self, j, got, sent):
                a, b = ref.zs.at[0], ref.zs.at[1]
                halves = [pl.ds(h * hr, hr) for h in range(2)]
                home = pltpu.make_async_copy(self.part.at[j], a, slot_sems.at[4])
                home.start()
                sent.wait_recv()
                come = [
                    pltpu.make_async_copy(got.at[j, rows, :], b.at[rows, :], slot_sems.at[5 + h])
                    for h, rows in enumerate(halves)
                ]
                for c in come:
                    c.start()
                home.wait()
                back = []
                for h, rows in enumerate(halves):
                    come[h].wait()
                    near = a.at[rows, :]
                    add_rows(near, [near, b.at[rows, :]], hr, LB, D)
                    back.append(
                        pltpu.make_async_copy(near, self.part.at[j, rows, :], slot_sems.at[7 + h])
                    )
                    back[-1].start()
                for c in back:
                    c.wait()
                sent.start()

            def step(self, tau):
                j = n_mp - 1 - tau + z

                @pl.when(jnp.logical_and(z > 0, jnp.logical_and(j < n_mp, tau >= z)))
                def _():
                    self.merge(j, self.below, self.up(j))

                i = tau - (n_mp - 1 - z)

                @pl.when(jnp.logical_and(z < n_mp - 1, i >= 0))
                def _():
                    self.merge(i, self.above, self.down(i))

            def arrive(self):
                @pl.when(z > 0)
                def _():
                    self.up(z).wait_recv()

                @pl.when(z < n_mp - 1)
                def _():
                    self.down(z).wait_recv()

            def load(self, out):
                home = pltpu.make_async_copy(self.part.at[z], out.at[0], slot_sems.at[4])
                home.start()

                @pl.when(z > 0)
                def _():
                    run([pltpu.make_async_copy(self.below.at[z], out.at[1], slot_sems.at[5])])

                @pl.when(z == 0)
                def _():
                    out[1] = jnp.zeros((R, D), bf16)

                @pl.when(z < n_mp - 1)
                def _():
                    run([pltpu.make_async_copy(self.above.at[z], out.at[2], slot_sems.at[6])])

                @pl.when(z == n_mp - 1)
                def _():
                    out[2] = jnp.zeros((R, D), bf16)

                home.wait()

            def finish(self):
                for j in range(n_mp):

                    @pl.when(j > z)
                    def _():
                        self.up(j).wait_send()

                    @pl.when(j < z)
                    def _():
                        self.down(j).wait_send()

        class Ring:
            def __init__(self, slots, first_sem):
                self.slots, self.first_sem, self.base, self.primed = slots, first_sem, 0, 0
                self.full = False

            def tile(self, copies, i, slot):
                return [
                    pltpu.make_async_copy(src, dst, slot_sems.at[self.first_sem + self.slots * n + slot])
                    for n, (src, dst) in enumerate(copies(i, slot))
                ]

            def start(self, copies, i, slot):
                for c in self.tile(copies, i, slot):
                    c.start()

            def fill(self, copies):
                for d in range(self.slots - 1):
                    self.start(copies, d, (self.base + d) % self.slots)

            def prime(self, copies):
                if not self.primed:
                    self.fill(copies)
                self.primed = self.slots - 1

            def step(self, count, copies, then, i):
                slot = lax.rem(self.base + i, self.slots)
                ahead = i + self.slots - 1

                def next_tile(slot):
                    wanted = ahead < count
                    if self.full:
                        wanted = jnp.logical_and(wanted, i > 0)
                    maybe_static(wanted, lambda: self.start(copies, ahead, slot))
                    if then is not None:
                        for d in range(self.slots - 1):
                            maybe_static(ahead == count + d, lambda: self.start(then, d, slot))

                next_tile(lax.rem(self.base + ahead, self.slots))
                for c in self.tile(copies, i, slot):
                    c.wait()
                return slot

            def turned(self, count, then):
                self.base = (self.base + count) % self.slots
                self.primed = 0 if then is None else self.slots - 1
                self.full = False

            def fill_last(self, copies):
                d = self.slots - 1
                self.start(copies, d, (self.base + d) % self.slots)
                self.full = True

            def run(self, count, copies, work, then=None):
                self.prime(copies)

                @pl.loop(0, count)
                def _(i):
                    work(i, self.step(count, copies, then, i))

                self.turned(count, then)

        tall_ring, wide_ring = Ring(3, 18), Ring(2, 22)

        normed, pulled = ref.full_normed, ref.full_pulled
        pulled_log, normed_log = {}, {}
        Nv, Gv, Av, Hv = ref.Nv, ref.Gv, ref.Av, ref.Hv
        own_rows = ds(z, R)
        vec_a, vec_b, vrow = ref.vec_a_all, ref.vec_b_all, ref.vrow
        vec_sent = []
        for m in range(1, n_dp):
            k = flip(me, m)
            vec_sent.append(wire.send(ref.vec_a, vec_a.at[me], vec_a.at[k], (k, z)))
        own_vec = [wire.local(ref.vec_a, vec_a.at[me]), wire.local(ref.vec_b, vec_b.at[me])]
        tok_copy = wire.local(ref.tokens, ref.tok)
        line_step(ref.cotangent, pulled, 1, 0, pulled_log)
        gather_step("up", 0)
        vec_b_sent = []
        for m in range(1, n_dp):
            k = flip(me, m)
            vec_b_sent.append(wire.send(ref.vec_b, vec_b.at[me], vec_b.at[k], (k, z)))
        gather_step("qkv", 0)
        own_loads = [
            c for n, w in enumerate(order) for c in moves(w, weights[w][0], weights[w][3], 3 * n, False)
        ]
        for c in own_loads:
            c.start()
        cot_copy = wire.local(ref.cotangent, Gv.at[own_rows, :])
        tables = [
            wire.local(a, b)
            for a, b in ((ref.rope_c, ref.tc), (ref.rope_s, ref.ts))
        ]

        for one in vec_sent:
            one.arrive()
        for c in own_vec:
            c.wait()
        for k in range(n_dp):
            for n in range(CD // 128):
                lanes = pl.ds(k * CD + n * 128, 128)
                for row in range(2):
                    at = row * (CD // 128) + n
                    vrow[row : row + 1, lanes] = vec_a[k, at : at + 1, :]
                one, two = 2 * (CD // 128) + n, 3 * (CD // 128) + n
                vrow[2:3, lanes] = vec_a[k, one : one + 1, :] + vec_a[k, two : two + 1, :]
        tok_copy.wait()
        tok = ref.tok

        def stats(rows):
            x = tok[rows, :].astype(f32)
            centre = jnp.mean(x, -1, keepdims=True)
            offset = x - centre
            spread = jnp.mean(offset * offset, -1, keepdims=True)
            scale = lax.rsqrt(spread + EPS)
            return x, offset * scale, scale


        @pl.loop(0, R // LB)
        def _(i):
            _, xhat, _ = stats(ds(i, LB))
            v = (xhat * vrow[0:1, :] + vrow[1:2, :]).astype(bf16)
            Nv[pl.ds(pl.multiple_of(z * R + i * LB, LB), LB), :] = v

        own_normed = Nv.at[own_rows, :]
        for hh in range(2):
            line_step(own_normed, normed, 1, hh, normed_log)

        for c in own_loads:
            c.wait()
        own_stores = [
            c
            for n, w in enumerate(order)
            for c in moves(w, weights[w][1](me, None), weights[w][3], 3 * n, True)
        ]
        for c in own_stores:
            c.start()
        for j in range(1, len(bits)):
            gather_step("up", j)
        gather_step("down", 0)
        for j in range(1, len(bits)):
            gather_step("qkv", j)
        gather_step("out", 0)
        for c in own_stores:
            c.wait()
        for c in tables:
            c.wait()
        for one in vec_b_sent:
            one.arrive()
        total = vec_b[0]
        for k in range(1, n_dp):
            total = total + vec_b[k]
        nq, nu = -(-3 * L // VB), F // VB
        for n in range(nq):
            vrow[3:4, n * VB : (n + 1) * VB] = total[n : n + 1, :]
        for n in range(nu):
            vrow[4:5, n * VB : (n + 1) * VB] = total[nq + n : nq + n + 1, :]

        loads = Loads()
        line_step(own_normed, normed, 2, 0, normed_log)
        line_step(own_normed, normed, 2, 1, normed_log)
        gather_mate("up")
        loads.rows(normed, Nv, 1)
        for s in range(2, NH):
            for hh in range(2):
                line_step(own_normed, normed, s + 1, hh, normed_log)
            loads.rows(normed, Nv, s)
        gathered("up")
        loads.wait()

        wa, wb = ref.wa, ref.wb
        WT = min(1024, F)
        C0, C1 = 0.7978845608028654, 0.044715

        def sequence_half(other, quarter=None):
            which = 1 - mine_half if other else mine_half
            if quarter is None:
                return ds(which, HS)
            return pl.ds(pl.multiple_of(which * HS + quarter * (HS // 2), HS // 2), HS // 2)

        own_quarters = [sequence_half(False, q) for q in range(2)]
        near_quarter = [ds(1 + lax.rem(1 + mine_half, 2), HS // 2)]
        far_quarter = [ds(3 - 3 * mine_half, HS // 2)]

        def tall(full, rows, i, slot, width):
            return [(full.at[:, ds(i, width)], wa.at[slot, pl.ds(0, rows), pl.ds(0, width)])]

        def tall_value(slot, rows, width):
            return wa[slot, 0:rows, 0:width]

        def wide_slot(slot):
            return pl.ds(pl.multiple_of(slot * T, T), T)

        def up_copies(i, slot):
            return tall(ref.full_up, D, i, slot, T)

        def hidden(parts, then=None):
            def work(i, slot):
                cols = ds(i, T)
                w = tall_value(slot, D, T)
                for rows in parts:
                    v = mm(Nv[rows, :], w, NN) + vrow[4:5, cols]
                    v2 = v * v
                    a = 0.5 * jnp.tanh(v * ((C0 * C1) * v2 + C0)) + 0.5
                    act = v * a
                    Av[rows, cols] = act.astype(bf16)
                    Hv[rows, cols] = (a + act * (1.0 - a) * ((6 * C0 * C1) * v2 + 2 * C0)).astype(bf16)

            tall_ring.run(F // T, up_copies, work, then)

        QKV, ATv, LSE = ref.QKV, ref.ATv, ref.LSE
        tc, ts = ref.tc, ref.ts
        first_turn = lax.rem(lax.broadcasted_iota(jnp.int32, (1, 128), 1), HD) < ROT // 2

        def turn(u, rows, sign):
            left = pltpu.roll(u, 128 - ROT // 2, 1)
            right = pltpu.roll(u, ROT // 2, 1)
            return u * tc[rows, :] + sign * (jnp.where(first_turn, left, right) * ts[rows, :])

        def qkv_copies(j, slot):
            return [(ref.full_qkv.at[j], wa.at[slot, :, pl.ds(0, L)])]

        def mix(parts):
            tall_ring.prime(qkv_copies)
            for j in range(3):
                slot = tall_ring.step(3, qkv_copies, None, j)
                w = tall_value(slot, D, L)
                for rows in parts:
                    v = mm(Nv[rows, :], w, NN) + vrow[3:4, j * L : (j + 1) * L]
                    for c in range(L // 128):
                        u = v[:, c * 128 : (c + 1) * 128]
                        if j < 2:
                            u = turn(u, rows, 1.0)
                        u = u.astype(bf16)
                        if j == 0:
                            u = u * bf16(HD**-0.5)
                        QKV[j, rows, pl.ds(c * 128, 128)] = u
            tall_ring.turned(3, None)

        if NH < n_mp - 1:
            line_step(own_normed, normed, NH + 1, 0, normed_log)
        hidden(own_quarters)
        tall_ring.prime(up_copies)
        for j in range(1, len(bits)):
            gather_step("down", j)
        for s in range(NH, n_mp - 1):
            for hh in range(2):
                if (s + 1, hh) not in normed_log:
                    line_step(own_normed, normed, s + 1, hh, normed_log)
            loads.rows(normed, Nv, s)
        line_step(ref.cotangent, pulled, 1, 1, pulled_log)
        loads.wait()
        hidden(near_quarter)
        gather_mate("qkv")
        for j in range(1, len(bits)):
            gather_step("out", j)
        gathered("qkv")
        mix(own_quarters + near_quarter)
        tall_ring.prime(up_copies)
        line_arrive(normed_log, n_mp - 1)
        loads.rows(normed, Nv, n_mp - 1)
        loads.wait()
        line_step(ref.cotangent, pulled, 2, 0, pulled_log)
        normed_mate = wire.send(Nv, ref.mate_normed, ref.mate_normed, mate)
        hidden(far_quarter, qkv_copies)
        line_step(ref.cotangent, pulled, 2, 1, pulled_log)
        for s in range(3, n_mp - 1):
            for hh in range(2):
                line_step(ref.cotangent, pulled, s, hh, pulled_log)
        mix(far_quarter)
        act_mate = wire.send(Av, ref.mate_act, ref.mate_act, mate)

        corner = lax.broadcasted_iota(jnp.int32, (RB, RB), 0) <= lax.broadcasted_iota(
            jnp.int32, (RB, RB), 1
        )
        lane = lax.broadcasted_iota(jnp.int32, (1, 128), 1)
        pair_masks = [lane < HD, lane >= HD]

        def only(values, mask):
            return jnp.where(mask, values, jnp.zeros_like(values))

        wo = ref.wo
        wo_load = pltpu.make_async_copy(ref.full_out, wo, wire.sem())

        def out_copies(i, slot):
            return tall(ref.full_down, F, i, slot, TD)

        def down_copies(i, slot):
            return [(ref.full_down.at[ds(i, T), :], wb.at[wide_slot(slot), :])]


        flat = ref.flat
        units = [(i, e) for i in range(S // RB) for e in range(2)]

        def places(i):
            return pl.ds(i * RB, RB), pl.ds(0, i * RB)

        def staggered(*phases):
            for t in range(len(units) + len(phases) - 1):
                for lag, phase in enumerate(phases):
                    if 0 <= t - lag < len(units):
                        phase(*units[t - lag])

        def attend_pair(hp):
            lanes = ds(hp, 128)

            flat[...] = QKV[2, :, lanes].T
            scores, weighted, done = {}, {}, {}

            def score(i, e):
                rows, past = places(i)
                q = only(QKV[0, rows, lanes], pair_masks[e])
                own = mm(QKV[1, rows, lanes], q, NT)
                scores[i, e] = own, mm(QKV[1, past, lanes], q, NT) if i else None

            def soften(i, e):
                own, earlier = scores.pop((i, e))
                own = jnp.where(corner, own, -1e30)
                top = jnp.max(own, 0, keepdims=True)
                if i:
                    top = jnp.maximum(top, jnp.max(earlier, 0, keepdims=True))
                    earlier = jnp.exp(earlier - top)
                own = jnp.exp(own - top)
                mass = jnp.sum(own, 0, keepdims=True)
                if i:
                    mass = mass + jnp.sum(earlier, 0, keepdims=True)
                inverse = 1.0 / mass
                LSE[hp * 2 + e, :, places(i)[0]] = top + jnp.log(mass)
                own = (own * inverse).astype(bf16)
                weighted[i, e] = own, (earlier * inverse).astype(bf16) if i else None

            def attend(i, e):
                rows, past = places(i)
                own, earlier = weighted.pop((i, e))
                values = flat.at[pl.ds(e * HD, HD), :]
                total = mm(values[:, rows], own, NN)
                if i:
                    total = total + mm(values[:, past], earlier, NN)
                done[e] = total
                if e == 1:
                    ATv[rows, lanes] = jnp.concatenate([done[0], done[1]], 0).T.astype(bf16)

            staggered(score, soften, attend)

        pairs = L // 128
        pl.loop(0, pairs // 2)(attend_pair)
        gather_mate("down")
        gather_mate("out")

        @pl.loop(pairs // 2, pairs)
        def _(hp):
            @pl.when(hp == pairs - 1)
            def _():
                for one in mates["out"] + mates["down"]:
                    one.into.wait_recv()
                wo_load.start()
                tall_ring.fill(out_copies)
                wide_ring.fill(down_copies)

            attend_pair(hp)

        for one in mates["out"] + mates["down"]:
            one.came = True
        tall_ring.primed, wide_ring.primed = 2, 1

        att_mate = wire.send(ATv, ref.mate_att, ref.mate_att, mate)
        line_step(ref.cotangent, pulled, n_mp - 1, 0, pulled_log)
        wo_load.wait()

        ob = ref.ob
        out_sems = ref.out_sems

        def put(part, half, i, slot):
            return [
                pltpu.make_async_copy(
                    ob.at[slot, pl.ds(j * R, R), :],
                    part.at[half * NH + j, :, ds(i, TD)],
                    out_sems.at[slot, j],
                )
                for j in range(NH)
            ]

        def product_half(part, other, ring, copies, value, then):
            half = 1 - mine_half if other else mine_half

            def work(i, slot):
                place_out = lax.rem(i, 2)

                @pl.when(i >= 2)
                def _():
                    for c in put(part, half, i - 2, place_out):
                        c.wait()

                for quarter in range(2):
                    v = value(sequence_half(other, quarter), slot, i)
                    ob[place_out, pl.ds(quarter * (HS // 2), HS // 2), :] = v.astype(bf16)
                for c in put(part, half, i, place_out):
                    c.start()

            ring.run(D // TD, copies, work, then)
            for i in range(D // TD - 2, D // TD):
                for c in put(part, half, i, i % 2):
                    c.wait()

        def out_value(rows, slot, i):
            v = mm(Av[rows, :], tall_value(slot, F, TD), NN)
            return v + mm(ATv[rows, :], wo[:, ds(i, TD)], NN)

        sum1 = LineSum(ref.part1, ref.below1, ref.above1)
        product_half(ref.part1, True, tall_ring, out_copies, out_value, out_copies)
        sum1.begin(False)
        line_step(ref.cotangent, pulled, n_mp - 1, 1, pulled_log)
        product_half(ref.part1, False, tall_ring, out_copies, out_value, None)
        sum1.begin(True)

        pulled_loads = Loads()
        last = n_mp - n_mp // 4
        for s in range(1, last):
            line_arrive(pulled_log, s)
            pulled_loads.rows(pulled, Gv, s)
        YP = ref.YP
        small = ref.small
        small[...] = jnp.zeros_like(small)
        act_mate.arrive()
        cot_copy.wait()
        pulled_loads.wait()
        half_a = sequence_half(False)
        half_b = sequence_half(True)

        def mate_half(half):
            return wire.send(
                Gv.at[half, :], ref.mate_pulled.at[half, :], ref.mate_pulled.at[half, :], mate
            )

        def load_mate_columns(source, rows):
            return [
                wire.local(source.at[rows, ds(flip(me, m), CD)], YP.at[n, rows, :])
                for n, m in enumerate(masks)
            ]

        pulled_a = mate_half(half_a)

        def push_hidden(parts, then):
            def work(i, slot):
                cols = ds(i, T)
                total = small[4:5, cols]
                for rows in parts:
                    d = mm(Gv[rows, :], wb[wide_slot(slot), :], NT) * Hv[rows, cols].astype(f32)
                    d = d.astype(bf16)
                    Hv[rows, cols] = d
                    total = total + jnp.sum(d.astype(f32), 0, keepdims=True)
                small[4:5, cols] = total

            wide_ring.run(F // T, down_copies, work, then)

        push_hidden(own_quarters + near_quarter, down_copies)
        wide_ring.fill_last(down_copies)
        pulled_a.arrive()
        mate_columns = load_mate_columns(ref.mate_pulled, half_a)
        for s in range(last, n_mp):
            line_arrive(pulled_log, s)
            pulled_loads.rows(pulled, Gv, s)
        pulled_loads.wait()
        pulled_b = mate_half(half_b)
        push_hidden(far_quarter, None)
        hid_mate = wire.send(Hv, ref.mate_hid, ref.mate_hid, mate)
        mate_tiles = [wire.local(ref.mate_act, wb.at[:, pl.ds(0, F)])]
        att_mate.arrive()
        mate_load = wire.local(ref.mate_att, wa.at[0, pl.ds(0, S), pl.ds(0, L)])
        pulled_b.arrive()
        mate_columns = mate_columns + load_mate_columns(ref.mate_pulled, half_b)
        DMv = ref.DMv
        for half in range(2):
            rows = pl.ds(half * HS, HS)
            ob[half, :, 0:L] = mm(Gv[rows, :], wo[...], NT).astype(bf16)
        for c in mate_tiles + mate_columns:
            c.wait()

        grad_info = {
            "down": (ref.gw_down, ref.rb_down, ref.st_down, ref.ta_down, F // 2, 128),
            "out": (ref.gw_out, ref.rb_out, ref.st_down.at[:, pl.ds(0, L)], ref.ta_down.at[:, :, pl.ds(0, L // 2)], L // 2, 128),
            "up": (ref.gw_up, ref.rb_up, ref.st_up, ref.ta_up, CD // 2, 16),
            "qkv": (ref.gw_qkv, ref.rb_qkv, ref.st_up, ref.ta_up, CD // 2, 16),
        }
        offset, position = 0, []
        for i in range(len(bits)):
            position.append(offset)
            offset += 2 ** (len(bits) - 1 - i)

        def half_of(w, chunk, h):
            return half_rows_of(chunk, grad_info[w][4], h, w == "qkv")

        came = {}

        def scatter_send(w, h, i, m):
            gw, rb = grad_info[w][:2]
            rest = span(orders[h][i + 1 :])
            keep = m - orders[h][i]
            got = half_of(w, rb.at[position[i] + rest.index(keep)], h)
            came[(w, h, i, keep)] = wire.send(
                half_of(w, gw.at[place[m]], h), got, got, (flip(me, orders[h][i]), z)
            )

        def scatter_first(w, m):
            for h in range(2):
                if m & orders[h][0]:
                    scatter_send(w, h, 0, m)

        def scatter_step(w, i):
            gw, rb, _, ta, n, block = grad_info[w]
            wide = 3 * L if w == "qkv" else ta.shape[-1]
            for k in range(2 ** (len(bits) - 1 - i)):
                work = []
                for h in range(2):
                    way = orders[h]
                    m = way[i] + span(way[i + 1 :])[k]
                    terms = []
                    for e in range(i):
                        came[(w, h, e, m)].arrive()
                        rest = span(way[e + 1 :])
                        terms.append(half_of(w, rb.at[position[e] + rest.index(m)], h))
                    home = half_of(w, gw.at[place[m]], h)
                    first = moves(w, home, ta.at[h, 0], 9 * h, False)
                    first = first + moves(w, terms[0], ta.at[h, 1], 9 * h + 3, False)
                    for c in first:
                        c.start()
                    work.append((h, m, home, terms, first))
                for h, m, home, terms, first in work:
                    for c in first:
                        c.wait()
                    add_rows(ta.at[h, 0], [ta.at[h, 0], ta.at[h, 1]], n, block, wide)
                    for term in terms[1:]:
                        run(moves(w, term, ta.at[h, 1], 9 * h + 3, False))
                        add_rows(ta.at[h, 0], [ta.at[h, 0], ta.at[h, 1]], n, block, wide)
                    for c in moves(w, home, ta.at[h, 0], 9 * h + 6, True):
                        c.start()
                for h, m, home, terms, first in work:
                    for c in moves(w, home, ta.at[h, 0], 9 * h + 6, True):
                        c.wait()
                    scatter_send(w, h, i, m)

        def scatter_done(w):
            for h in range(2):
                for i in range(len(bits)):
                    came[(w, h, i, 0)].arrive()

        finals = {
            "down": (ref.grad_down, ref.gs),
            "out": (ref.grad_out, ref.gs),
            "up": (ref.grad_up, ref.gt),
            "qkv": ([ref.grad_q, ref.grad_k, ref.grad_v], ref.gt),
        }

        def weight_sum(w):
            gw, rb, st, ta, n, _ = grad_info[w]
            out, staged = finals[w]
            scatter_done(w)
            near = [st.at[0], st.at[1]]
            far = [gw.at[place[0]]] + [rb.at[position[i]] for i in range(len(bits))]
            first = moves(w, far[0], near[0], 0, False) + moves(w, far[1], near[1], 3, False)
            for c in first:
                c.start()
            rest = []
            for q, source in enumerate(far[2:]):
                for h in range(2):
                    rest += moves(w, half_of(w, source, h), ta.at[h, q], 6 + 6 * q + 3 * h, False)
            for c in rest:
                c.start()
            for c in first + rest:
                c.wait()
            block = min(n, staged.shape[1])
            wide = 3 * L if w == "qkv" else gw.shape[-1]

            def out_of(h, i, slot):
                rows = pl.ds(pl.multiple_of(h * n + i * block, block), block)
                if w == "qkv":
                    return [
                        pltpu.make_async_copy(
                            staged.at[slot, pl.ds(0, block), pl.ds(j * L, L)],
                            out[j].at[rows, :],
                            slot_sems.at[18 + 3 * slot + j],
                        )
                        for j in range(3)
                    ]
                return [
                    pltpu.make_async_copy(
                        staged.at[slot, pl.ds(0, block), pl.ds(0, wide)],
                        out.at[rows, :],
                        slot_sems.at[18 + 3 * slot],
                    )
                ]

            count = n // block
            for h in range(2):

                @pl.loop(0, count)
                def _(i):
                    slot = lax.rem(h * count + i, 2)
                    rows = pl.ds(pl.multiple_of(h * n + i * block, block), block)
                    inner = pl.ds(pl.multiple_of(i * block, block), block)

                    def again():
                        for c in out_of(h, i, slot):
                            c.wait()

                    maybe_static(h * count + i >= 2, again)
                    total = st[0, rows, 0:wide].astype(f32) + st[1, rows, 0:wide].astype(f32)
                    for q in range(len(far) - 2):
                        total = total + ta[h, q, inner, 0:wide].astype(f32)
                    staged[slot, 0:block, 0:wide] = total
                    for c in out_of(h, i, slot):
                        c.start()

            for slot in range(min(2, 2 * count)):
                for c in out_of(0, 0, slot):
                    c.wait()

        def grad_chunks(*jobs, chosen=masks):
            pending = []

            def settle():
                for w, m, copies in pending:
                    for c in copies:
                        c.wait()
                    scatter_first(w, m)
                pending.clear()

            for n, m in enumerate(chosen):
                slot = n % 2
                fresh = []
                for number, (w, work, st) in enumerate(jobs):
                    gw = grad_info[w][0]
                    work(m, flip(me, m), st.at[slot])
                    copies = moves(w, gw.at[place[m]], st.at[slot], 6 * number + 3 * slot, True)
                    for c in copies:
                        c.start()
                    if number == 0:
                        settle()
                    fresh.append((w, m, copies))
                pending.extend(fresh)
            settle()

        def grad_down(m, k, st):
            @pl.loop(0, F // WT)
            def _(i):
                v = mm(Av[:, ds(i, WT)], Gv[:, ds(k, CD)], TN)
                v = v + mm(wb[:, ds(i, WT)], YP[place[m]], TN)
                st[ds(i, WT), :] = v.astype(bf16)


        def grad_out(m, k, st):
            v = mm(ATv[...], Gv[:, ds(k, CD)], TN)
            v = v + mm(wa[0, 0:S, 0:L], YP[place[m]], TN)
            st[...] = v.astype(bf16)

        mate_load.wait()
        out_place = ref.ta_down.at[:, 1, pl.ds(0, L)]
        branch_jobs = ("down", grad_down, ref.st_down), ("out", grad_out, out_place)
        grad_chunks(*branch_jobs, chosen=masks[:-1])
        sum1.step(1)
        def back_copies(i, slot):
            rows = ds(i, TD)
            return [(ref.full_up.at[rows, :], wb.at[wide_slot(slot), pl.ds(0, F)])] + [
                (ref.full_qkv.at[j, rows, :], wa.at[slot, pl.ds(j * TD, TD), pl.ds(0, L)])
                for j in range(3)
            ]

        def back_value(rows, slot, i):
            v = mm(Hv[rows, :], wb[wide_slot(slot), 0:F], NT)
            for j in range(3):
                w = wa[slot, j * TD : (j + 1) * TD, 0:L]
                v = v + mm(DMv[rows, j * L : (j + 1) * L], w, NT)
            return v

        back_ring = Ring(2, 24)
        back_ring.prime(back_copies)
        dk, dv = ref.dk, ref.dv

        @pl.loop(0, L // 128)
        def _(hp):
            lanes = ds(hp, 128)
            flat[...] = QKV[1, :, lanes].T
            dk[...] = jnp.zeros_like(dk)
            dv[...] = jnp.zeros_like(dv)
            scores, slopes, done = {}, {}, {}

            def score(i, e):
                rows, past = places(i)
                q = only(QKV[0, rows, lanes], pair_masks[e])
                do = ob[i * RB // HS, i * RB % HS : i * RB % HS + RB, lanes]
                do = only(do, pair_masks[e])
                found = [q, do]
                for where in [rows, past][: 1 + (i > 0)]:
                    found += [mm(QKV[1, where, lanes], q, NT), mm(QKV[2, where, lanes], do, NT)]
                scores[i, e] = found

            def slope(i, e):
                q, do, s, dp, *earlier = scores.pop((i, e))
                log_mass = LSE[hp * 2 + e, :, places(i)[0]]
                p = jnp.where(corner, jnp.exp(s - log_mass), 0.0)
                delta = jnp.sum(p * dp, 0, keepdims=True)
                if i:
                    s2, dp2 = earlier
                    p2 = jnp.exp(s2 - log_mass)
                    delta = delta + jnp.sum(p2 * dp2, 0, keepdims=True)
                found = [q, do, (p * (dp - delta)).astype(bf16), p.astype(bf16)]
                if i:
                    found += [(p2 * (dp2 - delta)).astype(bf16), p2.astype(bf16)]
                slopes[i, e] = found

            def push(i, e):
                rows, past = places(i)
                q, do, s, p, *earlier = slopes.pop((i, e))
                keys = flat.at[pl.ds(e * HD, HD), :]
                dk[rows, :] += mm(s, q, NN)
                dv[rows, :] += mm(p, do, NN)
                dq = mm(keys[:, rows], s, NN)
                if i:
                    s2, p2 = earlier
                    dk[past, :] += mm(s2, q, NN)
                    dv[past, :] += mm(p2, do, NN)
                    dq = dq + mm(keys[:, past], s2, NN)
                done[e] = dq
                if e == 1:
                    dq = jnp.concatenate([done[0], done[1]], 0).T * HD**-0.5
                    DMv[rows, lanes] = turn(dq, rows, -1.0).astype(bf16)

            staggered(score, slope, push)
            DMv[:, ds(hp + L // 128, 128)] = turn(dk[...], pl.ds(0, S), -1.0).astype(bf16)
            DMv[:, ds(hp + 2 * (L // 128), 128)] = dv[...].astype(bf16)

        mix_mate = wire.send(DMv, ref.mate_mix, ref.mate_mix, mate)
        sum2 = LineSum(ref.part2, ref.below2, ref.above2)
        product_half(ref.part2, True, back_ring, back_copies, back_value, None)
        sum2.begin(False)
        hid_mate.arrive()
        mate_tiles = [wire.local(ref.mate_hid, wb.at[:, pl.ds(0, F)])]

        normed_mate.arrive()
        mate_columns = load_mate_columns(ref.mate_normed, pl.ds(0, S))
        small[3:4, pl.ds(0, 3 * L)] = sum_rows_of(DMv, S)
        for i in range(1, len(bits)):
            scatter_step("down", i)

        for tau in range(2, n_mp - 1):
            sum1.step(tau)
        for c in mate_tiles + mate_columns:
            c.wait()

        def grad_up(m, k, st):
            @pl.loop(0, F // WT)
            def _(i):
                v = mm(Nv[:, ds(k, CD)], Hv[:, ds(i, WT)], TN)
                v = v + mm(YP[place[m]], wb[:, ds(i, WT)], TN)
                st[:, ds(i, WT)] = v.astype(bf16)

        grad_chunks(("up", grad_up, ref.st_up))
        back_ring.prime(back_copies)
        sum2.step(1)

        small_b, small_b_all = ref.small_b, ref.small_b_all
        for n in range(nq):
            small_b[n : n + 1, :] = small[3:4, n * VB : (n + 1) * VB]
        for n in range(nu):
            small_b[nq + n : nq + n + 1, :] = small[4:5, n * VB : (n + 1) * VB]
        for n in range(nq + nu, 8):
            small_b[n : n + 1, :] = jnp.zeros((1, VB), f32)
        biases = []
        for m in range(1, n_dp):
            k = flip(me, m)
            biases.append(wire.send(small_b, small_b_all.at[me], small_b_all.at[k], (k, z)))
        product_half(ref.part2, False, back_ring, back_copies, back_value, None)
        sum2.begin(True)

        mix_mate.arrive()
        loads_mix = [wire.local(ref.mate_mix, wb.at[:, pl.ds(0, 3 * L)])]
        for i in range(1, len(bits)):
            scatter_step("up", i)
        for i in range(1, len(bits)):
            scatter_step("out", i)
        for c in loads_mix:
            c.wait()

        def grad_qkv(m, k, st):
            v = mm(Nv[:, ds(k, CD)], DMv[...], TN)
            v = v + mm(YP[place[m]], wb[:, 0 : 3 * L], TN)
            st[:, 0 : 3 * L] = v.astype(bf16)

        grad_chunks(("qkv", grad_qkv, ref.st_up))
        own_loads = [
            wire.local(ref.mate_act, wb.at[:, pl.ds(0, F)]),
            wire.local(ref.mate_att, wa.at[0, pl.ds(0, S), pl.ds(0, L)]),
            wire.local(ref.mate_pulled.at[:, ds(me, CD)], YP.at[NC - 1]),
        ]

        for tau in range(2, n_mp - 1):
            sum2.step(tau)
        zs = ref.zs
        sum1.arrive()
        sum1.load(zs)
        @pl.loop(0, R // LB)
        def _(i):
            rows = ds(i, LB)
            v = tok[rows, :].astype(f32) + vrow[2:3, :]
            v = v + zs[0, rows, :].astype(f32)
            v = v + zs[1, rows, :].astype(f32) + zs[2, rows, :].astype(f32)
            zs[0, rows, :] = v.astype(bf16)

        lo_copy = wire.local(zs.at[0], ref.layer_out)
        small[2:3, :] = sum_rows_of(Gv, S)
        lo_copy.wait()


        for c in own_loads:
            c.wait()
        grad_chunks(*branch_jobs, chosen=masks[-1:])
        for w in ("down", "out"):
            weight_sum(w)
        for i in range(1, len(bits)):
            scatter_step("qkv", i)
        weight_sum("up")
        for one in biases:
            one.arrive()
        total = small_b[...]
        for m in range(1, n_dp):
            total = total + small_b_all[flip(me, m)]
        ref.bias_sums[...] = total

        sum2.arrive()
        sum2.load(zs)
        gt = ref.gt

        def gt_copy(i, slot):
            return pltpu.make_async_copy(
                gt.at[slot], ref.grad_tokens.at[ds(i, LB), :], slot_sems.at[slot]
            )

        @pl.loop(0, R // LB)
        def _(i):
            slot = lax.rem(i, 2)
            rows = ds(i, LB)
            _, xhat, scale = stats(rows)
            d = zs[0, rows, :].astype(f32) + zs[1, rows, :].astype(f32)
            d = d + zs[2, rows, :].astype(f32)
            small[0:1, :] += jnp.sum(d * xhat, 0, keepdims=True)
            small[1:2, :] += jnp.sum(d, 0, keepdims=True)
            e = d * vrow[0:1, :]
            centre = jnp.mean(e, -1, keepdims=True)
            along = jnp.mean(e * xhat, -1, keepdims=True)

            @pl.when(i >= 2)
            def _():
                gt_copy(i - 2, slot).wait()

            own = Gv[pl.ds(pl.multiple_of(z * R + i * LB, LB), LB), :].astype(f32)
            gt[slot] = own + scale * (e - centre - xhat * along)
            gt_copy(i, slot).start()

        for i in range(max(0, R // LB - 2), R // LB):
            gt_copy(i, i % 2).wait()
        small_k, small_all = ref.small_k, ref.small_all
        for k in range(n_dp):
            small_k[k] = small[:, k * CD : (k + 1) * CD]
        across = []
        for m in range(1, n_dp):
            k = flip(me, m)
            across.append(wire.send(small_k.at[k], small_all.at[me], small_all.at[k], (k, z)))
        for one in across:
            one.arrive()
        total = small_k[me]
        for m in range(1, n_dp):
            total = total + small_all[flip(me, m)]
        small_own, small_mp = ref.small_own, ref.small_mp
        small_own[...] = total
        across = []
        for k in range(1, n_mp):
            to = lax.rem(z + k, n_mp)
            across.append(wire.send(small_own, small_mp.at[k], small_mp.at[k], (me, to)))
        weight_sum("qkv")
        for one in across:
            one.arrive()
        others = small_mp[1]
        for k in range(2, n_mp):
            others = others + small_mp[k]
        first_two = lax.broadcasted_iota(jnp.int32, (8, 1), 0) < 2
        ref.row_sums[...] = total + jnp.where(first_two, others, 0.0)
        sum1.finish()
        sum2.finish()
        wire.finish()

    return kernel


def sum_rows_of(array, rows):
    total = None
    for i in range(rows // 128):
        part = jnp.sum(array[pl.ds(i * 128, 128), :].astype(f32), 0, keepdims=True)
        total = part if total is None else total + part
    return total


def rope_tables(length):
    places = np.arange(length, dtype=np.float64)
    inverse = 10000.0 ** (-np.arange(0, ROT, 2, dtype=np.float64) / ROT)
    angles = places[:, None] * inverse[None, :]
    cosine, sine = np.cos(angles), np.sin(angles)
    rest = np.zeros((length, HD - ROT))
    c = np.concatenate([cosine, cosine, rest + 1.0], -1)
    s = np.concatenate([-sine, sine, rest], -1)
    return [np.concatenate([t, t], -1).astype(np.float32) for t in (c, s)]


def make_body(n_dp, n_mp):
    def body(
        tokens, ln_gain, ln_bias, w_qkv, b_qkv, w_out, b_out, w_up, b_up, w_down, b_down, cotangent
    ):
        me = lax.axis_index("dp")
        R = tokens.shape[0]
        S = R * n_mp
        CD = D // n_dp
        NC = n_dp // 2
        F = w_up.shape[1]
        L = w_qkv.shape[2]
        heads = b_qkv.shape[1]
        share = HD // n_dp
        T = min(512, F)
        TD = 512
        nq, nu = -(-3 * L // VB), F // VB

        def spread(shape, own, axis, rows):
            whole = lax.dynamic_update_slice_in_dim(
                jnp.zeros(shape, f32), own.astype(f32), me * share, axis
            ).reshape(-1)
            return jnp.pad(whole, (0, rows * VB - whole.shape[0])).reshape(rows, VB)

        vec_a = jnp.concatenate([ln_gain, ln_bias, b_out, b_down]).astype(f32)
        vec_a = jnp.pad(vec_a, (0, 1024 - 4 * CD)).reshape(8, 128)
        vec_b = jnp.concatenate(
            [
                spread((3, heads, HD), b_qkv, 2, nq),
                spread((F // HD, HD), b_up, 1, nu),
                jnp.zeros((8 - nq - nu, VB), f32),
            ],
            0,
        )
        rope_c, rope_s = rope_tables(S)
        ins = dict(
            tokens=tokens,
            cotangent=cotangent,
            vec_a=vec_a,
            vec_b=vec_b,
            w_up=w_up,
            w_qkv=w_qkv.transpose(1, 0, 2),
            w_down=w_down,
            w_out=w_out,
            rope_c=jnp.asarray(rope_c),
            rope_s=jnp.asarray(rope_s),
        )
        any_spec = pl.BlockSpec(memory_space=pl.ANY)
        vmem_spec = pl.BlockSpec(memory_space=pltpu.VMEM)
        outs = dict(
            layer_out=((R, D), bf16),
            grad_tokens=((R, D), f32),
            row_sums=((8, CD), f32),
            bias_sums=((8, VB), f32),
            grad_up=((CD, F), f32),
            grad_q=((CD, L), f32),
            grad_k=((CD, L), f32),
            grad_v=((CD, L), f32),
            grad_down=((F, CD), f32),
            grad_out=((L, CD), f32),
            gw_up=((NC, CD, F), bf16),
            gw_qkv=((NC, 3, CD, L), bf16),
            gw_down=((NC, F, CD), bf16),
            gw_out=((NC, L, CD), bf16),
            rb_up=((NC - 1, CD, F), bf16),
            rb_qkv=((NC - 1, 3, CD, L), bf16),
            rb_down=((NC - 1, F, CD), bf16),
            rb_out=((NC - 1, L, CD), bf16),
            full_up=((D, F), bf16),
            full_qkv=((3, D, L), bf16),
            full_down=((F, D), bf16),
            full_out=((L, D), bf16),
            full_normed=((n_mp, R, D), bf16),
            full_pulled=((n_mp, R, D), bf16),
            mate_normed=((S, D), bf16),
            mate_pulled=((S, D), bf16),
            mate_act=((S, F), bf16),
            mate_hid=((S, F), bf16),
            mate_att=((S, L), bf16),
            mate_mix=((S, 3 * L), bf16),
            part1=((n_mp, R, D), bf16),
            below1=((n_mp, R, D), bf16),
            above1=((n_mp, R, D), bf16),
            part2=((n_mp, R, D), bf16),
            below2=((n_mp, R, D), bf16),
            above2=((n_mp, R, D), bf16),
        )
        n_sems = 33 * (n_dp + n_mp)
        scratch = dict(
            vec_a_all=pltpu.VMEM((n_dp, 8, 128), f32),
            vec_b_all=pltpu.VMEM((n_dp, 8, VB), f32),
            vrow=pltpu.VMEM((8, D), f32),
            small=pltpu.VMEM((8, D), f32),
            small_k=pltpu.VMEM((n_dp, 8, CD), f32),
            small_all=pltpu.VMEM((n_dp, 8, CD), f32),
            small_own=pltpu.VMEM((8, CD), f32),
            small_mp=pltpu.VMEM((n_mp, 8, CD), f32),
            small_b=pltpu.VMEM((8, VB), f32),
            small_b_all=pltpu.VMEM((n_dp, 8, VB), f32),
            tok=pltpu.VMEM((R, D), bf16),
            gt=pltpu.VMEM((2, LB, D), f32),
            gs=pltpu.VMEM((2, min(256, L // 2), CD), f32),
            tc=pltpu.VMEM((S, 128), f32),
            ts=pltpu.VMEM((S, 128), f32),
            Nv=pltpu.VMEM((S, D), bf16),
            Gv=pltpu.VMEM((S, D), bf16),
            Av=pltpu.VMEM((S, F), bf16),
            Hv=pltpu.VMEM((S, F), bf16),
            QKV=pltpu.VMEM((3, S, L), bf16),
            ATv=pltpu.VMEM((S, L), bf16),
            flat=pltpu.VMEM((128, S), bf16),
            DMv=pltpu.VMEM((S, 3 * L), bf16),
            LSE=pltpu.VMEM((heads, 1, S), f32),
            dk=pltpu.VMEM((S, 128), f32),
            dv=pltpu.VMEM((S, 128), f32),
            wa=pltpu.VMEM((3, D, T), bf16),
            wb=pltpu.VMEM((2 * T, D), bf16),
            wo=pltpu.VMEM((L, D), bf16),
            ob=pltpu.VMEM((2, S // 2, TD), bf16),
            YP=pltpu.VMEM((NC, S, CD), bf16),
            zs=pltpu.VMEM((3, R, D), bf16),
            st_up=pltpu.VMEM((2, CD, F), bf16),
            st_down=pltpu.VMEM((2, F, CD), bf16),
            ta_up=pltpu.VMEM((2, 2, CD // 2, F), bf16),
            ta_down=pltpu.VMEM((2, 2, F // 2, CD), bf16),
            sems=pltpu.SemaphoreType.DMA((n_sems,)),
            slot_sems=pltpu.SemaphoreType.DMA((32,)),
            out_sems=pltpu.SemaphoreType.DMA((2, n_mp)),
        )
        names = list(ins) + list(outs) + list(scratch)
        got = pl.pallas_call(
            make_kernel(n_dp, n_mp, R, F, L, names, n_sems),
            out_shape=[jax.ShapeDtypeStruct(s, t) for s, t in outs.values()],
            in_specs=[any_spec] * len(ins),
            out_specs=[vmem_spec if n.endswith("_sums") else any_spec for n in outs],
            scratch_shapes=list(scratch.values()),
            name="layer",
            cost_estimate=pl.CostEstimate(
                flops=6 * S * D * (4 * L + 2 * F), bytes_accessed=150 << 20, transcendentals=0
            ),
            compiler_params=pltpu.CompilerParams(
                collective_id=0, has_side_effects=True, vmem_limit_bytes=62 << 20
            ),
        )(*ins.values())
        got = types.SimpleNamespace(**dict(zip(outs, got)))

        def mine(values, axis):
            return lax.dynamic_slice_in_dim(values, me * share, share, axis)

        sums = got.bias_sums.reshape(-1)
        bias = got.row_sums[2]
        return (
            got.layer_out,
            got.grad_tokens,
            got.row_sums[0],
            got.row_sums[1],
            jnp.stack([got.grad_q, got.grad_k, got.grad_v], 1),
            mine(sums[: 3 * L].reshape(3, heads, HD), 2),
            got.grad_out,
            bias,
            got.grad_up,
            mine(sums[nq * VB : nq * VB + F].reshape(F // HD, HD), 1),
            got.grad_down,
            bias,
        )

    return body


def solution(mesh):
    n_dp, n_mp = mesh.shape["dp"], mesh.shape["mp"]
    weights_in = (
        P("dp"),
        P("dp"),
        P("dp", None, "mp"),
        P(None, "mp", "dp"),
        P("mp", "dp"),
        P("dp"),
        P("dp", "mp"),
        P("mp", "dp"),
        P("mp", "dp"),
        P("dp"),
    )
    rows = P(("dp", "mp"), None)
    return jax.shard_map(
        make_body(n_dp, n_mp),
        mesh=mesh,
        in_specs=(rows,) + weights_in + (rows,),
        out_specs=(rows, rows) + weights_in,
        check_vma=False,
    )
```
